32 devices in a mesh: ctx: 16 (over z, y, x), head: 2 (over core).
Axes of the slice: x: 2, y: 2, z: 4, core: 2. Of those that a mesh axis runs over, the one named last changes fastest.
Arguments:
- queries: bfloat16 [2048, 64, 128], P('ctx', 'head'), may hold values from -90 to 90
- key_heads: bfloat16 [2048, 8, 128], P('ctx', 'head'), may hold values from -4 to 4
- value_head_rows: bfloat16 [2048, 8, 128], P('ctx', 'head'), may hold values from -6 to 6
- doc_lengths: int32 [8], replicated, may hold values from 1 to 512, 2048 in all
Outputs:
- attended: bfloat16 [2048, 64, 128], P(('ctx', 'head'))
The draws below stay inside these ranges and needn't reach their ends.
Inputs may be any that keep to these rules, and one draw needn't show every extreme that they name: `doc_lengths`: lengths of 8 documents in order, summing to 2048; the longest is exactly 512.
All inputs are finite; a program needn't handle non-finite values.
Results may differ from the reference program's by a relative error of at most 0.0055.
Values may be sent and summed in bfloat16 or wider, within the bound.
No kernel may reach another device: no remote copies, remote signals or barrier semaphores. Data moves between devices by JAX's collectives and lax.ppermute only.
A program may use at most 128 MiB of HBM per device.

```python
import math
import jax
import jax.numpy as jnp
import numpy as np
from jax import lax

QUERY_HEADS = 64
KEY_VALUE_HEADS = 8
HEAD_WIDTH_SIZE = 128
BLOCK_TOKENS = 64
REACH_LOG = 3
SEQUENCE_TOKENS = 2048
LONGEST_DOCUMENT = 512
NDOC = 8
N_CTX = 16


def paired_draw(key):
    random_keys = jax.random.fold_in(key, 11)
    random_queries = jax.random.fold_in(key, 23)
    key_entries = jnp.clip(jax.random.normal(random_keys, (SEQUENCE_TOKENS, KEY_VALUE_HEADS, HEAD_WIDTH_SIZE), jnp.float32), -4.0, 4.0)
    query_entries = jnp.clip(jax.random.normal(random_queries, (SEQUENCE_TOKENS, QUERY_HEADS, HEAD_WIDTH_SIZE), jnp.float32), -4.0, 4.0)
    return (query_entries, key_entries)


def draw_queries(key, part):
    return paired_draw(key)[0].astype(jnp.bfloat16)


def draw_key_heads(key, part):
    return paired_draw(key)[1].astype(jnp.bfloat16)


def block_levels(own_key, extent, pieces, least, top_value):
    gain = 1.0
    for position, blocks in pieces:
        steps = jax.random.uniform(jax.random.fold_in(jax.random.fold_in(own_key, 6), position), (blocks,), jnp.float32, least / len(pieces), top_value / len(pieces))
        gain = gain * jnp.repeat(jnp.exp(steps), extent[position] // blocks).reshape((-1,) + (1,) * (len(extent) - 1 - position))
    return gain


def split_up(amount, total, reach, lean):
    portions = [(1 << 20) // math.isqrt(rank ** lean) + 1 for rank in range(2, amount + 1)]
    spare, holding = total - reach - (amount - 1), [1] * (amount - 1)
    while spare > 0:
        free = [i for i in range(amount - 1) if holding[i] < reach]
        pool, left = sum([portions[i] for i in free]), spare
        for i in free:
            extra = min(reach - holding[i], max(1, left * portions[i] // pool), spare)
            holding[i] = holding[i] + extra
            spare = spare - extra
    return np.array([reach] + holding)


def uneven(rng, number_of, total, most, skew):
    if number_of == 2:
        one = jax.random.randint(rng, (), max(1, total - most), min(most, total - 1) + 1)
        return jnp.stack([one, total - one])
    lengths = jnp.asarray(split_up(number_of, total, most, skew), jnp.int32)
    pairs = (number_of - 1) // 2
    source_of, receiver = lengths[1:1 + 2 * pairs:2], lengths[2:2 + 2 * pairs:2]
    margin = jnp.minimum(source_of - 1, most - receiver)
    passed = jax.random.randint(jax.random.fold_in(rng, 1), (pairs,), 0, 1 << 20) % (margin + 1)
    lengths = lengths.at[1:1 + 2 * pairs:2].set(source_of - passed).at[2:2 + 2 * pairs:2].set(receiver + passed)
    return lengths[jax.random.permutation(jax.random.fold_in(rng, 2), number_of)]


def normal_values(rng, extent, spread, most, shards=(), held_as=jnp.bfloat16):
    entries = jax.random.normal(rng, extent, jnp.float32) * spread
    if len(shards) > 0:
        entries = block_levels(rng, extent, shards, -0.22, 0.18) * entries
    return jnp.clip(entries, min=-most, max=most).astype(held_as)


def setup_inputs(seed: int = 0) -> dict:
    splits = jax.random.split(jax.random.key(seed), 5)
    return {
        "queries": draw_queries(jax.random.fold_in(splits[4], 71), 0),
        "key_heads": draw_key_heads(jax.random.fold_in(splits[4], 71), 0),
        "value_head_rows": normal_values(splits[2], (SEQUENCE_TOKENS, KEY_VALUE_HEADS, HEAD_WIDTH_SIZE), 1.0, 6.0, ((0, 16), (1, 2))),
        "doc_lengths": uneven(splits[3], NDOC, SEQUENCE_TOKENS, LONGEST_DOCUMENT, 2).astype(jnp.int32),
    }


MASKED_SCORE = -1.0e30


def natural_rows():
    places = jnp.arange(SEQUENCE_TOKENS, dtype=jnp.int32)
    stretch_idx = places // BLOCK_TOKENS
    in_stretch = places % BLOCK_TOKENS
    lower = stretch_idx < N_CTX
    device = jnp.where(lower, stretch_idx, 2 * N_CTX - 1 - stretch_idx)
    offset = jnp.where(lower, in_stretch, BLOCK_TOKENS + in_stretch)
    return (device * (2 * BLOCK_TOKENS) + offset).astype(jnp.int32)


def reference(queries, key_heads, value_head_rows, doc_lengths):
    row_ids = natural_rows()
    query_order = queries[row_ids]
    key_folded_rows = key_heads[row_ids]
    value_folded_rows = value_head_rows[row_ids]
    places = jnp.arange(SEQUENCE_TOKENS, dtype=jnp.int32)
    doc_ends = jnp.cumsum(doc_lengths).astype(jnp.int32)
    doc_starts = (doc_ends - doc_lengths).astype(jnp.int32)
    doc_order = jnp.sum((places[:, None] >= doc_ends[None, :]).astype(jnp.int32), axis=1).astype(jnp.int32)
    total_tiles = 2 ** REACH_LOG + 1
    visible_span = total_tiles * BLOCK_TOKENS
    query_group = QUERY_HEADS // KEY_VALUE_HEADS
    score_scale = 1.0 / (HEAD_WIDTH_SIZE ** 0.5)
    padded_keys = jnp.concatenate([jnp.zeros((LONGEST_DOCUMENT, KEY_VALUE_HEADS, HEAD_WIDTH_SIZE), key_folded_rows.dtype), key_folded_rows], axis=0)
    padded_values = jnp.concatenate([jnp.zeros((LONGEST_DOCUMENT, KEY_VALUE_HEADS, HEAD_WIDTH_SIZE), value_folded_rows.dtype), value_folded_rows], axis=0)
    doc_padded = jnp.concatenate([jnp.full((LONGEST_DOCUMENT,), -1, jnp.int32), doc_order], axis=0)

    def one_block(index):
        begin = (index * BLOCK_TOKENS).astype(jnp.int32)
        query_block = lax.dynamic_slice_in_dim(query_order, begin, BLOCK_TOKENS, 0).astype(jnp.float32)
        query_block = query_block.reshape(BLOCK_TOKENS, KEY_VALUE_HEADS, query_group, HEAD_WIDTH_SIZE)
        q_doc = lax.dynamic_slice_in_dim(doc_order, begin, BLOCK_TOKENS, 0)
        q_place = begin + jnp.arange(BLOCK_TOKENS, dtype=jnp.int32)
        first_start = jnp.sum(jnp.where(jnp.arange(NDOC, dtype=jnp.int32) == q_doc[0], doc_starts, 0)).astype(jnp.int32)
        leading_tile = ((first_start - begin + LONGEST_DOCUMENT) // BLOCK_TOKENS).astype(jnp.int32)

        def score_tile(tile, holding_array):
            start = (begin + tile * BLOCK_TOKENS).astype(jnp.int32)
            k_tile = lax.dynamic_slice_in_dim(padded_keys, start, BLOCK_TOKENS, 0).astype(jnp.float32)
            key_doc = lax.dynamic_slice_in_dim(doc_padded, start, BLOCK_TOKENS, 0)
            key_place = start - LONGEST_DOCUMENT + jnp.arange(BLOCK_TOKENS, dtype=jnp.int32)
            allowed = (q_doc[:, None] == key_doc[None, :]) & (key_place[None, :] <= q_place[:, None])
            scores = jnp.einsum("qkgd,tkd->kgqt", query_block, k_tile) * score_scale
            scores = jnp.where(allowed, scores, MASKED_SCORE)
            return lax.dynamic_update_slice_in_dim(holding_array, scores, (tile * BLOCK_TOKENS).astype(jnp.int32), 3)

        holding_array = jnp.full((KEY_VALUE_HEADS, query_group, BLOCK_TOKENS, visible_span), MASKED_SCORE, jnp.float32)
        holding_array = lax.fori_loop(leading_tile, total_tiles, score_tile, holding_array)
        live = holding_array > 0.5 * MASKED_SCORE
        largest = jnp.max(holding_array, axis=-1, keepdims=True)
        weights = jnp.where(live, jnp.exp(holding_array - largest), 0.0)
        totals = jnp.sum(weights, axis=-1)
        rounded = lax.optimization_barrier(weights.astype(jnp.bfloat16)).astype(jnp.float32)

        def combine_tile(tile, total):
            start = (begin + tile * BLOCK_TOKENS).astype(jnp.int32)
            v_tile = lax.dynamic_slice_in_dim(padded_values, start, BLOCK_TOKENS, 0).astype(jnp.float32)
            w_tile = lax.dynamic_slice_in_dim(rounded, (tile * BLOCK_TOKENS).astype(jnp.int32), BLOCK_TOKENS, 3)
            return total + jnp.einsum("kgqt,tkd->kgqd", w_tile, v_tile)

        combined_output = lax.fori_loop(leading_tile, total_tiles, combine_tile, jnp.zeros((KEY_VALUE_HEADS, query_group, BLOCK_TOKENS, HEAD_WIDTH_SIZE), jnp.float32))
        result = combined_output / totals[..., None]
        result = jnp.transpose(result, (2, 0, 1, 3)).reshape(BLOCK_TOKENS, QUERY_HEADS, HEAD_WIDTH_SIZE)
        return result.astype(jnp.bfloat16)

    blocks = lax.map(one_block, jnp.arange(SEQUENCE_TOKENS // BLOCK_TOKENS, dtype=jnp.int32))
    natural = blocks.reshape(SEQUENCE_TOKENS, QUERY_HEADS, HEAD_WIDTH_SIZE)
    return jnp.zeros((SEQUENCE_TOKENS, QUERY_HEADS, HEAD_WIDTH_SIZE), jnp.bfloat16).at[row_ids].set(natural)
```

```python
import functools
import math

import jax
import jax.numpy as jnp
from jax import lax
from jax.experimental import pallas as pl
from jax.experimental.pallas import tpu as pltpu
from jax.sharding import PartitionSpec as P

REACH_LOG = 3
MASKED_SCORE = -1e30


def query_bounds(first_place, lanes, group, doc_lengths):
    place = first_place + lax.broadcasted_iota(jnp.int32, (1, lanes), 1) // group
    begin = jnp.zeros((1, lanes), jnp.int32)
    end = jnp.int32(0)
    for j in range(doc_lengths.shape[0]):
        end = end + doc_lengths[j]
        begin = jnp.where(place >= end, end, begin)
    return place, begin


def attention_kernel(
    devices, doc_lengths, index, queries, gathered, out, window, bias, sems, *, group
):
    kv_count, block = window.shape[2], gathered.shape[4]
    reach = 2**REACH_LOG
    span = (reach + 1) * block
    lanes = block * group
    device = index[0]
    factor = math.log2(math.e) / math.sqrt(queries.shape[2])
    stretches = (device, 2 * devices - 1 - device)

    def copy(half, step):
        source = jnp.maximum(stretches[half] - reach + step, 0)
        folded = source >= devices
        row = jnp.where(folded, 2 * devices - 1 - source, source)
        return pltpu.make_async_copy(
            gathered.at[row, :, :, folded.astype(jnp.int32)],
            window.at[half, :, :, pl.ds(step * block, block)],
            sems.at[half, step],
        )

    for half in range(2):
        for step in range(reach + 1):
            copy(half, step).start()
    for half in range(2):
        first = stretches[half] * block
        place, begin = query_bounds(first, lanes, group, doc_lengths)
        key_place = first - reach * block + lax.broadcasted_iota(jnp.int32, (span, lanes), 0)
        allowed = (key_place >= begin) & (key_place <= place)
        bias[...] = jnp.where(allowed, 0.0, MASKED_SCORE)
        for step in range(reach + 1):
            copy(half, step).wait()
        rows = slice(half * block, (half + 1) * block)
        for pair in range(kv_count // 2):
            heads = slice(2 * pair * group, 2 * (pair + 1) * group)
            both = queries[rows, heads, :].astype(jnp.float32)
            done = []
            for part in range(2):
                head = 2 * pair + part
                q = both[:, part * group : (part + 1) * group, :]
                q = q.reshape(lanes, q.shape[2]).astype(jnp.bfloat16)
                scores = lax.dot_general(
                    window[half, 0, head],
                    q,
                    (((1,), (1,)), ((), ())),
                    preferred_element_type=jnp.float32,
                )
                scores = scores * factor + bias[...]
                weights = jnp.exp2(scores - jnp.max(scores, axis=0, keepdims=True))
                total = jnp.sum(weights, axis=0, keepdims=True)
                mixed = lax.dot_general(
                    window[half, 1, head],
                    weights.astype(jnp.bfloat16),
                    (((0,), (0,)), ((), ())),
                    preferred_element_type=jnp.float32,
                )
                mixed = (mixed / total).T
                done.append(mixed.reshape(block, group, mixed.shape[1]))
            out[rows, heads, :] = jnp.concatenate(done, axis=1).astype(out.dtype)


def shards(queries, key_heads, value_head_rows, doc_lengths):
    stride, heads, width = queries.shape
    kv_count = key_heads.shape[1]
    block = stride // 2
    group = heads // kv_count
    devices = lax.axis_size("ctx")
    index = lax.axis_index("ctx").astype(jnp.int32)[None]
    span = (2**REACH_LOG + 1) * block

    packed = jnp.stack([key_heads, value_head_rows])
    packed = packed.reshape(2, 2, block, kv_count, width).transpose(0, 3, 1, 2, 4)
    gathered = lax.all_gather(packed, "ctx")

    attended = pl.pallas_call(
        functools.partial(attention_kernel, devices, group=group),
        out_shape=jax.ShapeDtypeStruct(queries.shape, jnp.bfloat16),
        in_specs=[
            pl.BlockSpec(memory_space=pltpu.SMEM),
            pl.BlockSpec(memory_space=pltpu.SMEM),
            pl.BlockSpec(memory_space=pltpu.VMEM),
            pl.BlockSpec(memory_space=pl.ANY),
        ],
        out_specs=pl.BlockSpec(memory_space=pltpu.VMEM),
        scratch_shapes=[
            pltpu.VMEM((2, 2, kv_count, span, width), jnp.bfloat16),
            pltpu.VMEM((span, block * group), jnp.float32),
            pltpu.SemaphoreType.DMA((2, 2**REACH_LOG + 1)),
        ],
        compiler_params=pltpu.CompilerParams(vmem_limit_bytes=48 * 2**20),
        name="attention",
    )(doc_lengths, index, queries, gathered)
    return lax.all_to_all(attended, "head", split_axis=0, concat_axis=1, tiled=True)


def solution(mesh):
    in_specs = (P("ctx", "head", None), P("ctx", "head", None), P("ctx", "head", None), P())
    out_specs = P(("ctx", "head"), None, None)
    return jax.shard_map(shards, mesh=mesh, in_specs=in_specs, out_specs=out_specs, check_vma=False)
```

```python
import functools
import math

import jax
import jax.numpy as jnp
from jax import lax
from jax.experimental import pallas as pl
from jax.experimental.pallas import tpu as pltpu
from jax.sharding import PartitionSpec as P

REACH_LOG = 3
MASKED_SCORE = -1e30


def query_bounds(first_place, lanes, group, doc_lengths):
    place = first_place + lax.broadcasted_iota(jnp.int32, (1, lanes), 1) // group
    begin = jnp.zeros((1, lanes), jnp.int32)
    end = jnp.int32(0)
    for j in range(doc_lengths.shape[0]):
        end = end + doc_lengths[j]
        begin = jnp.where(place >= end, end, begin)
    return place, begin


def attention_kernel(doc_lengths, position, queries, partner_queries, *refs, group):
    reach = 2**REACH_LOG
    blocks, (out, all_queries, window, bias, sems) = refs[: reach + 1], refs[reach + 1 :]
    stretch, core = position[0], position[1]
    kv_count, block, width = blocks[0].shape[1:]
    span = (reach + 1) * block
    lanes = block * group
    half_heads = kv_count * group // 2
    factor = math.log2(math.e) / math.sqrt(width)

    copies = [
        pltpu.make_async_copy(
            queries.at[pl.ds(core * block, block)],
            all_queries.at[:, pl.ds(core * half_heads, half_heads)],
            sems.at[reach + 1],
        ),
        pltpu.make_async_copy(
            partner_queries,
            all_queries.at[:, pl.ds((1 - core) * half_heads, half_heads)],
            sems.at[reach + 2],
        ),
    ]
    for distance in range(reach + 1):
        rows = slice((reach - distance) * block, (reach - distance + 1) * block)
        copies.append(
            pltpu.make_async_copy(blocks[distance], window.at[:, :, rows], sems.at[distance])
        )
    for copy in copies:
        copy.start()
    first = stretch * block
    place, begin = query_bounds(first, lanes, group, doc_lengths)
    key_place = first - reach * block + lax.broadcasted_iota(jnp.int32, (span, lanes), 0)
    allowed = (key_place >= begin) & (key_place <= place)
    bias[...] = jnp.where(allowed, 0.0, MASKED_SCORE)
    for copy in copies:
        copy.wait()
    for pair in range(kv_count // 2):
        heads = slice(2 * pair * group, 2 * (pair + 1) * group)
        both = all_queries[:, heads, :].astype(jnp.float32)
        done = []
        for part in range(2):
            head = 2 * pair + part
            q = both[:, part * group : (part + 1) * group, :]
            q = q.reshape(lanes, width).astype(jnp.bfloat16)
            scores = lax.dot_general(
                window[0, head],
                q,
                (((1,), (1,)), ((), ())),
                preferred_element_type=jnp.float32,
            )
            scores = scores * factor + bias[...]
            weights = jnp.exp2(scores - jnp.max(scores, axis=0, keepdims=True))
            total = jnp.sum(weights, axis=0, keepdims=True)
            mixed = lax.dot_general(
                window[1, head],
                weights.astype(jnp.bfloat16),
                (((0,), (0,)), ((), ())),
                preferred_element_type=jnp.float32,
            )
            mixed = (mixed / total).T
            done.append(mixed.reshape(block, group, width))
        out[:, heads, :] = jnp.concatenate(done, axis=1).astype(out.dtype)


def shards(queries, key_heads, value_head_rows, doc_lengths):
    stride, heads, width = queries.shape
    kv_count = key_heads.shape[1]
    block = stride // 2
    group = heads // kv_count
    devices = lax.axis_size("ctx")
    device = lax.axis_index("ctx").astype(jnp.int32)
    core = lax.axis_index("head").astype(jnp.int32)
    stretch = jnp.where(core == 0, device, 2 * devices - 1 - device)
    reach = 2**REACH_LOG
    stretches = 2 * devices
    span = (reach + 1) * block

    def owner(place):
        return 2 * place if place < devices else 2 * (stretches - 1 - place) + 1

    def swap(array):
        return lax.ppermute(array, "head", [(0, 1), (1, 0)])

    packed = jnp.stack([key_heads, value_head_rows])
    packed = packed.reshape(2, 2, block, kv_count, width).transpose(1, 0, 3, 2, 4)
    keep = lax.dynamic_index_in_dim(packed, core, 0, keepdims=False)
    given = swap(lax.dynamic_index_in_dim(packed, 1 - core, 0, keepdims=False))
    own = jnp.concatenate(
        [jnp.where(core == 0, keep, given), jnp.where(core == 0, given, keep)], axis=1
    )
    partner_queries = swap(lax.dynamic_slice_in_dim(queries, (1 - core) * block, block, 0))
    blocks = [own]
    for distance in range(1, reach + 1):
        pairs = [(owner(at), owner(at + distance)) for at in range(stretches - distance)]
        blocks.append(lax.ppermute(own, ("ctx", "head"), pairs))

    return pl.pallas_call(
        functools.partial(attention_kernel, group=group),
        out_shape=jax.ShapeDtypeStruct((block, 2 * heads, width), jnp.bfloat16),
        in_specs=[pl.BlockSpec(memory_space=pltpu.SMEM)] * 2
        + [pl.BlockSpec(memory_space=pl.ANY)] * (reach + 3),
        out_specs=pl.BlockSpec(memory_space=pltpu.VMEM),
        scratch_shapes=[
            pltpu.VMEM((block, 2 * heads, width), jnp.bfloat16),
            pltpu.VMEM((2, 2 * kv_count, span, width), jnp.bfloat16),
            pltpu.VMEM((span, block * group), jnp.float32),
            pltpu.SemaphoreType.DMA((reach + 3,)),
        ],
        compiler_params=pltpu.CompilerParams(vmem_limit_bytes=48 * 2**20),
        name="attention",
    )(doc_lengths, jnp.stack([stretch, core]), queries, partner_queries, *blocks)


def solution(mesh):
    in_specs = (P("ctx", "head", None), P("ctx", "head", None), P("ctx", "head", None), P())
    out_specs = P(("ctx", "head"), None, None)
    return jax.shard_map(shards, mesh=mesh, in_specs=in_specs, out_specs=out_specs, check_vma=False)
```

```python
import functools
import math

import jax
import jax.numpy as jnp
from jax import lax
from jax.experimental import pallas as pl
from jax.experimental.pallas import tpu as pltpu
from jax.sharding import PartitionSpec as P

REACH_LOG = 3
MASKED_SCORE = -1e30


def query_bounds(first_place, lanes, group, doc_lengths):
    place = first_place + lax.broadcasted_iota(jnp.int32, (1, lanes), 1) // group
    begin = jnp.zeros((1, lanes), jnp.int32)
    end = jnp.int32(0)
    for j in range(doc_lengths.shape[0]):
        end = end + doc_lengths[j]
        begin = jnp.where(place >= end, end, begin)
    return place, begin


def block_bias(stretch, nearest, count, block, group, doc_lengths):
    lanes = block * group
    first = stretch * block
    place, begin = query_bounds(first, lanes, group, doc_lengths)
    lowest = first - (nearest + count - 1) * block
    key_place = lowest + lax.broadcasted_iota(jnp.int32, (count * block, lanes), 0)
    allowed = (key_place >= begin) & (key_place <= place)
    return jnp.where(allowed, 0.0, MASKED_SCORE)


def load_queries(queries, partner_queries, core, block, group, slot, half):
    heads = slice(2 * slot * group, 2 * (slot + 1) * group)
    rows = pl.ds(core * block, block)
    both = (queries[rows, heads, :] if half == 0 else partner_queries[:, heads, :]).astype(
        jnp.float32
    )
    width = both.shape[2]
    return [
        both[:, part * group : (part + 1) * group, :]
        .reshape(block * group, width)
        .astype(jnp.bfloat16)
        for part in range(2)
    ]


def weigh(q, keys, values, bias, floor):
    factor = math.log2(math.e) / math.sqrt(q.shape[1])
    scores = lax.dot_general(
        keys, q, (((1,), (1,)), ((), ())), preferred_element_type=jnp.float32
    )
    scores = scores * factor + bias
    largest = jnp.max(scores, axis=0, keepdims=True)
    if floor is not None:
        largest = jnp.maximum(largest, floor)
    weights = jnp.exp2(scores - largest)
    total = jnp.sum(weights, axis=0, keepdims=True)
    mixed = lax.dot_general(
        values,
        weights.astype(jnp.bfloat16),
        (((0,), (0,)), ((), ())),
        preferred_element_type=jnp.float32,
    )
    return largest, total, mixed


def near_kernel(doc_lengths, position, queries, partner_queries, *refs, group):
    blocks, (peak, sums, mixes, bias) = refs[:-4], refs[-4:]
    stretch, core = position[0], position[1]
    kv_count, block = blocks[0].shape[1:3]
    bias[...] = block_bias(stretch, 0, len(blocks), block, group, doc_lengths)
    for half in range(2):
        base = (core if half == 0 else 1 - core) * (kv_count // 2)
        for pair in range(kv_count // 4):
            both = load_queries(queries, partner_queries, core, block, group, pair, half)
            for part in range(2):
                head = base + 2 * pair + part
                slot = half * (kv_count // 2) + 2 * pair + part
                keys = jnp.concatenate([ref[0, head] for ref in blocks[::-1]], axis=0)
                values = jnp.concatenate([ref[1, head] for ref in blocks[::-1]], axis=0)
                largest, total, mixed = weigh(both[part], keys, values, bias[...], None)
                peak[slot] = largest
                sums[slot] = total
                mixes[slot] = mixed


def far_kernel(
    doc_lengths, position, queries, partner_queries, far, peak, sums, mixes, out, bias, *, group
):
    stretch, core = position[0], position[1]
    count, _, kv_count, block, width = far.shape
    half_heads = kv_count * group // 2
    bias[...] = block_bias(stretch, count + 1, count, block, group, doc_lengths)
    for half in range(2):
        side = core if half == 0 else 1 - core
        base = side * (kv_count // 2)
        for pair in range(kv_count // 4):
            both = load_queries(queries, partner_queries, core, block, group, pair, half)
            done = []
            for part in range(2):
                head = base + 2 * pair + part
                slot = half * (kv_count // 2) + 2 * pair + part
                keys = far[:, 0, head].reshape(count * block, width)
                values = far[:, 1, head].reshape(count * block, width)
                earlier = peak[slot]
                largest, total, mixed = weigh(both[part], keys, values, bias[...], earlier)
                shrink = jnp.exp2(earlier - largest)
                total = total + sums[slot] * shrink
                mixed = (mixed + mixes[slot] * shrink) / total
                done.append(mixed.T.reshape(block, group, width))
            begin = pl.multiple_of(side * half_heads + 2 * pair * group, 2 * group)
            out[:, pl.ds(begin, 2 * group), :] = jnp.concatenate(done, axis=1).astype(out.dtype)


def shards(queries, key_heads, value_head_rows, doc_lengths):
    stride, heads, width = queries.shape
    kv_half = key_heads.shape[1]
    kv_count = 2 * kv_half
    block = stride // 2
    group = heads // kv_half
    lanes = block * group
    devices = lax.axis_size("ctx")
    device = lax.axis_index("ctx").astype(jnp.int32)
    core = lax.axis_index("head").astype(jnp.int32)
    stretch = jnp.where(core == 0, device, 2 * devices - 1 - device)
    stretches = 2 * devices
    jump = 2**REACH_LOG // 2

    def owner(place):
        return 2 * place if place < devices else 2 * (stretches - 1 - place) + 1

    def swap(array):
        return lax.ppermute(array, "head", [(0, 1), (1, 0)])

    def from_below(array, distance):
        pairs = [(owner(at), owner(at + distance)) for at in range(stretches - distance)]
        return lax.ppermute(array, ("ctx", "head"), pairs)

    packed = jnp.stack([key_heads, value_head_rows])
    packed = packed.reshape(2, 2, block, kv_half, width).transpose(1, 0, 3, 2, 4)
    keep = lax.dynamic_index_in_dim(packed, core, 0, keepdims=False)
    given = swap(lax.dynamic_index_in_dim(packed, 1 - core, 0, keepdims=False))
    own = jnp.concatenate(
        [jnp.where(core == 0, keep, given), jnp.where(core == 0, given, keep)], axis=1
    )
    partner_queries = swap(lax.dynamic_slice_in_dim(queries, (1 - core) * block, block, 0))
    blocks = [own] + [from_below(own, distance) for distance in range(1, jump + 1)]
    far = from_below(jnp.stack(blocks[:0:-1]), jump)

    position = jnp.stack([stretch, core])
    smem = pl.BlockSpec(memory_space=pltpu.SMEM)
    vmem = pl.BlockSpec(memory_space=pltpu.VMEM)
    params = pltpu.CompilerParams(vmem_limit_bytes=40 * 2**20)

    def cost(keys):
        work = kv_count * keys * lanes
        return pl.CostEstimate(
            flops=4 * work * width, bytes_accessed=4 * 2**20, transcendentals=work
        )

    state = pl.pallas_call(
        functools.partial(near_kernel, group=group),
        out_shape=[
            jax.ShapeDtypeStruct((kv_count, 1, lanes), jnp.float32),
            jax.ShapeDtypeStruct((kv_count, 1, lanes), jnp.float32),
            jax.ShapeDtypeStruct((kv_count, width, lanes), jnp.float32),
        ],
        in_specs=[smem] * 2 + [vmem] * (jump + 3),
        out_specs=[vmem] * 3,
        scratch_shapes=[pltpu.VMEM(((jump + 1) * block, lanes), jnp.float32)],
        compiler_params=params,
        cost_estimate=cost((jump + 1) * block),
        name="near",
    )(doc_lengths, position, queries, partner_queries, *blocks)
    return pl.pallas_call(
        functools.partial(far_kernel, group=group),
        out_shape=jax.ShapeDtypeStruct((block, 2 * heads, width), jnp.bfloat16),
        in_specs=[smem] * 2 + [vmem] * 6,
        out_specs=vmem,
        scratch_shapes=[pltpu.VMEM((jump * block, lanes), jnp.float32)],
        compiler_params=params,
        cost_estimate=cost(jump * block),
        name="far",
    )(doc_lengths, position, queries, partner_queries, far, *state)


def solution(mesh):
    in_specs = (P("ctx", "head", None), P("ctx", "head", None), P("ctx", "head", None), P())
    out_specs = P(("ctx", "head"), None, None)
    return jax.shard_map(shards, mesh=mesh, in_specs=in_specs, out_specs=out_specs, check_vma=False)
```

```python
import functools
import math

import jax
import jax.numpy as jnp
from jax import lax
from jax.experimental import pallas as pl
from jax.experimental.pallas import tpu as pltpu
from jax.sharding import PartitionSpec as P

REACH_LOG = 3
MASKED_SCORE = -1e30


def query_bounds(first_place, lanes, group, doc_lengths):
    place = first_place + lax.broadcasted_iota(jnp.int32, (1, lanes), 1) // group
    begin = jnp.zeros((1, lanes), jnp.int32)
    end = jnp.int32(0)
    for j in range(doc_lengths.shape[0]):
        end = end + doc_lengths[j]
        begin = jnp.where(place >= end, end, begin)
    return place, begin


def block_bias(stretch, distance, block, group, doc_lengths):
    lanes = block * group
    first = stretch * block
    place, begin = query_bounds(first, lanes, group, doc_lengths)
    key_place = first - distance * block + lax.broadcasted_iota(jnp.int32, (block, lanes), 0)
    allowed = (key_place >= begin) & (key_place <= place)
    return jnp.where(allowed, 0.0, MASKED_SCORE)


def weigh(q, keys, values, bias, floor):
    factor = math.log2(math.e) / math.sqrt(q.shape[1])
    scores = lax.dot_general(
        keys, q, (((1,), (1,)), ((), ())), preferred_element_type=jnp.float32
    )
    scores = scores * factor + bias
    largest = jnp.max(scores, axis=0, keepdims=True)
    if floor is not None:
        largest = jnp.maximum(largest, floor)
    weights = jnp.exp2(scores - largest)
    total = jnp.sum(weights, axis=0, keepdims=True)
    mixed = lax.dot_general(
        values,
        weights.astype(jnp.bfloat16),
        (((0,), (0,)), ((), ())),
        preferred_element_type=jnp.float32,
    )
    return largest, total, mixed


def stage_kernel(doc_lengths, position, *refs, group, arrays, pieces, begins, ends):
    stretch, core = position[0], position[1]
    refs = list(refs)

    def take(count):
        taken = refs[:count]
        del refs[:count]
        return taken

    if begins:
        own_queries, partner_queries = take(2)
    else:
        (folded,) = take(1)
    blocks = take(arrays)
    earlier = None if begins else take(3)
    if ends:
        (out,) = take(1)
    else:
        if begins:
            (folded,) = take(1)
        later = take(3)
    (bias,) = take(1)
    if ends:
        staged, sems = take(2)
    kv_count, lanes, width = folded.shape
    block = lanes // group
    half_heads = kv_count * group // 2

    def gather(kind, head):
        parts = [
            blocks[at][kind, head] if index is None else blocks[at][index, kind, head]
            for at, index, _ in pieces
        ]
        return jnp.concatenate(parts, axis=0)

    for row, (_, _, distance) in enumerate(pieces):
        bias[row * block : (row + 1) * block, :] = block_bias(
            stretch, distance, block, group, doc_lengths
        )
    copies = []
    for half in range(2):
        side = core if half == 0 else 1 - core
        for pair in range(kv_count // 4):
            if begins:
                heads = slice(2 * pair * group, 2 * (pair + 1) * group)
                if half == 0:
                    both = own_queries[pl.ds(core * block, block), heads, :]
                else:
                    both = partner_queries[:, heads, :]
                both = both.astype(jnp.float32)
            done = []
            for part in range(2):
                head = side * (kv_count // 2) + 2 * pair + part
                slot = half * (kv_count // 2) + 2 * pair + part
                if begins:
                    q = both[:, part * group : (part + 1) * group, :]
                    q = q.reshape(lanes, width).astype(jnp.bfloat16)
                    folded[slot] = q
                else:
                    q = folded[slot]
                floor = None if begins else earlier[0][slot]
                largest, total, mixed = weigh(
                    q, gather(0, head), gather(1, head), bias[...], floor
                )
                if not begins:
                    shrink = jnp.exp2(floor - largest)
                    total = total + earlier[1][slot] * shrink
                    mixed = mixed + earlier[2][slot] * shrink
                if ends:
                    done.append((mixed / total).T.reshape(block, group, width))
                else:
                    later[0][slot] = largest
                    later[1][slot] = total
                    later[2][slot] = mixed
            if ends:
                number = half * (kv_count // 4) + pair
                staged[number] = jnp.concatenate(done, axis=1).astype(staged.dtype)
                begin = pl.multiple_of(side * half_heads + 2 * pair * group, 2 * group)
                copies.append(
                    pltpu.make_async_copy(
                        staged.at[number], out.at[:, pl.ds(begin, 2 * group)], sems.at[number]
                    )
                )
                copies[-1].start()
    for copy in copies:
        copy.wait()


def run_stage(name, scalars, queries, blocks, pieces, state, shape):
    block, kv_count, group, width = shape
    lanes = block * group
    begins, ends = state is None, name == "finish"
    smem = pl.BlockSpec(memory_space=pltpu.SMEM)
    vmem = pl.BlockSpec(memory_space=pltpu.VMEM)
    rows = len(pieces) * block
    scratch = [pltpu.VMEM((rows, lanes), jnp.float32)]
    if ends:
        out_shape = jax.ShapeDtypeStruct((block, kv_count * group, width), jnp.bfloat16)
        out_specs = pl.BlockSpec(memory_space=pl.ANY)
        scratch += [
            pltpu.VMEM((kv_count // 2, block, 2 * group, width), jnp.bfloat16),
            pltpu.SemaphoreType.DMA((kv_count // 2,)),
        ]
    else:
        out_shape = [
            jax.ShapeDtypeStruct((kv_count, 1, lanes), jnp.float32),
            jax.ShapeDtypeStruct((kv_count, 1, lanes), jnp.float32),
            jax.ShapeDtypeStruct((kv_count, width, lanes), jnp.float32),
        ]
        if begins:
            out_shape.insert(0, jax.ShapeDtypeStruct((kv_count, lanes, width), jnp.bfloat16))
        out_specs = [vmem] * len(out_shape)
    operands = [*queries, *blocks, *([] if begins else state)]
    work = kv_count * rows * lanes
    return pl.pallas_call(
        functools.partial(
            stage_kernel,
            group=group,
            arrays=len(blocks),
            pieces=pieces,
            begins=begins,
            ends=ends,
        ),
        out_shape=out_shape,
        in_specs=[smem] * 2 + [vmem] * len(operands),
        out_specs=out_specs,
        scratch_shapes=scratch,
        compiler_params=pltpu.CompilerParams(vmem_limit_bytes=32 * 2**20),
        cost_estimate=pl.CostEstimate(
            flops=4 * work * width, bytes_accessed=4 * 2**20, transcendentals=work
        ),
        name=name,
    )(*scalars, *operands)


def shards(queries, key_heads, value_head_rows, doc_lengths):
    stride, heads, width = queries.shape
    kv_half = key_heads.shape[1]
    block = stride // 2
    group = heads // kv_half
    devices = lax.axis_size("ctx")
    device = lax.axis_index("ctx").astype(jnp.int32)
    core = lax.axis_index("head").astype(jnp.int32)
    stretch = jnp.where(core == 0, device, 2 * devices - 1 - device)
    stretches = 2 * devices

    def owner(place):
        return 2 * place if place < devices else 2 * (stretches - 1 - place) + 1

    def swap(array):
        return lax.ppermute(array, "head", [(0, 1), (1, 0)])

    def from_below(array, distance):
        pairs = [(owner(at), owner(at + distance)) for at in range(stretches - distance)]
        return lax.ppermute(array, ("ctx", "head"), pairs)

    packed = jnp.stack([key_heads, value_head_rows])
    packed = packed.reshape(2, 2, block, kv_half, width).transpose(1, 0, 3, 2, 4)
    keep = lax.dynamic_index_in_dim(packed, core, 0, keepdims=False)
    given = swap(lax.dynamic_index_in_dim(packed, 1 - core, 0, keepdims=False))
    own = jnp.concatenate(
        [jnp.where(core == 0, keep, given), jnp.where(core == 0, given, keep)], axis=1
    )
    partner_queries = swap(lax.dynamic_slice_in_dim(queries, (1 - core) * block, block, 0))
    by_four = from_below(own, 4)
    by_one = from_below(own, 1)
    own, partner_queries = lax.optimization_barrier((own, partner_queries))
    by_two = from_below(own, 2)
    by_three = from_below(own, 3)
    outer = from_below(jnp.stack([by_four, by_one]), 4)
    inner = from_below(jnp.stack([by_three, by_two]), 4)

    scalars = (doc_lengths, jnp.stack([stretch, core]))
    shape = (block, 2 * kv_half, group, width)
    near = tuple((at, None, 4 - at) for at in range(5))
    folded, *state = run_stage(
        "near",
        scalars,
        (queries, partner_queries),
        (by_four, by_three, by_two, by_one, own),
        near,
        None,
        shape,
    )
    state = run_stage("outer", scalars, (folded,), (outer,), ((0, 0, 8), (0, 1, 5)), state, shape)
    return run_stage("finish", scalars, (folded,), (inner,), ((0, 0, 7), (0, 1, 6)), state, shape)


def solution(mesh):
    in_specs = (P("ctx", "head", None), P("ctx", "head", None), P("ctx", "head", None), P())
    out_specs = P(("ctx", "head"), None, None)
    return jax.shard_map(shards, mesh=mesh, in_specs=in_specs, out_specs=out_specs, check_vma=False)
```

```python
import functools
import math

import jax
import jax.numpy as jnp
from jax import lax
from jax.experimental import pallas as pl
from jax.experimental.pallas import tpu as pltpu
from jax.sharding import PartitionSpec as P

REACH_LOG = 3
MASKED_SCORE = -1e30

EARLY_CHOICES = ((2, (2, 0, 2, 2)), (1, (3, 1, 1, 1)))
LATE_CHOICES = ((3, (2, 2, 3, 2)), (0, (1, 1, 2, 0)))
FAR_DISTANCES = (7, 6, 8, 5)
EARLY_TARGETS = (0, 3, 1, 2)
LATE_TARGETS = (1, 2, 0, 3)
TURN_DISTANCES = ((7, 8, 6, 5), (6, 5, 8, 7), (6, 5, 8, 7), (6, 8, 7, 5))


def query_bounds(first_place, lanes, group, doc_lengths):
    place = first_place + lax.broadcasted_iota(jnp.int32, (1, lanes), 1) // group
    begin = jnp.zeros((1, lanes), jnp.int32)
    end = jnp.int32(0)
    for j in range(doc_lengths.shape[0]):
        end = end + doc_lengths[j]
        begin = jnp.where(place >= end, end, begin)
    return place, begin


def block_bias(stretch, distance, block, group, doc_lengths):
    lanes = block * group
    first = stretch * block
    place, begin = query_bounds(first, lanes, group, doc_lengths)
    key_place = first - distance * block + lax.broadcasted_iota(jnp.int32, (block, lanes), 0)
    allowed = (key_place >= begin) & (key_place <= place)
    return jnp.where(allowed, 0.0, MASKED_SCORE)


def score(q, keys, bias):
    factor = math.log2(math.e) / math.sqrt(q.shape[1])
    scores = lax.dot_general(
        keys, q, (((1,), (1,)), ((), ())), preferred_element_type=jnp.float32
    )
    return scores * factor + bias


def mix(values, weights):
    return lax.dot_general(
        values,
        weights.astype(jnp.bfloat16),
        (((0,), (0,)), ((), ())),
        preferred_element_type=jnp.float32,
    )


def stage_setup(position, bias, distances, block, group, doc_lengths):
    for row, distance in enumerate(distances):
        bias[row * block : (row + 1) * block, :] = block_bias(
            position[0], distance, block, group, doc_lengths
        )


def bundle_kernel(position, *refs, devices, choices):
    candidates, out = refs[:-1], refs[-1]
    source = position[0] - (devices - 4)
    for slot, (usual, special) in enumerate(choices):
        for candidate, ref in enumerate(candidates):
            chosen = jnp.bool_(candidate == usual)
            for row, number in enumerate(special):
                chosen = jnp.where(source == row, number == candidate, chosen)

            @pl.when(chosen)
            def _(slot=slot, ref=ref):
                out[slot] = ref[...]


def near_kernel(doc_lengths, position, queries, partner_queries, *refs, group):
    blocks, (folded, peak, sums, mixes, bias) = refs[:-5], refs[-5:]
    core = position[1]
    kv_count, block, width = blocks[0].shape[1:]
    lanes = block * group
    stage_setup(position, bias, range(len(blocks)), block, group, doc_lengths)

    def gather(kind, head):
        return jnp.concatenate([ref[kind, head] for ref in blocks], axis=0)

    for half in range(2):
        side = core if half == 0 else 1 - core
        for pair in range(kv_count // 4):
            heads = slice(2 * pair * group, 2 * (pair + 1) * group)
            if half == 0:
                both = queries[pl.ds(core * block, block), heads, :]
            else:
                both = partner_queries[:, heads, :]
            both = both.astype(jnp.float32)
            qs = [
                both[:, part * group : (part + 1) * group, :]
                .reshape(lanes, width)
                .astype(jnp.bfloat16)
                for part in range(2)
            ]
            first_head = side * (kv_count // 2) + 2 * pair
            slots = [half * (kv_count // 2) + 2 * pair + part for part in range(2)]
            scores = [
                score(q, gather(0, first_head + part), bias[...]) for part, q in enumerate(qs)
            ]
            largest = [jnp.max(each, axis=0, keepdims=True) for each in scores]
            weights = [jnp.exp2(each - top) for each, top in zip(scores, largest)]
            for part, slot in enumerate(slots):
                folded[slot] = qs[part]
                peak[slot] = largest[part]
                sums[slot] = jnp.sum(weights[part], axis=0, keepdims=True)
                mixes[slot] = mix(gather(1, first_head + part), weights[part])


def far_kernel(
    doc_lengths,
    position,
    folded,
    peak,
    sums,
    mixes,
    early,
    late,
    out,
    bias,
    staged,
    sems,
    *,
    devices,
    group,
):
    core = position[1]
    _, _, kv_count, block, width = early.shape
    lanes = block * group
    half_heads = kv_count * group // 2
    turn = position[0] - devices
    distances = []
    for column, distance in enumerate(FAR_DISTANCES):
        for row, special in enumerate(TURN_DISTANCES):
            distance = jnp.where(turn == row, special[column], distance)
        distances.append(distance)
    stage_setup(position, bias, distances, block, group, doc_lengths)

    def gather(kind, head):
        return jnp.concatenate(
            [ref[index, kind, head] for ref in (early, late) for index in range(2)], axis=0
        )

    copies = []
    for half in range(2):
        side = core if half == 0 else 1 - core
        for pair in range(kv_count // 4):
            first_head = side * (kv_count // 2) + 2 * pair
            slots = [half * (kv_count // 2) + 2 * pair + part for part in range(2)]
            scores = [
                score(folded[slot], gather(0, first_head + part), bias[...])
                for part, slot in enumerate(slots)
            ]
            largest = [
                jnp.maximum(jnp.max(each, axis=0, keepdims=True), peak[slot])
                for each, slot in zip(scores, slots)
            ]
            weights = [jnp.exp2(each - top) for each, top in zip(scores, largest)]
            shrinks = [jnp.exp2(peak[slot] - top) for slot, top in zip(slots, largest)]
            scales = [
                1.0 / (jnp.sum(each, axis=0, keepdims=True) + sums[slot] * shrink)
                for each, slot, shrink in zip(weights, slots, shrinks)
            ]
            mixed = [
                mix(gather(1, first_head + part), each) for part, each in enumerate(weights)
            ]
            done = [
                (each * scale + mixes[slot] * (shrink * scale)).T.reshape(block, group, width)
                for each, slot, shrink, scale in zip(mixed, slots, shrinks, scales)
            ]
            number = half * (kv_count // 4) + pair
            staged[number] = jnp.concatenate(done, axis=1).astype(staged.dtype)
            begin = pl.multiple_of(side * half_heads + 2 * pair * group, 2 * group)
            copy = pltpu.make_async_copy(
                staged.at[number], out.at[:, pl.ds(begin, 2 * group)], sems.at[number]
            )
            copy.start()
            copies.append(copy)
    for copy in copies:
        copy.wait()


def shards(queries, key_heads, value_head_rows, doc_lengths):
    stride, heads, width = queries.shape
    kv_half = key_heads.shape[1]
    kv_count = 2 * kv_half
    block = stride // 2
    group = heads // kv_half
    lanes = block * group
    devices = lax.axis_size("ctx")
    device = lax.axis_index("ctx").astype(jnp.int32)
    core = lax.axis_index("head").astype(jnp.int32)
    stretch = jnp.where(core == 0, device, 2 * devices - 1 - device)
    stretches = 2 * devices

    def owner(place):
        return 2 * place if place < devices else 2 * (stretches - 1 - place) + 1

    def swap(array):
        return lax.ppermute(array, "head", [(0, 1), (1, 0)])

    def from_below(array, distance, turned=()):
        target = {at: at + distance for at in range(stretches - distance)}
        for number, to in enumerate(turned):
            target[devices - 4 + number] = devices + to
        pairs = [(owner(at), owner(to)) for at, to in target.items()]
        return lax.ppermute(array, ("ctx", "head"), pairs)

    packed = jnp.stack([key_heads, value_head_rows])
    packed = packed.reshape(2, 2, block, kv_half, width).transpose(1, 0, 3, 2, 4)
    keep = lax.dynamic_index_in_dim(packed, core, 0, keepdims=False)
    given = swap(lax.dynamic_index_in_dim(packed, 1 - core, 0, keepdims=False))
    own = jnp.concatenate(
        [jnp.where(core == 0, keep, given), jnp.where(core == 0, given, keep)], axis=1
    )
    partner_queries = swap(lax.dynamic_slice_in_dim(queries, (1 - core) * block, block, 0))
    by_three = from_below(own, 3)
    own, partner_queries = lax.optimization_barrier((own, partner_queries))
    by_two = from_below(own, 2)
    by_four = from_below(own, 4)
    own, by_three = lax.optimization_barrier((own, by_three))
    by_one = from_below(own, 1)

    scalars = (doc_lengths, jnp.stack([stretch, core]))
    vmem = pl.BlockSpec(memory_space=pltpu.VMEM)

    def bundle(name, candidates, choices):
        return pl.pallas_call(
            functools.partial(bundle_kernel, devices=devices, choices=choices),
            out_shape=jax.ShapeDtypeStruct((2, *own.shape), own.dtype),
            in_specs=[pl.BlockSpec(memory_space=pltpu.SMEM)] + [vmem] * len(candidates),
            out_specs=vmem,
            compiler_params=pltpu.CompilerParams(vmem_limit_bytes=6 * 2**20),
            name=name,
        )(scalars[1], *candidates)

    early = from_below(
        bundle("early", (own, by_two, by_three, by_four), EARLY_CHOICES), 4, EARLY_TARGETS
    )
    late = from_below(
        bundle("late", (by_one, by_two, by_three, by_four), LATE_CHOICES), 4, LATE_TARGETS
    )

    blocks = (own, by_one, by_two, by_three, by_four)
    smem = pl.BlockSpec(memory_space=pltpu.SMEM)
    params = pltpu.CompilerParams(vmem_limit_bytes=14 * 2**20)

    def cost(count):
        work = kv_count * count * block * lanes
        return pl.CostEstimate(
            flops=4 * work * width, bytes_accessed=4 * 2**20, transcendentals=work
        )

    state = pl.pallas_call(
        functools.partial(near_kernel, group=group),
        out_shape=[
            jax.ShapeDtypeStruct((kv_count, lanes, width), jnp.bfloat16),
            jax.ShapeDtypeStruct((kv_count, 1, lanes), jnp.float32),
            jax.ShapeDtypeStruct((kv_count, 1, lanes), jnp.float32),
            jax.ShapeDtypeStruct((kv_count, width, lanes), jnp.float32),
        ],
        in_specs=[smem] * 2 + [vmem] * (2 + len(blocks)),
        out_specs=[vmem] * 4,
        scratch_shapes=[pltpu.VMEM((len(blocks) * block, lanes), jnp.float32)],
        compiler_params=params,
        cost_estimate=cost(len(blocks)),
        name="near",
    )(*scalars, queries, partner_queries, *blocks)
    return pl.pallas_call(
        functools.partial(far_kernel, devices=devices, group=group),
        out_shape=jax.ShapeDtypeStruct((block, 2 * heads, width), jnp.bfloat16),
        in_specs=[smem] * 2 + [vmem] * 6,
        out_specs=pl.BlockSpec(memory_space=pl.ANY),
        scratch_shapes=[
            pltpu.VMEM((4 * block, lanes), jnp.float32),
            pltpu.VMEM((kv_count // 2, block, 2 * group, width), jnp.bfloat16),
            pltpu.SemaphoreType.DMA((kv_count // 2,)),
        ],
        compiler_params=params,
        cost_estimate=cost(4),
        name="far",
    )(*scalars, *state, early, late)


def solution(mesh):
    in_specs = (P("ctx", "head", None), P("ctx", "head", None), P("ctx", "head", None), P())
    out_specs = P(("ctx", "head"), None, None)
    return jax.shard_map(shards, mesh=mesh, in_specs=in_specs, out_specs=out_specs, check_vma=False)
```

```python
import functools
import math

import jax
import jax.numpy as jnp
from jax import lax
from jax.experimental import pallas as pl
from jax.experimental.pallas import tpu as pltpu
from jax.sharding import PartitionSpec as P

REACH_LOG = 3
MASKED_SCORE = -1e30

EARLY_CHOICES = ((2, (2, 0, 2, 2)), (1, (3, 1, 1, 1)))
LATE_CHOICES = ((3, (2, 2, 3, 2)), (0, (1, 1, 2, 0)))
FAR_DISTANCES = (7, 6, 8, 5)
EARLY_TARGETS = (0, 3, 1, 2)
LATE_TARGETS = (1, 2, 0, 3)
TURN_DISTANCES = ((7, 8, 6, 5), (6, 5, 8, 7), (6, 5, 8, 7), (6, 8, 7, 5))


def query_bounds(first_place, lanes, group, doc_lengths):
    place = first_place + lax.broadcasted_iota(jnp.int32, (1, lanes), 1) // group
    begin = jnp.zeros((1, lanes), jnp.int32)
    end = jnp.int32(0)
    for j in range(doc_lengths.shape[0]):
        end = end + doc_lengths[j]
        begin = jnp.where(place >= end, end, begin)
    return place, begin


def block_bias(stretch, distance, block, group, doc_lengths):
    lanes = block * group
    first = stretch * block
    place, begin = query_bounds(first, lanes, group, doc_lengths)
    key_place = first - distance * block + lax.broadcasted_iota(jnp.int32, (block, lanes), 0)
    allowed = (key_place >= begin) & (key_place <= place)
    return jnp.where(allowed, 0.0, MASKED_SCORE)


def score(q, keys, bias):
    factor = math.log2(math.e) / math.sqrt(q.shape[1])
    scores = lax.dot_general(
        keys, q, (((1,), (1,)), ((), ())), preferred_element_type=jnp.float32
    )
    return scores * factor + bias


def mix(values, weights):
    return lax.dot_general(
        values,
        weights.astype(jnp.bfloat16),
        (((0,), (0,)), ((), ())),
        preferred_element_type=jnp.float32,
    )


def stage_setup(position, bias, distances, block, group, doc_lengths):
    for row, distance in enumerate(distances):
        bias[row * block : (row + 1) * block, :] = block_bias(
            position[0], distance, block, group, doc_lengths
        )


def bundle_kernel(position, *refs, devices, choices):
    candidates, out = refs[:-1], refs[-1]
    source = position[0] - (devices - 4)
    for slot, (usual, special) in enumerate(choices):
        for candidate, ref in enumerate(candidates):
            chosen = jnp.bool_(candidate == usual)
            for row, number in enumerate(special):
                chosen = jnp.where(source == row, number == candidate, chosen)

            @pl.when(chosen)
            def _(slot=slot, ref=ref):
                out[slot] = ref[...]


def near_kernel(doc_lengths, position, queries, partner_queries, *refs, group):
    blocks, (folded, peak, sums, mixes, bias) = refs[:-5], refs[-5:]
    core = position[1]
    kv_count, block, width = blocks[0].shape[1:]
    lanes = block * group
    stage_setup(position, bias, range(len(blocks)), block, group, doc_lengths)

    def gather(kind, head):
        return jnp.concatenate([ref[kind, head] for ref in blocks], axis=0)

    for half in range(2):
        side = core if half == 0 else 1 - core
        for pair in range(kv_count // 4):
            heads = slice(2 * pair * group, 2 * (pair + 1) * group)
            if half == 0:
                both = queries[pl.ds(core * block, block), heads, :]
            else:
                both = partner_queries[:, heads, :]
            both = both.astype(jnp.float32)
            qs = [
                both[:, part * group : (part + 1) * group, :]
                .reshape(lanes, width)
                .astype(jnp.bfloat16)
                for part in range(2)
            ]
            first_head = side * (kv_count // 2) + 2 * pair
            slots = [half * (kv_count // 2) + 2 * pair + part for part in range(2)]
            scores = [
                score(q, gather(0, first_head + part), bias[...]) for part, q in enumerate(qs)
            ]
            largest = [jnp.max(each, axis=0, keepdims=True) for each in scores]
            weights = [jnp.exp2(each - top) for each, top in zip(scores, largest)]
            for part, slot in enumerate(slots):
                folded[slot] = qs[part]
                peak[slot] = largest[part]
                sums[slot] = jnp.sum(weights[part], axis=0, keepdims=True)
                mixes[slot] = mix(gather(1, first_head + part), weights[part])


def far_kernel(
    doc_lengths,
    position,
    folded,
    peak,
    sums,
    mixes,
    early,
    late,
    out,
    bias,
    staged,
    sems,
    *,
    devices,
    group,
):
    core = position[1]
    _, _, kv_count, block, width = early.shape
    lanes = block * group
    half_heads = kv_count * group // 2
    turn = position[0] - devices
    distances = []
    for column, distance in enumerate(FAR_DISTANCES):
        for row, special in enumerate(TURN_DISTANCES):
            distance = jnp.where(turn == row, special[column], distance)
        distances.append(distance)
    stage_setup(position, bias, distances, block, group, doc_lengths)

    def gather(kind, head):
        return jnp.concatenate(
            [ref[index, kind, head] for ref in (early, late) for index in range(2)], axis=0
        )

    copies = []
    for half in range(2):
        side = core if half == 0 else 1 - core
        for pair in range(kv_count // 4):
            first_head = side * (kv_count // 2) + 2 * pair
            slots = [half * (kv_count // 2) + 2 * pair + part for part in range(2)]
            scores = [
                score(folded[slot], gather(0, first_head + part), bias[...])
                for part, slot in enumerate(slots)
            ]
            largest = [
                jnp.maximum(jnp.max(each, axis=0, keepdims=True), peak[slot])
                for each, slot in zip(scores, slots)
            ]
            weights = [jnp.exp2(each - top) for each, top in zip(scores, largest)]
            shrinks = [jnp.exp2(peak[slot] - top) for slot, top in zip(slots, largest)]
            scales = [
                1.0 / (jnp.sum(each, axis=0, keepdims=True) + sums[slot] * shrink)
                for each, slot, shrink in zip(weights, slots, shrinks)
            ]
            mixed = [
                mix(gather(1, first_head + part), each) for part, each in enumerate(weights)
            ]
            done = [
                (each * scale + mixes[slot] * (shrink * scale)).T.reshape(block, group, width)
                for each, slot, shrink, scale in zip(mixed, slots, shrinks, scales)
            ]
            number = half * (kv_count // 4) + pair
            staged[number] = jnp.concatenate(done, axis=1).astype(staged.dtype)
            begin = pl.multiple_of(side * half_heads + 2 * pair * group, 2 * group)
            copy = pltpu.make_async_copy(
                staged.at[number], out.at[:, pl.ds(begin, 2 * group)], sems.at[number]
            )
            copy.start()
            copies.append(copy)
    for copy in copies:
        copy.wait()


def shards(queries, key_heads, value_head_rows, doc_lengths):
    stride, heads, width = queries.shape
    kv_half = key_heads.shape[1]
    kv_count = 2 * kv_half
    block = stride // 2
    group = heads // kv_half
    lanes = block * group
    devices = lax.axis_size("ctx")
    device = lax.axis_index("ctx").astype(jnp.int32)
    core = lax.axis_index("head").astype(jnp.int32)
    stretch = jnp.where(core == 0, device, 2 * devices - 1 - device)
    stretches = 2 * devices

    def owner(place):
        return 2 * place if place < devices else 2 * (stretches - 1 - place) + 1

    def swap(array):
        return lax.ppermute(array, "head", [(0, 1), (1, 0)])

    def from_below(array, distance, turned=()):
        target = {at: at + distance for at in range(stretches - distance)}
        for number, to in enumerate(turned):
            target[devices - 4 + number] = devices + to
        pairs = [(owner(at), owner(to)) for at, to in target.items()]
        return lax.ppermute(array, ("ctx", "head"), pairs)

    packed = jnp.stack([key_heads, value_head_rows])
    packed = packed.reshape(2, 2, block, kv_half, width).transpose(1, 0, 3, 2, 4)
    keep = lax.dynamic_index_in_dim(packed, core, 0, keepdims=False)
    given = swap(lax.dynamic_index_in_dim(packed, 1 - core, 0, keepdims=False))
    own = jnp.concatenate(
        [jnp.where(core == 0, keep, given), jnp.where(core == 0, given, keep)], axis=1
    )
    partner_queries = swap(lax.dynamic_slice_in_dim(queries, (1 - core) * block, block, 0))
    by_three = from_below(own, 3)
    own, partner_queries = lax.optimization_barrier((own, partner_queries))
    by_two = from_below(own, 2)
    by_four = from_below(own, 4)
    by_one = from_below(own, 1)

    scalars = (doc_lengths, jnp.stack([stretch, core]))
    vmem = pl.BlockSpec(memory_space=pltpu.VMEM)

    def bundle(name, candidates, choices):
        return pl.pallas_call(
            functools.partial(bundle_kernel, devices=devices, choices=choices),
            out_shape=jax.ShapeDtypeStruct((2, *own.shape), own.dtype),
            in_specs=[pl.BlockSpec(memory_space=pltpu.SMEM)] + [vmem] * len(candidates),
            out_specs=vmem,
            compiler_params=pltpu.CompilerParams(vmem_limit_bytes=6 * 2**20),
            name=name,
        )(scalars[1], *candidates)

    early = from_below(
        bundle("early", (own, by_two, by_three, by_four), EARLY_CHOICES), 4, EARLY_TARGETS
    )
    late = from_below(
        bundle("late", (by_one, by_two, by_three, by_four), LATE_CHOICES), 4, LATE_TARGETS
    )

    blocks = (own, by_one, by_two, by_three, by_four)
    smem = pl.BlockSpec(memory_space=pltpu.SMEM)
    params = pltpu.CompilerParams(vmem_limit_bytes=14 * 2**20)

    def cost(count):
        work = kv_count * count * block * lanes
        return pl.CostEstimate(
            flops=4 * work * width, bytes_accessed=4 * 2**20, transcendentals=work
        )

    state = pl.pallas_call(
        functools.partial(near_kernel, group=group),
        out_shape=[
            jax.ShapeDtypeStruct((kv_count, lanes, width), jnp.bfloat16),
            jax.ShapeDtypeStruct((kv_count, 1, lanes), jnp.float32),
            jax.ShapeDtypeStruct((kv_count, 1, lanes), jnp.float32),
            jax.ShapeDtypeStruct((kv_count, width, lanes), jnp.float32),
        ],
        in_specs=[smem] * 2 + [vmem] * (2 + len(blocks)),
        out_specs=[vmem] * 4,
        scratch_shapes=[pltpu.VMEM((len(blocks) * block, lanes), jnp.float32)],
        compiler_params=params,
        cost_estimate=cost(len(blocks)),
        name="near",
    )(*scalars, queries, partner_queries, *blocks)
    return pl.pallas_call(
        functools.partial(far_kernel, devices=devices, group=group),
        out_shape=jax.ShapeDtypeStruct((block, 2 * heads, width), jnp.bfloat16),
        in_specs=[smem] * 2 + [vmem] * 6,
        out_specs=pl.BlockSpec(memory_space=pl.ANY),
        scratch_shapes=[
            pltpu.VMEM((4 * block, lanes), jnp.float32),
            pltpu.VMEM((kv_count // 2, block, 2 * group, width), jnp.bfloat16),
            pltpu.SemaphoreType.DMA((kv_count // 2,)),
        ],
        compiler_params=params,
        cost_estimate=cost(4),
        name="far",
    )(*scalars, *state, early, late)


def solution(mesh):
    in_specs = (P("ctx", "head", None), P("ctx", "head", None), P("ctx", "head", None), P())
    out_specs = P(("ctx", "head"), None, None)
    return jax.shard_map(shards, mesh=mesh, in_specs=in_specs, out_specs=out_specs, check_vma=False)
```

```python
import functools
import math

import jax
import jax.numpy as jnp
from jax import lax
from jax.experimental import pallas as pl
from jax.experimental.pallas import tpu as pltpu
from jax.sharding import PartitionSpec as P

REACH_LOG = 3
MASKED_SCORE = -1e30


def query_bounds(first_place, lanes, group, doc_lengths):
    place = first_place + lax.broadcasted_iota(jnp.int32, (1, lanes), 1) // group
    begin = jnp.zeros((1, lanes), jnp.int32)
    end = jnp.int32(0)
    for j in range(doc_lengths.shape[0]):
        end = end + doc_lengths[j]
        begin = jnp.where(place >= end, end, begin)
    return place, begin


def block_bias(stretch, distance, block, group, doc_lengths):
    lanes = block * group
    first = stretch * block
    place, begin = query_bounds(first, lanes, group, doc_lengths)
    key_place = first - distance * block + lax.broadcasted_iota(jnp.int32, (block, lanes), 0)
    allowed = (key_place >= begin) & (key_place <= place)
    return jnp.where(allowed, 0.0, MASKED_SCORE)


def score(q, keys, bias):
    factor = math.log2(math.e) / math.sqrt(q.shape[1])
    scores = lax.dot_general(
        keys, q, (((1,), (1,)), ((), ())), preferred_element_type=jnp.float32
    )
    return scores * factor + bias


def mix(values, weights):
    return lax.dot_general(
        values,
        weights.astype(jnp.bfloat16),
        (((0,), (0,)), ((), ())),
        preferred_element_type=jnp.float32,
    )


def stage_kernel(doc_lengths, position, *refs, group, arrays, pieces, begins, ends):
    stretch, core = position[0], position[1]
    refs = list(refs)

    def take(count):
        taken = refs[:count]
        del refs[:count]
        return taken

    if begins:
        own_queries, partner_queries = take(2)
    else:
        (folded,) = take(1)
        peak, sums, mixes = take(3)
    blocks = take(arrays)
    if ends:
        (out,) = take(1)
    else:
        if begins:
            (folded,) = take(1)
        new_peak, new_sums, new_mixes = take(3)
    (bias,) = take(1)
    if ends:
        staged, sems = take(2)
    kv_count, lanes, width = folded.shape
    block = lanes // group
    half_heads = kv_count * group // 2

    def gather(kind, head):
        parts = [
            blocks[at][kind, head] if index is None else blocks[at][index, kind, head]
            for at, index, _ in pieces
        ]
        return jnp.concatenate(parts, axis=0)

    for row, (_, _, distance) in enumerate(pieces):
        bias[row * block : (row + 1) * block, :] = block_bias(
            stretch, distance, block, group, doc_lengths
        )
    copies = []
    for half in range(2):
        side = core if half == 0 else 1 - core
        for pair in range(kv_count // 4):
            first_head = side * (kv_count // 2) + 2 * pair
            slots = [half * (kv_count // 2) + 2 * pair + part for part in range(2)]
            if begins:
                heads = slice(2 * pair * group, 2 * (pair + 1) * group)
                if half == 0:
                    both = own_queries[pl.ds(core * block, block), heads, :]
                else:
                    both = partner_queries[:, heads, :]
                both = both.astype(jnp.float32)
                qs = [
                    both[:, part * group : (part + 1) * group, :]
                    .reshape(lanes, width)
                    .astype(jnp.bfloat16)
                    for part in range(2)
                ]
                for slot, q in zip(slots, qs):
                    folded[slot] = q
            else:
                qs = [folded[slot] for slot in slots]
            scores = [
                score(q, gather(0, first_head + part), bias[...]) for part, q in enumerate(qs)
            ]
            largest = [jnp.max(each, axis=0, keepdims=True) for each in scores]
            if not begins:
                largest = [jnp.maximum(top, peak[slot]) for top, slot in zip(largest, slots)]
            weights = [jnp.exp2(each - top) for each, top in zip(scores, largest)]
            totals = [jnp.sum(each, axis=0, keepdims=True) for each in weights]
            mixed = [
                mix(gather(1, first_head + part), each) for part, each in enumerate(weights)
            ]
            if not begins:
                shrinks = [jnp.exp2(peak[slot] - top) for slot, top in zip(slots, largest)]
                totals = [
                    total + sums[slot] * shrink
                    for total, slot, shrink in zip(totals, slots, shrinks)
                ]
            if not ends:
                for part, slot in enumerate(slots):
                    new_peak[slot] = largest[part]
                    new_sums[slot] = totals[part]
                    if begins:
                        new_mixes[slot] = mixed[part]
                    else:
                        new_mixes[slot] = mixed[part] + mixes[slot] * shrinks[part]
                continue
            scales = [1.0 / total for total in totals]
            done = [
                (each * scale + mixes[slot] * (shrink * scale)).T.reshape(block, group, width)
                for each, slot, shrink, scale in zip(mixed, slots, shrinks, scales)
            ]
            number = half * (kv_count // 4) + pair
            staged[number] = jnp.concatenate(done, axis=1).astype(staged.dtype)
            begin = pl.multiple_of(side * half_heads + 2 * pair * group, 2 * group)
            copy = pltpu.make_async_copy(
                staged.at[number], out.at[:, pl.ds(begin, 2 * group)], sems.at[number]
            )
            copy.start()
            copies.append(copy)
    for copy in copies:
        copy.wait()


def run_stage(name, scalars, queries, state, blocks, pieces, shape, ends=False):
    block, kv_count, group, width = shape
    lanes = block * group
    begins = state is None
    smem = pl.BlockSpec(memory_space=pltpu.SMEM)
    vmem = pl.BlockSpec(memory_space=pltpu.VMEM)
    rows = len(pieces) * block
    scratch = [pltpu.VMEM((rows, lanes), jnp.float32)]
    if ends:
        out_shape = jax.ShapeDtypeStruct((block, kv_count * group, width), jnp.bfloat16)
        out_specs = pl.BlockSpec(memory_space=pl.ANY)
        scratch += [
            pltpu.VMEM((kv_count // 2, block, 2 * group, width), jnp.bfloat16),
            pltpu.SemaphoreType.DMA((kv_count // 2,)),
        ]
    else:
        out_shape = [
            jax.ShapeDtypeStruct((kv_count, 1, lanes), jnp.float32),
            jax.ShapeDtypeStruct((kv_count, 1, lanes), jnp.float32),
            jax.ShapeDtypeStruct((kv_count, width, lanes), jnp.float32),
        ]
        if begins:
            out_shape.insert(0, jax.ShapeDtypeStruct((kv_count, lanes, width), jnp.bfloat16))
        out_specs = [vmem] * len(out_shape)
    operands = [*queries, *([] if begins else state), *blocks]
    work = kv_count * rows * lanes
    return pl.pallas_call(
        functools.partial(
            stage_kernel,
            group=group,
            arrays=len(blocks),
            pieces=pieces,
            begins=begins,
            ends=ends,
        ),
        out_shape=out_shape,
        in_specs=[smem] * 2 + [vmem] * len(operands),
        out_specs=out_specs,
        scratch_shapes=scratch,
        compiler_params=pltpu.CompilerParams(vmem_limit_bytes=14 * 2**20),
        cost_estimate=pl.CostEstimate(
            flops=4 * work * width, bytes_accessed=4 * 2**20, transcendentals=work
        ),
        name=name,
    )(*scalars, *operands)


def shards(queries, key_heads, value_head_rows, doc_lengths):
    stride, heads, width = queries.shape
    kv_half = key_heads.shape[1]
    block = stride // 2
    group = heads // kv_half
    devices = lax.axis_size("ctx")
    device = lax.axis_index("ctx").astype(jnp.int32)
    core = lax.axis_index("head").astype(jnp.int32)
    stretch = jnp.where(core == 0, device, 2 * devices - 1 - device)
    stretches = 2 * devices

    def owner(place):
        return 2 * place if place < devices else 2 * (stretches - 1 - place) + 1

    def swap(array):
        return lax.ppermute(array, "head", [(0, 1), (1, 0)])

    def from_below(array, distance):
        pairs = [(owner(at), owner(at + distance)) for at in range(stretches - distance)]
        return lax.ppermute(array, ("ctx", "head"), pairs)

    packed = jnp.stack([key_heads, value_head_rows])
    packed = packed.reshape(2, 2, block, kv_half, width).transpose(1, 0, 3, 2, 4)
    keep = lax.dynamic_index_in_dim(packed, core, 0, keepdims=False)
    given = swap(lax.dynamic_index_in_dim(packed, 1 - core, 0, keepdims=False))
    own = jnp.concatenate(
        [jnp.where(core == 0, keep, given), jnp.where(core == 0, given, keep)], axis=1
    )
    partner_queries = swap(lax.dynamic_slice_in_dim(queries, (1 - core) * block, block, 0))
    by_three = from_below(own, 3)
    own, partner_queries = lax.optimization_barrier((own, partner_queries))
    by_four = from_below(own, 4)
    by_one = from_below(own, 1)
    by_two = from_below(own, 2)
    early = from_below(jnp.stack([by_three, by_four]), 4)
    late = from_below(jnp.stack([by_one, by_two]), 4)

    scalars = (doc_lengths, jnp.stack([stretch, core]))
    shape = (block, 2 * kv_half, group, width)
    near = tuple((at, None, at) for at in range(5))
    folded, *state = run_stage(
        "near",
        scalars,
        (queries, partner_queries),
        None,
        (own, by_one, by_two, by_three, by_four),
        near,
        shape,
    )
    state = run_stage(
        "middle", scalars, (folded,), state, (early,), ((0, 0, 7), (0, 1, 8)), shape
    )
    return run_stage(
        "finish", scalars, (folded,), state, (late,), ((0, 0, 5), (0, 1, 6)), shape, ends=True
    )


def solution(mesh):
    in_specs = (P("ctx", "head", None), P("ctx", "head", None), P("ctx", "head", None), P())
    out_specs = P(("ctx", "head"), None, None)
    return jax.shard_map(shards, mesh=mesh, in_specs=in_specs, out_specs=out_specs, check_vma=False)
```

```python
import functools
import math

import jax
import jax.numpy as jnp
from jax import lax
from jax.experimental import pallas as pl
from jax.experimental.pallas import tpu as pltpu
from jax.sharding import PartitionSpec as P

REACH_LOG = 3
MASKED_SCORE = -1e30

EARLY_TARGETS = (0, 2, 3, 1)
LATE_TARGETS = (1, 3, 0, 2)
EARLY_CHOICES = ((1, (1, 1, 1, 1)), (2, (2, 0, 0, 2)))
LATE_CHOICES = ((1, (3, 1, 3, 3)), (2, (2, 0, 4, 4)))
EARLY_DISTANCES = ((7, (7, 5, 8, 8)), (8, (8, 6, 5, 5)))
LATE_DISTANCES = ((5, (5, 8, 6, 7)), (6, (6, 7, 7, 6)))


def query_bounds(first_place, lanes, group, doc_lengths):
    place = first_place + lax.broadcasted_iota(jnp.int32, (1, lanes), 1) // group
    begin = jnp.zeros((1, lanes), jnp.int32)
    end = jnp.int32(0)
    for j in range(doc_lengths.shape[0]):
        end = end + doc_lengths[j]
        begin = jnp.where(place >= end, end, begin)
    return place, begin


def block_bias(stretch, distance, block, group, doc_lengths):
    lanes = block * group
    first = stretch * block
    place, begin = query_bounds(first, lanes, group, doc_lengths)
    key_place = first - distance * block + lax.broadcasted_iota(jnp.int32, (block, lanes), 0)
    allowed = (key_place >= begin) & (key_place <= place)
    return jnp.where(allowed, 0.0, MASKED_SCORE)


def score(q, keys, bias):
    factor = math.log2(math.e) / math.sqrt(q.shape[1])
    scores = lax.dot_general(
        keys, q, (((1,), (1,)), ((), ())), preferred_element_type=jnp.float32
    )
    return scores * factor + bias


def mix(values, weights):
    return lax.dot_general(
        values,
        weights.astype(jnp.bfloat16),
        (((0,), (0,)), ((), ())),
        preferred_element_type=jnp.float32,
    )


def pack_kernel(keys, values, queries, keep, given, given_queries, staged, sems):
    core = lax.axis_index("head")
    block = given_queries.shape[0]
    kept_rows, given_rows = pl.ds(core * block, block), pl.ds((1 - core) * block, block)
    copies = [
        pltpu.make_async_copy(keys, staged.at[0], sems.at[0]),
        pltpu.make_async_copy(values, staged.at[1], sems.at[1]),
        pltpu.make_async_copy(queries.at[given_rows], given_queries, sems.at[2]),
    ]
    for copy in copies:
        copy.start()
    for kind in range(2):
        copies[kind].wait()
        for rows, out in ((given_rows, given), (kept_rows, keep)):
            part = staged[kind, rows].astype(jnp.float32)
            out[kind] = jnp.swapaxes(part, 0, 1).astype(out.dtype)
    copies[2].wait()


def bundle_kernel(position, *refs, devices, choices):
    candidates, out = refs[:-1], refs[-1]
    source = position[0] - (devices - 4)
    for slot, (usual, special) in enumerate(choices):
        for candidate, ref in enumerate(candidates):
            if candidate != usual and candidate not in special:
                continue
            chosen = jnp.bool_(candidate == usual)
            for row, number in enumerate(special):
                chosen = jnp.where(source == row, number == candidate, chosen)

            @pl.when(chosen)
            def _(slot=slot, ref=ref):
                out[slot] = ref[...]


def stage_kernel(doc_lengths, position, *refs, devices, group, arrays, pieces, begins, ends):
    step = 2 if begins else 4
    stretch, core = position[0], position[1]
    refs = list(refs)

    def take(count):
        taken = refs[:count]
        del refs[:count]
        return taken

    if begins:
        own_queries, partner_queries = take(2)
    else:
        (folded,) = take(1)
        peak, sums, mixes = take(3)
    blocks = take(arrays)
    if ends:
        (out,) = take(1)
    else:
        if begins:
            (folded,) = take(1)
        new_peak, new_sums, new_mixes = take(3)
    (bias,) = take(1)
    if ends:
        staged, sems = take(2)
    kv_count, lanes, width = folded.shape
    block = lanes // group

    def gather(kind, head):
        parts = [
            blocks[at][kind, head] if index is None else blocks[at][index, kind, head]
            for at, index, _ in pieces
        ]
        return jnp.concatenate(parts, axis=0)

    turn = stretch - devices
    for row, (_, _, (distance, special)) in enumerate(pieces):
        for number, other in enumerate(special):
            distance = jnp.where(turn == number, other, distance)
        bias[row * block : (row + 1) * block, :] = block_bias(
            stretch, distance, block, group, doc_lengths
        )
    copies = []
    for half in range(2):
        side = core if half == 0 else 1 - core
        for begin in range(0, kv_count // 2, step):
            first_head = side * (kv_count // 2) + begin
            slots = [half * (kv_count // 2) + begin + part for part in range(step)]
            if begins:
                heads = slice(begin * group, (begin + step) * group)
                if half == 0:
                    some = own_queries[pl.ds(core * block, block), heads, :]
                else:
                    some = partner_queries[:, heads, :]
                some = some.astype(jnp.float32)
                qs = [
                    some[:, part * group : (part + 1) * group, :]
                    .reshape(lanes, width)
                    .astype(jnp.bfloat16)
                    for part in range(step)
                ]
                for slot, q in zip(slots, qs):
                    folded[slot] = q
            else:
                qs = [folded[slot] for slot in slots]
            scores = [
                score(q, gather(0, first_head + part), bias[...]) for part, q in enumerate(qs)
            ]
            largest = [jnp.max(each, axis=0, keepdims=True) for each in scores]
            if not begins:
                largest = [jnp.maximum(top, peak[slot]) for top, slot in zip(largest, slots)]
            weights = [jnp.exp2(each - top) for each, top in zip(scores, largest)]
            totals = [jnp.sum(each, axis=0, keepdims=True) for each in weights]
            mixed = [
                mix(gather(1, first_head + part), each) for part, each in enumerate(weights)
            ]
            if not begins:
                shrinks = [jnp.exp2(peak[slot] - top) for slot, top in zip(slots, largest)]
                totals = [
                    total + sums[slot] * shrink
                    for total, slot, shrink in zip(totals, slots, shrinks)
                ]
            if not ends:
                for part, slot in enumerate(slots):
                    new_peak[slot] = largest[part]
                    new_sums[slot] = totals[part]
                    if begins:
                        new_mixes[slot] = mixed[part]
                    else:
                        new_mixes[slot] = mixed[part] + mixes[slot] * shrinks[part]
                continue
            scales = [1.0 / total for total in totals]
            done = [
                (each * scale + mixes[slot] * (shrink * scale)).T.reshape(block, group, width)
                for each, slot, shrink, scale in zip(mixed, slots, shrinks, scales)
            ]
            for part in range(0, step, 2):
                number = slots[part] // 2
                pair = jnp.concatenate(done[part : part + 2], axis=1)
                staged[number] = pair.astype(staged.dtype)
            for part in range(0, step, 2):
                number = slots[part] // 2
                first = pl.multiple_of((first_head + part) * group, 2 * group)
                copy = pltpu.make_async_copy(
                    staged.at[number], out.at[:, pl.ds(first, 2 * group)], sems.at[number]
                )
                copy.start()
                copies.append(copy)
    for copy in copies:
        copy.wait()


def run_stage(name, scalars, queries, state, blocks, pieces, shape, ends=False):
    devices, block, kv_count, group, width = shape
    lanes = block * group
    begins = state is None
    smem = pl.BlockSpec(memory_space=pltpu.SMEM)
    vmem = pl.BlockSpec(memory_space=pltpu.VMEM)
    rows = len(pieces) * block
    scratch = [pltpu.VMEM((rows, lanes), jnp.float32)]
    if ends:
        out_shape = jax.ShapeDtypeStruct((block, kv_count * group, width), jnp.bfloat16)
        out_specs = pl.BlockSpec(memory_space=pl.ANY)
        scratch += [
            pltpu.VMEM((kv_count // 2, block, 2 * group, width), jnp.bfloat16),
            pltpu.SemaphoreType.DMA((kv_count // 2,)),
        ]
    else:
        out_shape = [
            jax.ShapeDtypeStruct((kv_count, 1, lanes), jnp.float32),
            jax.ShapeDtypeStruct((kv_count, 1, lanes), jnp.float32),
            jax.ShapeDtypeStruct((kv_count, width, lanes), jnp.float32),
        ]
        if begins:
            out_shape.insert(0, jax.ShapeDtypeStruct((kv_count, lanes, width), jnp.bfloat16))
        out_specs = [vmem] * len(out_shape)
    operands = [*queries, *([] if begins else state), *blocks]
    work = kv_count * rows * lanes
    return pl.pallas_call(
        functools.partial(
            stage_kernel,
            devices=devices,
            group=group,
            arrays=len(blocks),
            pieces=pieces,
            begins=begins,
            ends=ends,
        ),
        out_shape=out_shape,
        in_specs=[smem] * 2 + [vmem] * len(operands),
        out_specs=out_specs,
        scratch_shapes=scratch,
        compiler_params=pltpu.CompilerParams(vmem_limit_bytes=14 * 2**20),
        cost_estimate=pl.CostEstimate(
            flops=4 * work * width, bytes_accessed=4 * 2**20, transcendentals=work
        ),
        name=name,
    )(*scalars, *operands)


def shards(queries, key_heads, value_head_rows, doc_lengths):
    stride, heads, width = queries.shape
    kv_half = key_heads.shape[1]
    block = stride // 2
    group = heads // kv_half
    devices = lax.axis_size("ctx")
    device = lax.axis_index("ctx").astype(jnp.int32)
    core = lax.axis_index("head").astype(jnp.int32)
    stretch = jnp.where(core == 0, device, 2 * devices - 1 - device)
    stretches = 2 * devices

    def owner(place):
        return 2 * place if place < devices else 2 * (stretches - 1 - place) + 1

    def swap(array):
        return lax.ppermute(array, "head", [(0, 1), (1, 0)])

    def from_below(array, distance, turned=()):
        target = {at: at + distance for at in range(stretches - distance)}
        for number, to in enumerate(turned):
            target[devices - 4 + number] = devices + to
        pairs = [(owner(at), owner(to)) for at, to in target.items()]
        return lax.ppermute(array, ("ctx", "head"), pairs)

    smem = pl.BlockSpec(memory_space=pltpu.SMEM)
    vmem = pl.BlockSpec(memory_space=pltpu.VMEM)
    inputs = (key_heads, value_head_rows, queries)
    half = jax.ShapeDtypeStruct((2, kv_half, block, width), jnp.bfloat16)
    keep, given, given_queries = pl.pallas_call(
        pack_kernel,
        out_shape=[half, half, jax.ShapeDtypeStruct((block, heads, width), jnp.bfloat16)],
        in_specs=[pl.BlockSpec(memory_space=pltpu.HBM)] * 3,
        out_specs=[vmem] * 3,
        scratch_shapes=[
            pltpu.VMEM((2, stride, kv_half, width), jnp.bfloat16),
            pltpu.SemaphoreType.DMA((3,)),
        ],
        compiler_params=pltpu.CompilerParams(vmem_limit_bytes=6 * 2**20),
        name="pack",
    )(*[pltpu.with_memory_space_constraint(array, pltpu.HBM) for array in inputs])
    given = swap(given)
    own = jnp.concatenate(
        [jnp.where(core == 0, keep, given), jnp.where(core == 0, given, keep)], axis=1
    )
    own, given_queries = lax.optimization_barrier((own, given_queries))
    partner_queries = swap(given_queries)
    by_three = from_below(own, 3)
    own, partner_queries = lax.optimization_barrier((own, partner_queries))
    by_four = from_below(own, 4)
    by_one = from_below(own, 1)
    by_two = from_below(own, 2)

    scalars = (doc_lengths, jnp.stack([stretch, core]))

    def bundle(name, candidates, choices):
        return pl.pallas_call(
            functools.partial(bundle_kernel, devices=devices, choices=choices),
            out_shape=jax.ShapeDtypeStruct((2, *own.shape), own.dtype),
            in_specs=[smem] + [vmem] * len(candidates),
            out_specs=vmem,
            compiler_params=pltpu.CompilerParams(vmem_limit_bytes=6 * 2**20),
            name=name,
        )(scalars[1], *candidates)

    early = from_below(
        bundle("early", (own, by_three, by_four), EARLY_CHOICES), 4, EARLY_TARGETS
    )
    late = from_below(
        bundle("late", (own, by_one, by_two, by_three, by_four), LATE_CHOICES), 4, LATE_TARGETS
    )

    shape = (devices, block, 2 * kv_half, group, width)
    near = tuple((at, None, (at, ())) for at in range(5))
    folded, *state = run_stage(
        "near",
        scalars,
        (queries, partner_queries),
        None,
        (own, by_one, by_two, by_three, by_four),
        near,
        shape,
    )
    pieces = [
        tuple((0, index, distances) for index, distances in enumerate(table))
        for table in (EARLY_DISTANCES, LATE_DISTANCES)
    ]
    state = run_stage("middle", scalars, (folded,), state, (early,), pieces[0], shape)
    return run_stage(
        "finish", scalars, (folded,), state, (late,), pieces[1], shape, ends=True
    )


def solution(mesh):
    in_specs = (P("ctx", "head", None), P("ctx", "head", None), P("ctx", "head", None), P())
    out_specs = P(("ctx", "head"), None, None)
    return jax.shard_map(shards, mesh=mesh, in_specs=in_specs, out_specs=out_specs, check_vma=False)
```

```python
import functools
import math

import jax
import jax.numpy as jnp
from jax import lax
from jax.experimental import pallas as pl
from jax.experimental.pallas import tpu as pltpu
from jax.sharding import PartitionSpec as P

REACH_LOG = 3
MASKED_SCORE = -1e30

EARLY_TARGETS = (0, 2, 3, 1)
LATE_TARGETS = (1, 3, 0, 2)
EARLY_CHOICES = ((1, (1, 1, 1, 1)), (2, (2, 0, 0, 2)))
LATE_CHOICES = ((1, (3, 1, 3, 3)), (2, (2, 0, 4, 4)))
EARLY_DISTANCES = ((7, (7, 5, 8, 8)), (8, (8, 6, 5, 5)))
LATE_DISTANCES = ((5, (5, 8, 6, 7)), (6, (6, 7, 7, 6)))


def query_bounds(first_place, lanes, group, doc_lengths):
    place = first_place + lax.broadcasted_iota(jnp.int32, (1, lanes), 1) // group
    begin = jnp.zeros((1, lanes), jnp.int32)
    end = jnp.int32(0)
    for j in range(doc_lengths.shape[0]):
        end = end + doc_lengths[j]
        begin = jnp.where(place >= end, end, begin)
    return place, begin


def block_bias(stretch, distance, block, group, doc_lengths):
    lanes = block * group
    first = stretch * block
    place, begin = query_bounds(first, lanes, group, doc_lengths)
    key_place = first - distance * block + lax.broadcasted_iota(jnp.int32, (block, lanes), 0)
    allowed = (key_place >= begin) & (key_place <= place)
    return jnp.where(allowed, 0.0, MASKED_SCORE)


def score(q, keys, bias):
    factor = math.log2(math.e) / math.sqrt(q.shape[1])
    scores = lax.dot_general(
        keys, q, (((1,), (1,)), ((), ())), preferred_element_type=jnp.float32
    )
    return scores * factor + bias


def mix(values, weights):
    return lax.dot_general(
        values,
        weights.astype(jnp.bfloat16),
        (((0,), (0,)), ((), ())),
        preferred_element_type=jnp.float32,
    )


def pack_kernel(keys, values, queries, keep, given, given_queries, staged, sems):
    core = lax.axis_index("head")
    block = given_queries.shape[0]
    kept_rows, given_rows = pl.ds(core * block, block), pl.ds((1 - core) * block, block)
    copies = [
        pltpu.make_async_copy(keys, staged.at[0], sems.at[0]),
        pltpu.make_async_copy(values, staged.at[1], sems.at[1]),
        pltpu.make_async_copy(queries.at[given_rows], given_queries, sems.at[2]),
    ]
    for copy in copies:
        copy.start()
    for kind in range(2):
        copies[kind].wait()
        for rows, out in ((given_rows, given), (kept_rows, keep)):
            part = staged[kind, rows].astype(jnp.float32)
            out[kind] = jnp.swapaxes(part, 0, 1).astype(out.dtype)
    copies[2].wait()


def chain_position(devices):
    device, core = lax.axis_index("ctx"), lax.axis_index("head")
    return jnp.where(core == 0, device, 2 * devices - 1 - device)


def bundle_kernel(*refs, devices, choices):
    candidates, out = refs[:-1], refs[-1]
    source = chain_position(devices) - (devices - 4)
    for slot, (usual, special) in enumerate(choices):
        for candidate, ref in enumerate(candidates):
            if candidate != usual and candidate not in special:
                continue
            chosen = jnp.bool_(candidate == usual)
            for row, number in enumerate(special):
                chosen = jnp.where(source == row, number == candidate, chosen)

            @pl.when(chosen)
            def _(slot=slot, ref=ref):
                out[slot] = ref[...]


def near_kernel(doc_lengths, queries, partner_queries, *refs, devices, group):
    blocks, (folded, far_bias, peak, sums, mixes, bias) = refs[:-6], refs[-6:]
    stretch, core = chain_position(devices), lax.axis_index("head")
    kv_count, block, width = blocks[0].shape[1:]
    lanes = block * group
    for distance in range(len(blocks)):
        bias[distance * block : (distance + 1) * block, :] = block_bias(
            stretch, distance, block, group, doc_lengths
        )

    def gather(kind, head):
        return jnp.concatenate([ref[kind, head] for ref in blocks], axis=0)

    for half in range(2):
        side = core if half == 0 else 1 - core
        for begin in range(0, kv_count // 2, 2):
            first_head = side * (kv_count // 2) + begin
            slots = [half * (kv_count // 2) + begin + part for part in range(2)]
            heads = slice(begin * group, (begin + 2) * group)
            if half == 0:
                both = queries[pl.ds(core * block, block), heads, :]
            else:
                both = partner_queries[:, heads, :]
            both = both.astype(jnp.float32)
            qs = [
                both[:, part * group : (part + 1) * group, :]
                .reshape(lanes, width)
                .astype(jnp.bfloat16)
                for part in range(2)
            ]
            scores = [
                score(q, gather(0, first_head + part), bias[...]) for part, q in enumerate(qs)
            ]
            largest = [jnp.max(each, axis=0, keepdims=True) for each in scores]
            weights = [jnp.exp2(each - top) for each, top in zip(scores, largest)]
            for part, slot in enumerate(slots):
                folded[slot] = qs[part]
                peak[slot] = largest[part]
                sums[slot] = jnp.sum(weights[part], axis=0, keepdims=True)
                mixes[slot] = mix(gather(1, first_head + part), weights[part])
    turn = stretch - devices
    for number, table in enumerate((EARLY_DISTANCES, LATE_DISTANCES)):
        for row, (distance, special) in enumerate(table):
            for at, other in enumerate(special):
                distance = jnp.where(turn == at, other, distance)
            far_bias[number, row * block : (row + 1) * block, :] = block_bias(
                stretch, distance, block, group, doc_lengths
            )


def far_kernel(folded, far_bias, peak, sums, mixes, blocks, *refs, number):
    ends = number == 1
    if ends:
        out, staged, sems = refs
    else:
        new_peak, new_sums, new_mixes = refs
    core = lax.axis_index("head")
    _, _, kv_count, block, width = blocks.shape
    group = folded.shape[1] // block
    step = kv_count // 2
    copies = []
    for half in range(2):
        side = core if half == 0 else 1 - core
        first_head = side * step
        slots = [half * step + part for part in range(step)]
        scores = [
            score(
                folded[slot],
                blocks[:, 0, first_head + part].reshape(2 * block, width),
                far_bias[number],
            )
            for part, slot in enumerate(slots)
        ]
        largest = [
            jnp.maximum(jnp.max(each, axis=0, keepdims=True), peak[slot])
            for each, slot in zip(scores, slots)
        ]
        weights = [jnp.exp2(each - top) for each, top in zip(scores, largest)]
        shrinks = [jnp.exp2(peak[slot] - top) for slot, top in zip(slots, largest)]
        totals = [
            jnp.sum(each, axis=0, keepdims=True) + sums[slot] * shrink
            for each, slot, shrink in zip(weights, slots, shrinks)
        ]
        mixed = [
            mix(blocks[:, 1, first_head + part].reshape(2 * block, width), each)
            for part, each in enumerate(weights)
        ]
        if not ends:
            for part, slot in enumerate(slots):
                new_peak[slot] = largest[part]
                new_sums[slot] = totals[part]
                new_mixes[slot] = mixed[part] + mixes[slot] * shrinks[part]
            continue
        for part in range(0, step, 2):
            done = []
            for at in range(part, part + 2):
                scale = 1.0 / totals[at]
                result = mixed[at] * scale + mixes[slots[at]] * (shrinks[at] * scale)
                done.append(result.T.reshape(block, group, width))
            pair = slots[part] // 2
            staged[pair] = jnp.concatenate(done, axis=1).astype(staged.dtype)
            first = pl.multiple_of((first_head + part) * group, 2 * group)
            copy = pltpu.make_async_copy(
                staged.at[pair], out.at[:, pl.ds(first, 2 * group)], sems.at[pair]
            )
            copy.start()
            copies.append(copy)
    for copy in copies:
        copy.wait()


def shards(queries, key_heads, value_head_rows, doc_lengths):
    stride, heads, width = queries.shape
    kv_half = key_heads.shape[1]
    block = stride // 2
    kv_count = 2 * kv_half
    group = heads // kv_half
    lanes = block * group
    devices = lax.axis_size("ctx")
    core = lax.axis_index("head")
    stretches = 2 * devices

    def owner(place):
        return 2 * place if place < devices else 2 * (stretches - 1 - place) + 1

    def swap(array):
        return lax.ppermute(array, "head", [(0, 1), (1, 0)])

    def from_below(array, distance, turned=()):
        target = {at: at + distance for at in range(stretches - distance)}
        for number, to in enumerate(turned):
            target[devices - 4 + number] = devices + to
        pairs = [(owner(at), owner(to)) for at, to in target.items()]
        return lax.ppermute(array, ("ctx", "head"), pairs)

    smem = pl.BlockSpec(memory_space=pltpu.SMEM)
    vmem = pl.BlockSpec(memory_space=pltpu.VMEM)
    inputs = (key_heads, value_head_rows, queries)
    half = jax.ShapeDtypeStruct((2, kv_half, block, width), jnp.bfloat16)
    keep, given, given_queries = pl.pallas_call(
        pack_kernel,
        out_shape=[half, half, jax.ShapeDtypeStruct((block, heads, width), jnp.bfloat16)],
        in_specs=[pl.BlockSpec(memory_space=pltpu.HBM)] * 3,
        out_specs=[vmem] * 3,
        scratch_shapes=[
            pltpu.VMEM((2, stride, kv_half, width), jnp.bfloat16),
            pltpu.SemaphoreType.DMA((3,)),
        ],
        compiler_params=pltpu.CompilerParams(vmem_limit_bytes=6 * 2**20),
        name="pack",
    )(*[pltpu.with_memory_space_constraint(array, pltpu.HBM) for array in inputs])
    given = swap(given)
    own = jnp.concatenate(
        [jnp.where(core == 0, keep, given), jnp.where(core == 0, given, keep)], axis=1
    )
    own, given_queries = lax.optimization_barrier((own, given_queries))
    partner_queries = swap(given_queries)
    by_three = from_below(own, 3)
    own, partner_queries = lax.optimization_barrier((own, partner_queries))
    by_four = from_below(own, 4)
    by_one = from_below(own, 1)
    by_two = from_below(own, 2)

    def bundle(name, candidates, choices):
        return pl.pallas_call(
            functools.partial(bundle_kernel, devices=devices, choices=choices),
            out_shape=jax.ShapeDtypeStruct((2, *own.shape), own.dtype),
            in_specs=[vmem] * len(candidates),
            out_specs=vmem,
            compiler_params=pltpu.CompilerParams(vmem_limit_bytes=6 * 2**20),
            name=name,
        )(*candidates)

    early = from_below(
        bundle("early", (own, by_three, by_four), EARLY_CHOICES), 4, EARLY_TARGETS
    )
    late = from_below(
        bundle("late", (own, by_one, by_two, by_three, by_four), LATE_CHOICES), 4, LATE_TARGETS
    )

    params = pltpu.CompilerParams(vmem_limit_bytes=14 * 2**20)
    row = jax.ShapeDtypeStruct((kv_count, 1, lanes), jnp.float32)
    state = [row, row, jax.ShapeDtypeStruct((kv_count, width, lanes), jnp.float32)]

    def cost(count):
        work = kv_count * count * block * lanes
        return pl.CostEstimate(
            flops=4 * work * width, bytes_accessed=4 * 2**20, transcendentals=work
        )

    near = (own, by_one, by_two, by_three, by_four)
    folded, far_bias, *known = pl.pallas_call(
        functools.partial(near_kernel, devices=devices, group=group),
        out_shape=[
            jax.ShapeDtypeStruct((kv_count, lanes, width), jnp.bfloat16),
            jax.ShapeDtypeStruct((2, 2 * block, lanes), jnp.float32),
            *state,
        ],
        in_specs=[smem] + [vmem] * (2 + len(near)),
        out_specs=[vmem] * 5,
        scratch_shapes=[pltpu.VMEM((len(near) * block, lanes), jnp.float32)],
        compiler_params=params,
        cost_estimate=cost(len(near)),
        name="near",
    )(doc_lengths, queries, partner_queries, *near)
    known = pl.pallas_call(
        functools.partial(far_kernel, number=0),
        out_shape=state,
        in_specs=[vmem] * 6,
        out_specs=[vmem] * 3,
        compiler_params=params,
        cost_estimate=cost(2),
        name="middle",
    )(folded, far_bias, *known, early)
    return pl.pallas_call(
        functools.partial(far_kernel, number=1),
        out_shape=jax.ShapeDtypeStruct((block, 2 * heads, width), jnp.bfloat16),
        in_specs=[vmem] * 6,
        out_specs=pl.BlockSpec(memory_space=pl.ANY),
        scratch_shapes=[
            pltpu.VMEM((kv_count // 2, block, 2 * group, width), jnp.bfloat16),
            pltpu.SemaphoreType.DMA((kv_count // 2,)),
        ],
        compiler_params=params,
        cost_estimate=cost(2),
        name="finish",
    )(folded, far_bias, *known, late)


def solution(mesh):
    in_specs = (P("ctx", "head", None), P("ctx", "head", None), P("ctx", "head", None), P())
    out_specs = P(("ctx", "head"), None, None)
    return jax.shard_map(shards, mesh=mesh, in_specs=in_specs, out_specs=out_specs, check_vma=False)
```

```python
import functools
import math

import jax
import jax.numpy as jnp
from jax import lax
from jax.experimental import pallas as pl
from jax.experimental.pallas import tpu as pltpu
from jax.sharding import PartitionSpec as P

REACH_LOG = 3
MASKED_SCORE = -1e30

EARLY_TARGETS = (0, 2, 3, 1)
LATE_TARGETS = (1, 3, 0, 2)
EARLY_CHOICES = ((1, (1, 1, 1, 1)), (2, (2, 0, 0, 2)))
LATE_CHOICES = ((1, (3, 1, 3, 3)), (2, (2, 0, 4, 4)))
EARLY_DISTANCES = ((7, (7, 5, 8, 8)), (8, (8, 6, 5, 5)))
LATE_DISTANCES = ((5, (5, 8, 6, 7)), (6, (6, 7, 7, 6)))


def query_bounds(first_place, lanes, group, doc_lengths):
    place = first_place + lax.broadcasted_iota(jnp.int32, (1, lanes), 1) // group
    begin = jnp.zeros((1, lanes), jnp.int32)
    end = jnp.int32(0)
    for j in range(doc_lengths.shape[0]):
        end = end + doc_lengths[j]
        begin = jnp.where(place >= end, end, begin)
    return place, begin


def block_bias(stretch, distance, block, group, doc_lengths):
    lanes = block * group
    first = stretch * block
    place, begin = query_bounds(first, lanes, group, doc_lengths)
    key_place = first - distance * block + lax.broadcasted_iota(jnp.int32, (block, lanes), 0)
    allowed = (key_place >= begin) & (key_place <= place)
    return jnp.where(allowed, 0.0, MASKED_SCORE)


def score(q, keys, bias):
    factor = math.log2(math.e) / math.sqrt(q.shape[1])
    scores = lax.dot_general(
        keys, q, (((1,), (1,)), ((), ())), preferred_element_type=jnp.float32
    )
    return scores * factor + bias


def mix(values, weights):
    return lax.dot_general(
        values,
        weights.astype(jnp.bfloat16),
        (((0,), (0,)), ((), ())),
        preferred_element_type=jnp.float32,
    )


def pack_kernel(*refs, kept):
    if kept:
        keys, values, queries, out, given_queries, staged, sems = refs
    else:
        keys, values, out, staged, sems = refs
    core = lax.axis_index("head")
    block = out.shape[2]
    given_rows = pl.ds((1 - core) * block, block)
    rows = pl.ds(core * block, block) if kept else given_rows
    copies = [
        pltpu.make_async_copy(keys.at[rows], staged.at[0], sems.at[0]),
        pltpu.make_async_copy(values.at[rows], staged.at[1], sems.at[1]),
    ]
    if kept:
        copies.append(pltpu.make_async_copy(queries.at[given_rows], given_queries, sems.at[2]))
    for copy in copies:
        copy.start()
    for kind in range(2):
        copies[kind].wait()
        out[kind] = jnp.swapaxes(staged[kind].astype(jnp.float32), 0, 1).astype(out.dtype)
    for copy in copies[2:]:
        copy.wait()


def chain_position(devices):
    device, core = lax.axis_index("ctx"), lax.axis_index("head")
    return jnp.where(core == 0, device, 2 * devices - 1 - device)


def bundle_kernel(*refs, devices, choices):
    candidates, out = refs[:-1], refs[-1]
    source = chain_position(devices) - (devices - 4)
    for slot, (usual, special) in enumerate(choices):
        for candidate, ref in enumerate(candidates):
            if candidate != usual and candidate not in special:
                continue
            chosen = jnp.bool_(candidate == usual)
            for row, number in enumerate(special):
                chosen = jnp.where(source == row, number == candidate, chosen)

            @pl.when(chosen)
            def _(slot=slot, ref=ref):
                out[slot] = ref[...]


def near_kernel(doc_lengths, queries, partner_queries, *refs, devices, group):
    blocks, (folded, far_bias, peak, sums, mixes, bias) = refs[:-6], refs[-6:]
    stretch, core = chain_position(devices), lax.axis_index("head")
    kv_count, block, width = blocks[0].shape[1:]
    lanes = block * group
    for distance in range(len(blocks)):
        bias[distance * block : (distance + 1) * block, :] = block_bias(
            stretch, distance, block, group, doc_lengths
        )

    def gather(kind, head):
        return jnp.concatenate([ref[kind, head] for ref in blocks], axis=0)

    for half in range(2):
        side = core if half == 0 else 1 - core
        for begin in range(0, kv_count // 2, 2):
            first_head = side * (kv_count // 2) + begin
            slots = [half * (kv_count // 2) + begin + part for part in range(2)]
            heads = slice(begin * group, (begin + 2) * group)
            if half == 0:
                both = queries[pl.ds(core * block, block), heads, :]
            else:
                both = partner_queries[:, heads, :]
            both = both.astype(jnp.float32)
            qs = [
                both[:, part * group : (part + 1) * group, :]
                .reshape(lanes, width)
                .astype(jnp.bfloat16)
                for part in range(2)
            ]
            scores = [
                score(q, gather(0, first_head + part), bias[...]) for part, q in enumerate(qs)
            ]
            largest = [jnp.max(each, axis=0, keepdims=True) for each in scores]
            weights = [jnp.exp2(each - top) for each, top in zip(scores, largest)]
            for part, slot in enumerate(slots):
                folded[slot] = qs[part]
                peak[slot] = largest[part]
                sums[slot] = jnp.sum(weights[part], axis=0, keepdims=True)
                mixes[slot] = mix(gather(1, first_head + part), weights[part])
    turn = stretch - devices
    for number, table in enumerate((EARLY_DISTANCES, LATE_DISTANCES)):
        for row, (distance, special) in enumerate(table):
            for at, other in enumerate(special):
                distance = jnp.where(turn == at, other, distance)
            far_bias[number, row * block : (row + 1) * block, :] = block_bias(
                stretch, distance, block, group, doc_lengths
            )


def far_kernel(folded, far_bias, peak, sums, mixes, blocks, *refs, number):
    ends = number == 1
    if ends:
        out, staged, sems = refs
    else:
        new_peak, new_sums, new_mixes = refs
    core = lax.axis_index("head")
    _, _, kv_count, block, width = blocks.shape
    group = folded.shape[1] // block
    step = kv_count // 2
    copies = []
    for half in range(2):
        side = core if half == 0 else 1 - core
        first_head = side * step
        slots = [half * step + part for part in range(step)]
        scores = [
            score(
                folded[slot],
                blocks[:, 0, first_head + part].reshape(2 * block, width),
                far_bias[number],
            )
            for part, slot in enumerate(slots)
        ]
        largest = [
            jnp.maximum(jnp.max(each, axis=0, keepdims=True), peak[slot])
            for each, slot in zip(scores, slots)
        ]
        weights = [jnp.exp2(each - top) for each, top in zip(scores, largest)]
        shrinks = [jnp.exp2(peak[slot] - top) for slot, top in zip(slots, largest)]
        totals = [
            jnp.sum(each, axis=0, keepdims=True) + sums[slot] * shrink
            for each, slot, shrink in zip(weights, slots, shrinks)
        ]
        mixed = [
            mix(blocks[:, 1, first_head + part].reshape(2 * block, width), each)
            for part, each in enumerate(weights)
        ]
        if not ends:
            for part, slot in enumerate(slots):
                new_peak[slot] = largest[part]
                new_sums[slot] = totals[part]
                new_mixes[slot] = mixed[part] + mixes[slot] * shrinks[part]
            continue
        for part in range(0, step, 2):
            done = []
            for at in range(part, part + 2):
                scale = 1.0 / totals[at]
                result = mixed[at] * scale + mixes[slots[at]] * (shrinks[at] * scale)
                done.append(result.T.reshape(block, group, width))
            pair = slots[part] // 2
            done = jnp.concatenate(done, axis=1).astype(staged.dtype)
            first = pl.multiple_of((first_head + part) * group, 2 * group)
            for piece in range(2):
                rows = slice(piece * block // 2, (piece + 1) * block // 2)
                staged[pair, rows] = done[rows]
                copy = pltpu.make_async_copy(
                    staged.at[pair, rows],
                    out.at[rows, pl.ds(first, 2 * group)],
                    sems.at[pair, piece],
                )
                copy.start()
                copies.append(copy)
    for copy in copies:
        copy.wait()


def shards(queries, key_heads, value_head_rows, doc_lengths):
    stride, heads, width = queries.shape
    kv_half = key_heads.shape[1]
    block = stride // 2
    kv_count = 2 * kv_half
    group = heads // kv_half
    lanes = block * group
    devices = lax.axis_size("ctx")
    core = lax.axis_index("head")
    stretches = 2 * devices

    def owner(place):
        return 2 * place if place < devices else 2 * (stretches - 1 - place) + 1

    def swap(array):
        return lax.ppermute(array, "head", [(0, 1), (1, 0)])

    def from_below(array, distance, turned=()):
        target = {at: at + distance for at in range(stretches - distance)}
        for number, to in enumerate(turned):
            target[devices - 4 + number] = devices + to
        pairs = [(owner(at), owner(to)) for at, to in target.items()]
        return lax.ppermute(array, ("ctx", "head"), pairs)

    smem = pl.BlockSpec(memory_space=pltpu.SMEM)
    vmem = pl.BlockSpec(memory_space=pltpu.VMEM)
    def pack(kept):
        arrays = (key_heads, value_head_rows, queries) if kept else (key_heads, value_head_rows)
        out_shape = [jax.ShapeDtypeStruct((2, kv_half, block, width), jnp.bfloat16)]
        if kept:
            out_shape.append(jax.ShapeDtypeStruct((block, heads, width), jnp.bfloat16))
        return pl.pallas_call(
            functools.partial(pack_kernel, kept=kept),
            out_shape=out_shape,
            in_specs=[pl.BlockSpec(memory_space=pltpu.HBM)] * len(arrays),
            out_specs=[vmem] * len(out_shape),
            scratch_shapes=[
                pltpu.VMEM((2, block, kv_half, width), jnp.bfloat16),
                pltpu.SemaphoreType.DMA((len(arrays),)),
            ],
            compiler_params=pltpu.CompilerParams(vmem_limit_bytes=6 * 2**20),
            cost_estimate=pl.CostEstimate(
                flops=0, bytes_accessed=len(arrays) * 2**20, transcendentals=0
            ),
            name="keep" if kept else "give",
        )(*[pltpu.with_memory_space_constraint(array, pltpu.HBM) for array in arrays])

    (given,) = pack(False)
    given = swap(given)
    keep, given_queries = pack(True)
    own = jnp.concatenate(
        [jnp.where(core == 0, keep, given), jnp.where(core == 0, given, keep)], axis=1
    )
    own, given_queries = lax.optimization_barrier((own, given_queries))
    partner_queries = swap(given_queries)
    by_three = from_below(own, 3)
    own, partner_queries = lax.optimization_barrier((own, partner_queries))
    by_four = from_below(own, 4)
    by_one = from_below(own, 1)
    by_two = from_below(own, 2)

    def bundle(name, candidates, choices):
        return pl.pallas_call(
            functools.partial(bundle_kernel, devices=devices, choices=choices),
            out_shape=jax.ShapeDtypeStruct((2, *own.shape), own.dtype),
            in_specs=[vmem] * len(candidates),
            out_specs=vmem,
            compiler_params=pltpu.CompilerParams(vmem_limit_bytes=6 * 2**20),
            name=name,
        )(*candidates)

    early = from_below(
        bundle("early", (own, by_three, by_four), EARLY_CHOICES), 4, EARLY_TARGETS
    )
    late = from_below(
        bundle("late", (own, by_one, by_two, by_three, by_four), LATE_CHOICES), 4, LATE_TARGETS
    )

    params = pltpu.CompilerParams(vmem_limit_bytes=14 * 2**20)
    row = jax.ShapeDtypeStruct((kv_count, 1, lanes), jnp.float32)
    state = [row, row, jax.ShapeDtypeStruct((kv_count, width, lanes), jnp.float32)]

    def cost(count):
        work = kv_count * count * block * lanes
        return pl.CostEstimate(
            flops=4 * work * width, bytes_accessed=4 * 2**20, transcendentals=work
        )

    near = (own, by_one, by_two, by_three, by_four)
    folded, far_bias, *known = pl.pallas_call(
        functools.partial(near_kernel, devices=devices, group=group),
        out_shape=[
            jax.ShapeDtypeStruct((kv_count, lanes, width), jnp.bfloat16),
            jax.ShapeDtypeStruct((2, 2 * block, lanes), jnp.float32),
            *state,
        ],
        in_specs=[smem] + [vmem] * (2 + len(near)),
        out_specs=[vmem] * 5,
        scratch_shapes=[pltpu.VMEM((len(near) * block, lanes), jnp.float32)],
        compiler_params=params,
        cost_estimate=cost(len(near)),
        name="near",
    )(doc_lengths, queries, partner_queries, *near)
    known = pl.pallas_call(
        functools.partial(far_kernel, number=0),
        out_shape=state,
        in_specs=[vmem] * 6,
        out_specs=[vmem] * 3,
        compiler_params=params,
        cost_estimate=cost(2),
        name="middle",
    )(folded, far_bias, *known, early)
    return pl.pallas_call(
        functools.partial(far_kernel, number=1),
        out_shape=jax.ShapeDtypeStruct((block, 2 * heads, width), jnp.bfloat16),
        in_specs=[vmem] * 6,
        out_specs=pl.BlockSpec(memory_space=pl.ANY),
        scratch_shapes=[
            pltpu.VMEM((kv_count // 2, block, 2 * group, width), jnp.bfloat16),
            pltpu.SemaphoreType.DMA((kv_count // 2, 2)),
        ],
        compiler_params=params,
        cost_estimate=cost(2),
        name="finish",
    )(folded, far_bias, *known, late)


def solution(mesh):
    in_specs = (P("ctx", "head", None), P("ctx", "head", None), P("ctx", "head", None), P())
    out_specs = P(("ctx", "head"), None, None)
    return jax.shard_map(shards, mesh=mesh, in_specs=in_specs, out_specs=out_specs, check_vma=False)
```

```python
import functools
import math

import jax
import jax.numpy as jnp
from jax import lax
from jax.experimental import pallas as pl
from jax.experimental.pallas import tpu as pltpu
from jax.sharding import PartitionSpec as P

REACH_LOG = 3
MASKED_SCORE = -1e30

STEPS = ((3, 1), (4, 4), (1, 3), (2, 2))
EARLY_TARGETS = (0, 1, 3, 2)
LATE_TARGETS = (0, 2, 1, 3)
EARLY_CHOICES = ((1, (1, 1, 1, 1)), (2, (2, 2, 0, 2)))
LATE_CHOICES = ((3, (3, 1, 3, 1)), (4, (4, 0, 4, 2)))
EARLY_DISTANCES = ((5, 7, (5, 7, 6, 6)), (8, 8, (8, 8, 7, 5)))
LATE_DISTANCES = ((7, 5, (7, 6, 8, 7)), (6, 6, (6, 5, 5, 8)))


def query_bounds(first_place, lanes, group, doc_lengths):
    place = first_place + lax.broadcasted_iota(jnp.int32, (1, lanes), 1) // group
    begin = jnp.zeros((1, lanes), jnp.int32)
    end = jnp.int32(0)
    for j in range(doc_lengths.shape[0]):
        end = end + doc_lengths[j]
        begin = jnp.where(place >= end, end, begin)
    return place, begin


def block_bias(stretch, distance, block, group, doc_lengths):
    lanes = block * group
    first = stretch * block
    place, begin = query_bounds(first, lanes, group, doc_lengths)
    key_place = first - distance * block + lax.broadcasted_iota(jnp.int32, (block, lanes), 0)
    allowed = (key_place >= begin) & (key_place <= place)
    return jnp.where(allowed, 0.0, MASKED_SCORE)


def score(q, keys, bias):
    factor = math.log2(math.e) / math.sqrt(q.shape[1])
    scores = lax.dot_general(
        keys, q, (((1,), (1,)), ((), ())), preferred_element_type=jnp.float32
    )
    return scores * factor + bias


def mix(values, weights):
    return lax.dot_general(
        values,
        weights.astype(jnp.bfloat16),
        (((0,), (0,)), ((), ())),
        preferred_element_type=jnp.float32,
    )


def pack_kernel(*refs, kept):
    if kept:
        keys, values, queries, out, given_queries, staged, sems = refs
    else:
        keys, values, out, staged, sems = refs
    core = lax.axis_index("head")
    block = out.shape[2]
    given_rows = pl.ds((1 - core) * block, block)
    rows = pl.ds(core * block, block) if kept else given_rows
    copies = [
        pltpu.make_async_copy(keys.at[rows], staged.at[0], sems.at[0]),
        pltpu.make_async_copy(values.at[rows], staged.at[1], sems.at[1]),
    ]
    if kept:
        copies.append(pltpu.make_async_copy(queries.at[given_rows], given_queries, sems.at[2]))
    for copy in copies:
        copy.start()
    for kind in range(2):
        copies[kind].wait()
        out[kind] = jnp.swapaxes(staged[kind].astype(jnp.float32), 0, 1).astype(out.dtype)
    for copy in copies[2:]:
        copy.wait()


def chain_position(devices):
    device, core = lax.axis_index("ctx"), lax.axis_index("head")
    return jnp.where(core == 0, device, 2 * devices - 1 - device)


def bundle_kernel(*refs, devices, choices):
    held, out = refs[:-1], refs[-1]
    source = chain_position(devices) - (devices - 4)
    for slot, (usual, special) in enumerate(choices):
        for number, ref in enumerate(held):
            if number != usual and number not in special:
                continue
            chosen = jnp.bool_(number == usual)
            for row, other in enumerate(special):
                chosen = jnp.where(source == row, number == other, chosen)

            @pl.when(chosen)
            def _(slot=slot, ref=ref):
                out[slot] = ref[...]


def near_kernel(doc_lengths, queries, partner_queries, *refs, devices, group):
    blocks, (folded, far_bias, peak, sums, mixes, bias) = refs[:-6], refs[-6:]
    stretch, core = chain_position(devices), lax.axis_index("head")
    kv_count, block, width = blocks[0].shape[1:]
    lanes = block * group
    odd = stretch % 2 == 1
    for row in range(len(blocks)):
        distance = 0
        if row > 0:
            by_even, by_odd = STEPS[row - 1]
            if by_even % 2 == 1:
                by_even, by_odd = by_odd, by_even
            distance = jnp.where(odd, by_odd, by_even)
        bias[row * block : (row + 1) * block, :] = block_bias(
            stretch, distance, block, group, doc_lengths
        )

    def gather(kind, head):
        return jnp.concatenate([ref[kind, head] for ref in blocks], axis=0)

    for half in range(2):
        side = core if half == 0 else 1 - core
        for begin in range(0, kv_count // 2, 2):
            first_head = side * (kv_count // 2) + begin
            slots = [half * (kv_count // 2) + begin + part for part in range(2)]
            heads = slice(begin * group, (begin + 2) * group)
            if half == 0:
                both = queries[pl.ds(core * block, block), heads, :]
            else:
                both = partner_queries[:, heads, :]
            both = both.astype(jnp.float32)
            qs = [
                both[:, part * group : (part + 1) * group, :]
                .reshape(lanes, width)
                .astype(jnp.bfloat16)
                for part in range(2)
            ]
            scores = [
                score(q, gather(0, first_head + part), bias[...]) for part, q in enumerate(qs)
            ]
            largest = [jnp.max(each, axis=0, keepdims=True) for each in scores]
            weights = [jnp.exp2(each - top) for each, top in zip(scores, largest)]
            for part, slot in enumerate(slots):
                folded[slot] = qs[part]
                peak[slot] = largest[part]
                sums[slot] = jnp.sum(weights[part], axis=0, keepdims=True)
                mixes[slot] = mix(gather(1, first_head + part), weights[part])
    turn = stretch - devices
    for number, table in enumerate((EARLY_DISTANCES, LATE_DISTANCES)):
        for row, (even_distance, odd_distance, special) in enumerate(table):
            distance = jnp.where(odd, odd_distance, even_distance)
            for at, other in enumerate(special):
                distance = jnp.where(turn == at, other, distance)
            far_bias[number, row * block : (row + 1) * block, :] = block_bias(
                stretch, distance, block, group, doc_lengths
            )


def far_kernel(folded, far_bias, peak, sums, mixes, blocks, *refs, number):
    ends = number == 1
    if ends:
        out, staged, sems = refs
    else:
        new_peak, new_sums, new_mixes = refs
    core = lax.axis_index("head")
    _, _, kv_count, block, width = blocks.shape
    group = folded.shape[1] // block
    step = kv_count // 2
    copies = []
    for half in range(2):
        side = core if half == 0 else 1 - core
        first_head = side * step
        slots = [half * step + part for part in range(step)]
        scores = [
            score(
                folded[slot],
                blocks[:, 0, first_head + part].reshape(2 * block, width),
                far_bias[number],
            )
            for part, slot in enumerate(slots)
        ]
        largest = [
            jnp.maximum(jnp.max(each, axis=0, keepdims=True), peak[slot])
            for each, slot in zip(scores, slots)
        ]
        weights = [jnp.exp2(each - top) for each, top in zip(scores, largest)]
        shrinks = [jnp.exp2(peak[slot] - top) for slot, top in zip(slots, largest)]
        totals = [
            jnp.sum(each, axis=0, keepdims=True) + sums[slot] * shrink
            for each, slot, shrink in zip(weights, slots, shrinks)
        ]
        mixed = [
            mix(blocks[:, 1, first_head + part].reshape(2 * block, width), each)
            for part, each in enumerate(weights)
        ]
        if not ends:
            for part, slot in enumerate(slots):
                new_peak[slot] = largest[part]
                new_sums[slot] = totals[part]
                new_mixes[slot] = mixed[part] + mixes[slot] * shrinks[part]
            continue
        for part in range(0, step, 2):
            done = []
            for at in range(part, part + 2):
                scale = 1.0 / totals[at]
                result = mixed[at] * scale + mixes[slots[at]] * (shrinks[at] * scale)
                done.append(result.T.reshape(block, group, width))
            pair = slots[part] // 2
            done = jnp.concatenate(done, axis=1).astype(staged.dtype)
            first = pl.multiple_of((first_head + part) * group, 2 * group)
            for piece in range(2):
                rows = slice(piece * block // 2, (piece + 1) * block // 2)
                staged[pair, rows] = done[rows]
                copy = pltpu.make_async_copy(
                    staged.at[pair, rows],
                    out.at[rows, pl.ds(first, 2 * group)],
                    sems.at[pair, piece],
                )
                copy.start()
                copies.append(copy)
    for copy in copies:
        copy.wait()


def shards(queries, key_heads, value_head_rows, doc_lengths):
    stride, heads, width = queries.shape
    kv_half = key_heads.shape[1]
    block = stride // 2
    kv_count = 2 * kv_half
    group = heads // kv_half
    lanes = block * group
    devices = lax.axis_size("ctx")
    core = lax.axis_index("head")
    stretches = 2 * devices

    def owner(place):
        return 2 * place if place < devices else 2 * (stretches - 1 - place) + 1

    def swap(array):
        return lax.ppermute(array, "head", [(0, 1), (1, 0)])

    def upwards(array, steps, turned=()):
        target = {at: at + steps[at % 2] for at in range(stretches)}
        for number, to in enumerate(turned):
            target[devices - 4 + number] = devices + to
        pairs = [(owner(at), owner(to)) for at, to in target.items() if to < stretches]
        return lax.ppermute(array, ("ctx", "head"), pairs)

    smem = pl.BlockSpec(memory_space=pltpu.SMEM)
    vmem = pl.BlockSpec(memory_space=pltpu.VMEM)
    def pack(kept):
        arrays = (key_heads, value_head_rows, queries) if kept else (key_heads, value_head_rows)
        out_shape = [jax.ShapeDtypeStruct((2, kv_half, block, width), jnp.bfloat16)]
        if kept:
            out_shape.append(jax.ShapeDtypeStruct((block, heads, width), jnp.bfloat16))
        return pl.pallas_call(
            functools.partial(pack_kernel, kept=kept),
            out_shape=out_shape,
            in_specs=[pl.BlockSpec(memory_space=pltpu.HBM)] * len(arrays),
            out_specs=[vmem] * len(out_shape),
            scratch_shapes=[
                pltpu.VMEM((2, block, kv_half, width), jnp.bfloat16),
                pltpu.SemaphoreType.DMA((len(arrays),)),
            ],
            compiler_params=pltpu.CompilerParams(vmem_limit_bytes=6 * 2**20),
            cost_estimate=pl.CostEstimate(
                flops=0, bytes_accessed=len(arrays) * 2**20, transcendentals=0
            ),
            name="keep" if kept else "give",
        )(*[pltpu.with_memory_space_constraint(array, pltpu.HBM) for array in arrays])

    (given,) = pack(False)
    given = swap(given)
    keep, given_queries = pack(True)
    own = jnp.concatenate(
        [jnp.where(core == 0, keep, given), jnp.where(core == 0, given, keep)], axis=1
    )
    own, given_queries = lax.optimization_barrier((own, given_queries))
    partner_queries = swap(given_queries)
    first = upwards(own, STEPS[0])
    own, partner_queries = lax.optimization_barrier((own, partner_queries))
    second, third, fourth = [upwards(own, steps) for steps in STEPS[1:]]

    def bundle(name, held, choices):
        return pl.pallas_call(
            functools.partial(bundle_kernel, devices=devices, choices=choices),
            out_shape=jax.ShapeDtypeStruct((2, *own.shape), own.dtype),
            in_specs=[vmem] * len(held),
            out_specs=vmem,
            compiler_params=pltpu.CompilerParams(vmem_limit_bytes=6 * 2**20),
            name=name,
        )(*held)

    early = upwards(bundle("early", (own, first, second), EARLY_CHOICES), (4, 4), EARLY_TARGETS)
    late = upwards(
        bundle("late", (own, first, second, third, fourth), LATE_CHOICES), (4, 4), LATE_TARGETS
    )

    params = pltpu.CompilerParams(vmem_limit_bytes=14 * 2**20)
    row = jax.ShapeDtypeStruct((kv_count, 1, lanes), jnp.float32)
    state = [row, row, jax.ShapeDtypeStruct((kv_count, width, lanes), jnp.float32)]

    def cost(count):
        work = kv_count * count * block * lanes
        return pl.CostEstimate(
            flops=4 * work * width, bytes_accessed=4 * 2**20, transcendentals=work
        )

    near = (own, first, second, third, fourth)
    folded, far_bias, *known = pl.pallas_call(
        functools.partial(near_kernel, devices=devices, group=group),
        out_shape=[
            jax.ShapeDtypeStruct((kv_count, lanes, width), jnp.bfloat16),
            jax.ShapeDtypeStruct((2, 2 * block, lanes), jnp.float32),
            *state,
        ],
        in_specs=[smem] + [vmem] * (2 + len(near)),
        out_specs=[vmem] * 5,
        scratch_shapes=[pltpu.VMEM((len(near) * block, lanes), jnp.float32)],
        compiler_params=params,
        cost_estimate=cost(len(near)),
        name="near",
    )(doc_lengths, queries, partner_queries, *near)
    known = pl.pallas_call(
        functools.partial(far_kernel, number=0),
        out_shape=state,
        in_specs=[vmem] * 6,
        out_specs=[vmem] * 3,
        compiler_params=params,
        cost_estimate=cost(2),
        name="middle",
    )(folded, far_bias, *known, early)
    return pl.pallas_call(
        functools.partial(far_kernel, number=1),
        out_shape=jax.ShapeDtypeStruct((block, 2 * heads, width), jnp.bfloat16),
        in_specs=[vmem] * 6,
        out_specs=pl.BlockSpec(memory_space=pl.ANY),
        scratch_shapes=[
            pltpu.VMEM((kv_count // 2, block, 2 * group, width), jnp.bfloat16),
            pltpu.SemaphoreType.DMA((kv_count // 2, 2)),
        ],
        compiler_params=params,
        cost_estimate=cost(2),
        name="finish",
    )(folded, far_bias, *known, late)


def solution(mesh):
    in_specs = (P("ctx", "head", None), P("ctx", "head", None), P("ctx", "head", None), P())
    out_specs = P(("ctx", "head"), None, None)
    return jax.shard_map(shards, mesh=mesh, in_specs=in_specs, out_specs=out_specs, check_vma=False)
```

```python
import functools
import math

import jax
import jax.numpy as jnp
from jax import lax
from jax.experimental import pallas as pl
from jax.experimental.pallas import tpu as pltpu
from jax.sharding import PartitionSpec as P

REACH_LOG = 3
MASKED_SCORE = -1e30

STEPS = ((3, 1), (4, 4), (1, 3), (2, 2))
EARLY_TARGETS = (0, 1, 3, 2)
LATE_TARGETS = (0, 2, 1, 3)
EARLY_CHOICES = ((1, (1, 1, 1, 1)), (2, (2, 2, 0, 2)))
LATE_CHOICES = ((3, (3, 1, 3, 1)), (4, (4, 0, 4, 2)))
EARLY_DISTANCES = ((5, 7, (5, 7, 6, 6)), (8, 8, (8, 8, 7, 5)))
LATE_DISTANCES = ((7, 5, (7, 6, 8, 7)), (6, 6, (6, 5, 5, 8)))


def query_bounds(first_place, lanes, group, doc_lengths):
    place = first_place + lax.broadcasted_iota(jnp.int32, (1, lanes), 1) // group
    begin = jnp.zeros((1, lanes), jnp.int32)
    end = jnp.int32(0)
    for j in range(doc_lengths.shape[0]):
        end = end + doc_lengths[j]
        begin = jnp.where(place >= end, end, begin)
    return place, begin


def block_bias(stretch, distance, block, group, doc_lengths):
    lanes = block * group
    first = stretch * block
    place, begin = query_bounds(first, lanes, group, doc_lengths)
    key_place = first - distance * block + lax.broadcasted_iota(jnp.int32, (block, lanes), 0)
    allowed = (key_place >= begin) & (key_place <= place)
    return jnp.where(allowed, 0.0, MASKED_SCORE)


def score(q, keys, bias):
    factor = math.log2(math.e) / math.sqrt(q.shape[0])
    return jnp.dot(keys, q, preferred_element_type=jnp.float32) * factor + bias


def mix(values, weights):
    return lax.dot_general(
        values,
        weights.astype(jnp.bfloat16),
        (((0,), (0,)), ((), ())),
        preferred_element_type=jnp.float32,
    )


def pack_kernel(*refs, kept):
    if kept:
        keys, values, queries, out, given_queries, staged, sems = refs
    else:
        keys, values, out, staged, sems = refs
    core = lax.axis_index("head")
    block = out.shape[2]
    given_rows = pl.ds((1 - core) * block, block)
    rows = pl.ds(core * block, block) if kept else given_rows
    copies = [
        pltpu.make_async_copy(keys.at[rows], staged.at[0], sems.at[0]),
        pltpu.make_async_copy(values.at[rows], staged.at[1], sems.at[1]),
    ]
    if kept:
        copies.append(pltpu.make_async_copy(queries.at[given_rows], given_queries, sems.at[2]))
    for copy in copies:
        copy.start()
    for kind in range(2):
        copies[kind].wait()
        out[kind] = jnp.swapaxes(staged[kind].astype(jnp.float32), 0, 1).astype(out.dtype)
    for copy in copies[2:]:
        copy.wait()


def chain_position(devices):
    device, core = lax.axis_index("ctx"), lax.axis_index("head")
    return jnp.where(core == 0, device, 2 * devices - 1 - device)


def bundle_kernel(*refs, devices, choices):
    held, out = refs[:-1], refs[-1]
    source = chain_position(devices) - (devices - 4)
    for slot, (usual, special) in enumerate(choices):
        for number, ref in enumerate(held):
            if number != usual and number not in special:
                continue
            chosen = jnp.bool_(number == usual)
            for row, other in enumerate(special):
                chosen = jnp.where(source == row, number == other, chosen)

            @pl.when(chosen)
            def _(slot=slot, ref=ref):
                out[slot] = ref[...]


def near_kernel(doc_lengths, queries, partner_queries, *refs, devices, group):
    blocks, (folded, far_bias, peak, sums, mixes, bias) = refs[:-6], refs[-6:]
    stretch, core = chain_position(devices), lax.axis_index("head")
    kv_count, block, width = blocks[0].shape[1:]
    lanes = block * group
    odd = stretch % 2 == 1
    for row in range(len(blocks)):
        distance = 0
        if row > 0:
            by_even, by_odd = STEPS[row - 1]
            if by_even % 2 == 1:
                by_even, by_odd = by_odd, by_even
            distance = jnp.where(odd, by_odd, by_even)
        bias[row * block : (row + 1) * block, :] = block_bias(
            stretch, distance, block, group, doc_lengths
        )

    def gather(kind, head):
        return jnp.concatenate([ref[kind, head] for ref in blocks], axis=0)

    for half in range(2):
        side = core if half == 0 else 1 - core
        for begin in range(0, kv_count // 2, 2):
            first_head = side * (kv_count // 2) + begin
            slots = [half * (kv_count // 2) + begin + part for part in range(2)]
            heads = slice(begin * group, (begin + 2) * group)
            if half == 0:
                both = queries[pl.ds(core * block, block), heads, :]
            else:
                both = partner_queries[:, heads, :]
            both = both.astype(jnp.float32)
            qs = [
                both[:, part * group : (part + 1) * group, :]
                .reshape(lanes, width)
                .T.astype(jnp.bfloat16)
                for part in range(2)
            ]
            scores = [
                score(q, gather(0, first_head + part), bias[...]) for part, q in enumerate(qs)
            ]
            largest = [jnp.max(each, axis=0, keepdims=True) for each in scores]
            weights = [jnp.exp2(each - top) for each, top in zip(scores, largest)]
            for part, slot in enumerate(slots):
                folded[slot] = qs[part]
                peak[slot] = largest[part]
                sums[slot] = jnp.sum(weights[part], axis=0, keepdims=True)
                mixes[slot] = mix(gather(1, first_head + part), weights[part])
    turn = stretch - devices
    for number, table in enumerate((EARLY_DISTANCES, LATE_DISTANCES)):
        for row, (even_distance, odd_distance, special) in enumerate(table):
            distance = jnp.where(odd, odd_distance, even_distance)
            for at, other in enumerate(special):
                distance = jnp.where(turn == at, other, distance)
            far_bias[number, row * block : (row + 1) * block, :] = block_bias(
                stretch, distance, block, group, doc_lengths
            )


def far_kernel(folded, far_bias, peak, sums, mixes, blocks, *refs, number):
    ends = number == 1
    if ends:
        out, staged, sems = refs
    else:
        new_peak, new_sums, new_mixes = refs
    core = lax.axis_index("head")
    _, _, kv_count, block, width = blocks.shape
    group = folded.shape[2] // block
    step = kv_count // 2
    copies = []
    for half in range(2):
        side = core if half == 0 else 1 - core
        first_head = side * step
        slots = [half * step + part for part in range(step)]
        scores = [
            score(
                folded[slot],
                blocks[:, 0, first_head + part].reshape(2 * block, width),
                far_bias[number],
            )
            for part, slot in enumerate(slots)
        ]
        largest = [
            jnp.maximum(jnp.max(each, axis=0, keepdims=True), peak[slot])
            for each, slot in zip(scores, slots)
        ]
        weights = [jnp.exp2(each - top) for each, top in zip(scores, largest)]
        shrinks = [jnp.exp2(peak[slot] - top) for slot, top in zip(slots, largest)]
        totals = [
            jnp.sum(each, axis=0, keepdims=True) + sums[slot] * shrink
            for each, slot, shrink in zip(weights, slots, shrinks)
        ]
        mixed = [
            mix(blocks[:, 1, first_head + part].reshape(2 * block, width), each)
            for part, each in enumerate(weights)
        ]
        if not ends:
            for part, slot in enumerate(slots):
                new_peak[slot] = largest[part]
                new_sums[slot] = totals[part]
                new_mixes[slot] = mixed[part] + mixes[slot] * shrinks[part]
            continue
        for part in range(0, step, 2):
            done = []
            for at in range(part, part + 2):
                scale = 1.0 / totals[at]
                result = mixed[at] * scale + mixes[slots[at]] * (shrinks[at] * scale)
                done.append(result.T.reshape(block, group, width))
            pair = slots[part] // 2
            done = jnp.concatenate(done, axis=1).astype(staged.dtype)
            first = pl.multiple_of((first_head + part) * group, 2 * group)
            for piece in range(2):
                rows = slice(piece * block // 2, (piece + 1) * block // 2)
                staged[pair, rows] = done[rows]
                copy = pltpu.make_async_copy(
                    staged.at[pair, rows],
                    out.at[rows, pl.ds(first, 2 * group)],
                    sems.at[pair, piece],
                )
                copy.start()
                copies.append(copy)
    for copy in copies:
        copy.wait()


def shards(queries, key_heads, value_head_rows, doc_lengths):
    stride, heads, width = queries.shape
    kv_half = key_heads.shape[1]
    block = stride // 2
    kv_count = 2 * kv_half
    group = heads // kv_half
    lanes = block * group
    devices = lax.axis_size("ctx")
    core = lax.axis_index("head")
    stretches = 2 * devices

    def owner(place):
        return 2 * place if place < devices else 2 * (stretches - 1 - place) + 1

    def swap(array):
        return lax.ppermute(array, "head", [(0, 1), (1, 0)])

    def upwards(array, steps, turned=()):
        target = {at: at + steps[at % 2] for at in range(stretches)}
        for number, to in enumerate(turned):
            target[devices - 4 + number] = devices + to
        pairs = [(owner(at), owner(to)) for at, to in target.items() if to < stretches]
        return lax.ppermute(array, ("ctx", "head"), pairs)

    smem = pl.BlockSpec(memory_space=pltpu.SMEM)
    vmem = pl.BlockSpec(memory_space=pltpu.VMEM)
    def pack(kept):
        arrays = (key_heads, value_head_rows, queries) if kept else (key_heads, value_head_rows)
        out_shape = [jax.ShapeDtypeStruct((2, kv_half, block, width), jnp.bfloat16)]
        if kept:
            out_shape.append(jax.ShapeDtypeStruct((block, heads, width), jnp.bfloat16))
        return pl.pallas_call(
            functools.partial(pack_kernel, kept=kept),
            out_shape=out_shape,
            in_specs=[pl.BlockSpec(memory_space=pltpu.HBM)] * len(arrays),
            out_specs=[vmem] * len(out_shape),
            scratch_shapes=[
                pltpu.VMEM((2, block, kv_half, width), jnp.bfloat16),
                pltpu.SemaphoreType.DMA((len(arrays),)),
            ],
            compiler_params=pltpu.CompilerParams(vmem_limit_bytes=6 * 2**20),
            cost_estimate=pl.CostEstimate(
                flops=0, bytes_accessed=len(arrays) * 2**20, transcendentals=0
            ),
            name="keep" if kept else "give",
        )(*[pltpu.with_memory_space_constraint(array, pltpu.HBM) for array in arrays])

    (given,) = pack(False)
    given = swap(given)
    keep, given_queries = pack(True)
    own = jnp.concatenate(
        [jnp.where(core == 0, keep, given), jnp.where(core == 0, given, keep)], axis=1
    )
    own, given_queries = lax.optimization_barrier((own, given_queries))
    partner_queries = swap(given_queries)
    first = upwards(own, STEPS[0])
    own, partner_queries = lax.optimization_barrier((own, partner_queries))
    second, third, fourth = [upwards(own, steps) for steps in STEPS[1:]]

    def bundle(name, held, choices):
        return pl.pallas_call(
            functools.partial(bundle_kernel, devices=devices, choices=choices),
            out_shape=jax.ShapeDtypeStruct((2, *own.shape), own.dtype),
            in_specs=[vmem] * len(held),
            out_specs=vmem,
            compiler_params=pltpu.CompilerParams(vmem_limit_bytes=6 * 2**20),
            name=name,
        )(*held)

    early = upwards(bundle("early", (own, first, second), EARLY_CHOICES), (4, 4), EARLY_TARGETS)
    late = upwards(
        bundle("late", (own, first, second, third, fourth), LATE_CHOICES), (4, 4), LATE_TARGETS
    )

    params = pltpu.CompilerParams(vmem_limit_bytes=14 * 2**20)
    row = jax.ShapeDtypeStruct((kv_count, 1, lanes), jnp.float32)
    state = [row, row, jax.ShapeDtypeStruct((kv_count, width, lanes), jnp.float32)]

    def cost(count):
        work = kv_count * count * block * lanes
        return pl.CostEstimate(
            flops=4 * work * width, bytes_accessed=4 * 2**20, transcendentals=work
        )

    near = (own, first, second, third, fourth)
    folded, far_bias, *known = pl.pallas_call(
        functools.partial(near_kernel, devices=devices, group=group),
        out_shape=[
            jax.ShapeDtypeStruct((kv_count, width, lanes), jnp.bfloat16),
            jax.ShapeDtypeStruct((2, 2 * block, lanes), jnp.float32),
            *state,
        ],
        in_specs=[smem] + [vmem] * (2 + len(near)),
        out_specs=[vmem] * 5,
        scratch_shapes=[pltpu.VMEM((len(near) * block, lanes), jnp.float32)],
        compiler_params=params,
        cost_estimate=cost(len(near)),
        name="near",
    )(doc_lengths, queries, partner_queries, *near)
    known = pl.pallas_call(
        functools.partial(far_kernel, number=0),
        out_shape=state,
        in_specs=[vmem] * 6,
        out_specs=[vmem] * 3,
        compiler_params=params,
        cost_estimate=cost(2),
        name="middle",
    )(folded, far_bias, *known, early)
    return pl.pallas_call(
        functools.partial(far_kernel, number=1),
        out_shape=jax.ShapeDtypeStruct((block, 2 * heads, width), jnp.bfloat16),
        in_specs=[vmem] * 6,
        out_specs=pl.BlockSpec(memory_space=pl.ANY),
        scratch_shapes=[
            pltpu.VMEM((kv_count // 2, block, 2 * group, width), jnp.bfloat16),
            pltpu.SemaphoreType.DMA((kv_count // 2, 2)),
        ],
        compiler_params=params,
        cost_estimate=cost(2),
        name="finish",
    )(folded, far_bias, *known, late)


def solution(mesh):
    in_specs = (P("ctx", "head", None), P("ctx", "head", None), P("ctx", "head", None), P())
    out_specs = P(("ctx", "head"), None, None)
    return jax.shard_map(shards, mesh=mesh, in_specs=in_specs, out_specs=out_specs, check_vma=False)
```

```python
import functools
import math

import jax
import jax.numpy as jnp
from jax import lax
from jax.experimental import pallas as pl
from jax.experimental.pallas import tpu as pltpu
from jax.sharding import PartitionSpec as P

REACH_LOG = 3
MASKED_SCORE = -1e30

STEPS = ((3, 1), (4, 4), (1, 3), (2, 2))
EARLY_TARGETS = (0, 1, 3, 2)
LATE_TARGETS = (0, 2, 1, 3)
EARLY_CHOICES = ((1, (1, 1, 1, 1)), (2, (2, 2, 0, 2)))
LATE_CHOICES = ((3, (3, 1, 3, 1)), (4, (4, 0, 4, 2)))
EARLY_DISTANCES = ((5, 7, (5, 7, 6, 6)), (8, 8, (8, 8, 7, 5)))
LATE_DISTANCES = ((7, 5, (7, 6, 8, 7)), (6, 6, (6, 5, 5, 8)))


def query_bounds(first_place, lanes, group, doc_lengths):
    place = first_place + lax.broadcasted_iota(jnp.int32, (1, lanes), 1) // group
    begin = jnp.zeros((1, lanes), jnp.int32)
    end = jnp.int32(0)
    for j in range(doc_lengths.shape[0]):
        end = end + doc_lengths[j]
        begin = jnp.where(place >= end, end, begin)
    return place, begin


def block_bias(stretch, distance, block, group, doc_lengths):
    lanes = block * group
    first = stretch * block
    place, begin = query_bounds(first, lanes, group, doc_lengths)
    key_place = first - distance * block + lax.broadcasted_iota(jnp.int32, (block, lanes), 0)
    allowed = (key_place >= begin) & (key_place <= place)
    return jnp.where(allowed, 0.0, MASKED_SCORE)


def score(q, keys, bias):
    factor = math.log2(math.e) / math.sqrt(q.shape[0])
    return jnp.dot(keys, q, preferred_element_type=jnp.float32) * factor + bias


def mix(values, weights):
    return lax.dot_general(
        values,
        weights.astype(jnp.bfloat16),
        (((0,), (0,)), ((), ())),
        preferred_element_type=jnp.float32,
    )


def pack_kernel(*refs, kept):
    if kept:
        keys, values, queries, out, given_queries, staged, sems = refs
    else:
        keys, values, out, staged, sems = refs
    core = lax.axis_index("head")
    block = out.shape[2]
    given_rows = pl.ds((1 - core) * block, block)
    rows = pl.ds(core * block, block) if kept else given_rows
    copies = [
        pltpu.make_async_copy(keys.at[rows], staged.at[0], sems.at[0]),
        pltpu.make_async_copy(values.at[rows], staged.at[1], sems.at[1]),
    ]
    if kept:
        copies.append(pltpu.make_async_copy(queries.at[given_rows], given_queries, sems.at[2]))
    for copy in copies:
        copy.start()
    for kind in range(2):
        copies[kind].wait()
        out[kind] = jnp.swapaxes(staged[kind].astype(jnp.float32), 0, 1).astype(out.dtype)
    for copy in copies[2:]:
        copy.wait()


def chain_position(devices):
    device, core = lax.axis_index("ctx"), lax.axis_index("head")
    return jnp.where(core == 0, device, 2 * devices - 1 - device)


def bundle_kernel(*refs, devices, choices):
    held, out = refs[:-1], refs[-1]
    source = chain_position(devices) - (devices - 4)
    for slot, (usual, special) in enumerate(choices):
        for number, ref in enumerate(held):
            if number != usual and number not in special:
                continue
            chosen = jnp.bool_(number == usual)
            for row, other in enumerate(special):
                chosen = jnp.where(source == row, number == other, chosen)

            @pl.when(chosen)
            def _(slot=slot, ref=ref):
                out[slot] = ref[...]


def near_kernel(doc_lengths, queries, partner_queries, *refs, devices, group):
    blocks, (folded, far_bias, peak, sums, mixes, bias) = refs[:-6], refs[-6:]
    stretch, core = chain_position(devices), lax.axis_index("head")
    kv_count, block, width = blocks[0].shape[1:]
    lanes = block * group
    odd = stretch % 2 == 1
    for row in range(len(blocks)):
        distance = 0
        if row > 0:
            by_even, by_odd = STEPS[row - 1]
            if by_even % 2 == 1:
                by_even, by_odd = by_odd, by_even
            distance = jnp.where(odd, by_odd, by_even)
        bias[row * block : (row + 1) * block, :] = block_bias(
            stretch, distance, block, group, doc_lengths
        )

    def gather(kind, head):
        return jnp.concatenate([ref[kind, head] for ref in blocks], axis=0)

    for half in range(2):
        side = core if half == 0 else 1 - core
        for begin in range(0, kv_count // 2, 2):
            first_head = side * (kv_count // 2) + begin
            slots = [half * (kv_count // 2) + begin + part for part in range(2)]
            heads = slice(begin * group, (begin + 2) * group)
            if half == 0:
                both = queries[pl.ds(core * block, block), heads, :]
            else:
                both = partner_queries[:, heads, :]
            both = both.astype(jnp.float32)
            qs = [
                both[:, part * group : (part + 1) * group, :]
                .reshape(lanes, width)
                .T.astype(jnp.bfloat16)
                for part in range(2)
            ]
            scores = [
                score(q, gather(0, first_head + part), bias[...]) for part, q in enumerate(qs)
            ]
            largest = [jnp.max(each, axis=0, keepdims=True) for each in scores]
            weights = [jnp.exp2(each - top) for each, top in zip(scores, largest)]
            for part, slot in enumerate(slots):
                folded[slot] = qs[part]
                peak[slot] = largest[part]
                sums[slot] = jnp.sum(weights[part], axis=0, keepdims=True)
                mixes[slot] = mix(gather(1, first_head + part), weights[part])
    turn = stretch - devices
    for number, table in enumerate((EARLY_DISTANCES, LATE_DISTANCES)):
        for row, (even_distance, odd_distance, special) in enumerate(table):
            distance = jnp.where(odd, odd_distance, even_distance)
            for at, other in enumerate(special):
                distance = jnp.where(turn == at, other, distance)
            far_bias[number, row * block : (row + 1) * block, :] = block_bias(
                stretch, distance, block, group, doc_lengths
            )


def far_kernel(folded, far_bias, peak, sums, mixes, blocks, *refs, number):
    ends = number == 1
    if ends:
        out, staged, sems = refs
    else:
        new_peak, new_sums, new_mixes = refs
    core = lax.axis_index("head")
    _, _, kv_count, block, width = blocks.shape
    group = folded.shape[2] // block
    half = kv_count // 2
    copies = []

    def weigh(slots, heads):
        scores = [
            score(
                folded[slot], blocks[:, 0, head].reshape(2 * block, width), far_bias[number]
            )
            for slot, head in zip(slots, heads)
        ]
        largest = [
            jnp.maximum(jnp.max(each, axis=0, keepdims=True), peak[slot])
            for each, slot in zip(scores, slots)
        ]
        weights = [jnp.exp2(each - top) for each, top in zip(scores, largest)]
        shrinks = [jnp.exp2(peak[slot] - top) for slot, top in zip(slots, largest)]
        totals = [
            jnp.sum(each, axis=0, keepdims=True) + sums[slot] * shrink
            for each, slot, shrink in zip(weights, slots, shrinks)
        ]
        return largest, weights, shrinks, totals

    def merge(slots, heads, largest, weights, shrinks, totals):
        mixed = [
            mix(blocks[:, 1, head].reshape(2 * block, width), each)
            for head, each in zip(heads, weights)
        ]
        if not ends:
            for part, slot in enumerate(slots):
                new_peak[slot] = largest[part]
                new_sums[slot] = totals[part]
                new_mixes[slot] = mixed[part] + mixes[slot] * shrinks[part]
            return
        done = []
        for part, slot in enumerate(slots):
            scale = 1.0 / totals[part]
            result = mixed[part] * scale + mixes[slot] * (shrinks[part] * scale)
            done.append(result.T.reshape(block, group, width))
        pair = slots[0] // 2
        staged[pair] = jnp.concatenate(done, axis=1).astype(staged.dtype)
        first = pl.multiple_of(heads[0] * group, 2 * group)
        copy = pltpu.make_async_copy(
            staged.at[pair], out.at[:, pl.ds(first, 2 * group)], sems.at[pair]
        )
        copy.start()
        copies.append(copy)

    waiting = None
    for begin in range(0, kv_count, 2):
        side = core if begin < half else 1 - core
        slots = [begin, begin + 1]
        heads = [side * half + slot % half for slot in slots]
        weighed = weigh(slots, heads)
        if waiting is not None:
            merge(*waiting)
        waiting = (slots, heads, *weighed)
    merge(*waiting)
    for copy in copies:
        copy.wait()


def shards(queries, key_heads, value_head_rows, doc_lengths):
    stride, heads, width = queries.shape
    kv_half = key_heads.shape[1]
    block = stride // 2
    kv_count = 2 * kv_half
    group = heads // kv_half
    lanes = block * group
    devices = lax.axis_size("ctx")
    core = lax.axis_index("head")
    stretches = 2 * devices

    def owner(place):
        return 2 * place if place < devices else 2 * (stretches - 1 - place) + 1

    def swap(array):
        return lax.ppermute(array, "head", [(0, 1), (1, 0)])

    def upwards(array, steps, turned=()):
        target = {at: at + steps[at % 2] for at in range(stretches)}
        for number, to in enumerate(turned):
            target[devices - 4 + number] = devices + to
        pairs = [(owner(at), owner(to)) for at, to in target.items() if to < stretches]
        return lax.ppermute(array, ("ctx", "head"), pairs)

    smem = pl.BlockSpec(memory_space=pltpu.SMEM)
    vmem = pl.BlockSpec(memory_space=pltpu.VMEM)
    def pack(kept):
        arrays = (key_heads, value_head_rows, queries) if kept else (key_heads, value_head_rows)
        out_shape = [jax.ShapeDtypeStruct((2, kv_half, block, width), jnp.bfloat16)]
        if kept:
            out_shape.append(jax.ShapeDtypeStruct((block, heads, width), jnp.bfloat16))
        return pl.pallas_call(
            functools.partial(pack_kernel, kept=kept),
            out_shape=out_shape,
            in_specs=[pl.BlockSpec(memory_space=pltpu.HBM)] * len(arrays),
            out_specs=[vmem] * len(out_shape),
            scratch_shapes=[
                pltpu.VMEM((2, block, kv_half, width), jnp.bfloat16),
                pltpu.SemaphoreType.DMA((len(arrays),)),
            ],
            compiler_params=pltpu.CompilerParams(vmem_limit_bytes=6 * 2**20),
            cost_estimate=pl.CostEstimate(
                flops=0, bytes_accessed=len(arrays) * 2**20, transcendentals=0
            ),
            name="keep" if kept else "give",
        )(*[pltpu.with_memory_space_constraint(array, pltpu.HBM) for array in arrays])

    (given,) = pack(False)
    given = swap(given)
    keep, given_queries = pack(True)
    own = jnp.concatenate(
        [jnp.where(core == 0, keep, given), jnp.where(core == 0, given, keep)], axis=1
    )
    own, given_queries = lax.optimization_barrier((own, given_queries))
    partner_queries = swap(given_queries)
    first = upwards(own, STEPS[0])
    own, partner_queries = lax.optimization_barrier((own, partner_queries))
    second, third, fourth = [upwards(own, steps) for steps in STEPS[1:]]

    def bundle(name, held, choices):
        return pl.pallas_call(
            functools.partial(bundle_kernel, devices=devices, choices=choices),
            out_shape=jax.ShapeDtypeStruct((2, *own.shape), own.dtype),
            in_specs=[vmem] * len(held),
            out_specs=vmem,
            compiler_params=pltpu.CompilerParams(vmem_limit_bytes=6 * 2**20),
            name=name,
        )(*held)

    early = upwards(bundle("early", (own, first, second), EARLY_CHOICES), (4, 4), EARLY_TARGETS)
    late = upwards(
        bundle("late", (own, first, second, third, fourth), LATE_CHOICES), (4, 4), LATE_TARGETS
    )

    params = pltpu.CompilerParams(vmem_limit_bytes=14 * 2**20)
    row = jax.ShapeDtypeStruct((kv_count, 1, lanes), jnp.float32)
    state = [row, row, jax.ShapeDtypeStruct((kv_count, width, lanes), jnp.float32)]

    def cost(count):
        work = kv_count * count * block * lanes
        return pl.CostEstimate(
            flops=4 * work * width, bytes_accessed=4 * 2**20, transcendentals=work
        )

    near = (own, first, second, third, fourth)
    folded, far_bias, *known = pl.pallas_call(
        functools.partial(near_kernel, devices=devices, group=group),
        out_shape=[
            jax.ShapeDtypeStruct((kv_count, width, lanes), jnp.bfloat16),
            jax.ShapeDtypeStruct((2, 2 * block, lanes), jnp.float32),
            *state,
        ],
        in_specs=[smem] + [vmem] * (2 + len(near)),
        out_specs=[vmem] * 5,
        scratch_shapes=[pltpu.VMEM((len(near) * block, lanes), jnp.float32)],
        compiler_params=params,
        cost_estimate=cost(len(near)),
        name="near",
    )(doc_lengths, queries, partner_queries, *near)
    known = pl.pallas_call(
        functools.partial(far_kernel, number=0),
        out_shape=state,
        in_specs=[vmem] * 6,
        out_specs=[vmem] * 3,
        compiler_params=params,
        cost_estimate=cost(2),
        name="middle",
    )(folded, far_bias, *known, early)
    return pl.pallas_call(
        functools.partial(far_kernel, number=1),
        out_shape=jax.ShapeDtypeStruct((block, 2 * heads, width), jnp.bfloat16),
        in_specs=[vmem] * 6,
        out_specs=pl.BlockSpec(memory_space=pl.ANY),
        scratch_shapes=[
            pltpu.VMEM((kv_count // 2, block, 2 * group, width), jnp.bfloat16),
            pltpu.SemaphoreType.DMA((kv_count // 2,)),
        ],
        compiler_params=params,
        cost_estimate=cost(2),
        name="finish",
    )(folded, far_bias, *known, late)


def solution(mesh):
    in_specs = (P("ctx", "head", None), P("ctx", "head", None), P("ctx", "head", None), P())
    out_specs = P(("ctx", "head"), None, None)
    return jax.shard_map(shards, mesh=mesh, in_specs=in_specs, out_specs=out_specs, check_vma=False)
```

```python
import functools
import math

import jax
import jax.numpy as jnp
from jax import lax
from jax.experimental import pallas as pl
from jax.experimental.pallas import tpu as pltpu
from jax.sharding import PartitionSpec as P

REACH_LOG = 3
MASKED_SCORE = -1e30

ORDERS = (
    ((3, 4, 1, 2), (1, 4, 3, 2), (3, 4, 1, 2), (1, 4, 3, 2)),
    ((3, 4, 1, 2), (1, 3, 4, 2), (4, 3, 1, 2), (1, 4, 3, 2)),
)
EARLY_TARGETS = (0, 1, 3, 2)
LATE_TARGETS = (0, 2, 3, 1)
EARLY_CHOICES = ((1, (1, 1, 1, 1)), (2, (2, 2, 0, 2)))
LATE_CHOICES = ((3, (3, 1, 3, 1)), (4, (4, 0, 4, 2)))


def schedule(stretches):
    middle = stretches // 2
    near_steps = [{} for _ in range(4)]
    held = [{0: at} for at in range(stretches)]
    for at in range(stretches):
        for distance, step in enumerate(ORDERS[at >= middle][at % 4], 1):
            if at + distance < stretches:
                near_steps[step - 1][at] = at + distance
                held[at + distance][step] = at
    nothing = stretches
    distances = [
        [to - held[to].get(step, to - nothing) for step in range(1, 5)] + [nothing] * 4
        for to in range(stretches)
    ]
    far_steps = []
    for number, (targets, choices) in enumerate(
        ((EARLY_TARGETS, EARLY_CHOICES), (LATE_TARGETS, LATE_CHOICES))
    ):
        far_steps.append({})
        for at in range(stretches - 4):
            turning = middle - 4 <= at < middle
            row = at - (middle - 4)
            to = middle + targets[row] if turning else at + 4
            sent = [special[row] if turning else usual for usual, special in choices]
            if not any(what in held[at] for what in sent):
                continue
            far_steps[-1][at] = to
            for slot, what in enumerate(sent):
                if what in held[at]:
                    distances[to][4 + 2 * number + slot] = to - held[at][what]
    return near_steps, far_steps, distances


def query_bounds(first_place, lanes, group, doc_lengths):
    place = first_place + lax.broadcasted_iota(jnp.int32, (1, lanes), 1) // group
    begin = jnp.zeros((1, lanes), jnp.int32)
    end = jnp.int32(0)
    for j in range(doc_lengths.shape[0]):
        end = end + doc_lengths[j]
        begin = jnp.where(place >= end, end, begin)
    return place, begin


def block_bias(stretch, distance, block, group, doc_lengths):
    lanes = block * group
    first = stretch * block
    place, begin = query_bounds(first, lanes, group, doc_lengths)
    key_place = first - distance * block + lax.broadcasted_iota(jnp.int32, (block, lanes), 0)
    allowed = (key_place >= begin) & (key_place <= place)
    return jnp.where(allowed, 0.0, MASKED_SCORE)


def score(q, keys, bias):
    factor = math.log2(math.e) / math.sqrt(q.shape[0])
    return jnp.dot(keys, q, preferred_element_type=jnp.float32) * factor + bias


def mix(values, weights):
    return lax.dot_general(
        values,
        weights.astype(jnp.bfloat16),
        (((0,), (0,)), ((), ())),
        preferred_element_type=jnp.float32,
    )


def pack_kernel(*refs, kept):
    if kept:
        keys, values, queries, out, given_queries, staged, sems = refs
    else:
        keys, values, out, staged, sems = refs
    core = lax.axis_index("head")
    block = out.shape[2]
    given_rows = pl.ds((1 - core) * block, block)
    rows = pl.ds(core * block, block) if kept else given_rows
    copies = [
        pltpu.make_async_copy(keys.at[rows], staged.at[0], sems.at[0]),
        pltpu.make_async_copy(values.at[rows], staged.at[1], sems.at[1]),
    ]
    if kept:
        copies.append(pltpu.make_async_copy(queries.at[given_rows], given_queries, sems.at[2]))
    for copy in copies:
        copy.start()
    for kind in range(2):
        copies[kind].wait()
        out[kind] = jnp.swapaxes(staged[kind].astype(jnp.float32), 0, 1).astype(out.dtype)
    for copy in copies[2:]:
        copy.wait()


def chain_position(devices):
    device, core = lax.axis_index("ctx"), lax.axis_index("head")
    return jnp.where(core == 0, device, 2 * devices - 1 - device)


def bundle_kernel(*refs, devices, choices):
    held, out = refs[:-1], refs[-1]
    source = chain_position(devices) - (devices - 4)
    for slot, (usual, special) in enumerate(choices):
        for number, ref in enumerate(held):
            if number != usual and number not in special:
                continue
            chosen = jnp.bool_(number == usual)
            for row, other in enumerate(special):
                chosen = jnp.where(source == row, number == other, chosen)

            @pl.when(chosen)
            def _(slot=slot, ref=ref):
                out[slot] = ref[...]


def near_kernel(doc_lengths, distances, queries, partner_queries, *refs, devices, group):
    blocks, (folded, far_bias, peak, sums, mixes, bias) = refs[:-6], refs[-6:]
    stretch, core = chain_position(devices), lax.axis_index("head")
    kv_count, block, width = blocks[0].shape[1:]
    lanes = block * group
    for row in range(len(blocks)):
        distance = 0 if row == 0 else distances[stretch, row - 1]
        bias[row * block : (row + 1) * block, :] = block_bias(
            stretch, distance, block, group, doc_lengths
        )

    def gather(kind, head):
        return jnp.concatenate([ref[kind, head] for ref in blocks], axis=0)

    for half in range(2):
        side = core if half == 0 else 1 - core
        for begin in range(0, kv_count // 2, 2):
            first_head = side * (kv_count // 2) + begin
            slots = [half * (kv_count // 2) + begin + part for part in range(2)]
            heads = slice(begin * group, (begin + 2) * group)
            if half == 0:
                both = queries[pl.ds(core * block, block), heads, :]
            else:
                both = partner_queries[:, heads, :]
            both = both.astype(jnp.float32)
            qs = [
                both[:, part * group : (part + 1) * group, :]
                .reshape(lanes, width)
                .T.astype(jnp.bfloat16)
                for part in range(2)
            ]
            scores = [
                score(q, gather(0, first_head + part), bias[...]) for part, q in enumerate(qs)
            ]
            largest = [jnp.max(each, axis=0, keepdims=True) for each in scores]
            weights = [jnp.exp2(each - top) for each, top in zip(scores, largest)]
            for part, slot in enumerate(slots):
                folded[slot] = qs[part]
                peak[slot] = largest[part]
                sums[slot] = jnp.sum(weights[part], axis=0, keepdims=True)
                mixes[slot] = mix(gather(1, first_head + part), weights[part])
    for number in range(2):
        for row in range(2):
            far_bias[number, row * block : (row + 1) * block, :] = block_bias(
                stretch, distances[stretch, 4 + 2 * number + row], block, group, doc_lengths
            )


def far_kernel(folded, far_bias, peak, sums, mixes, blocks, *refs, number):
    ends = number == 1
    if ends:
        out, staged, sems = refs
    else:
        new_peak, new_sums, new_mixes = refs
    core = lax.axis_index("head")
    _, _, kv_count, block, width = blocks.shape
    group = folded.shape[2] // block
    half = kv_count // 2
    copies = []

    def weigh(slots, heads):
        scores = [
            score(
                folded[slot], blocks[:, 0, head].reshape(2 * block, width), far_bias[number]
            )
            for slot, head in zip(slots, heads)
        ]
        largest = [
            jnp.maximum(jnp.max(each, axis=0, keepdims=True), peak[slot])
            for each, slot in zip(scores, slots)
        ]
        weights = [jnp.exp2(each - top) for each, top in zip(scores, largest)]
        shrinks = [jnp.exp2(peak[slot] - top) for slot, top in zip(slots, largest)]
        totals = [
            jnp.sum(each, axis=0, keepdims=True) + sums[slot] * shrink
            for each, slot, shrink in zip(weights, slots, shrinks)
        ]
        return largest, weights, shrinks, totals

    def merge(slots, heads, largest, weights, shrinks, totals):
        mixed = [
            mix(blocks[:, 1, head].reshape(2 * block, width), each)
            for head, each in zip(heads, weights)
        ]
        if not ends:
            for part, slot in enumerate(slots):
                new_peak[slot] = largest[part]
                new_sums[slot] = totals[part]
                new_mixes[slot] = mixed[part] + mixes[slot] * shrinks[part]
            return
        done = []
        for part, slot in enumerate(slots):
            scale = 1.0 / totals[part]
            result = mixed[part] * scale + mixes[slot] * (shrinks[part] * scale)
            done.append(result.T.reshape(block, group, width))
        pair = slots[0] // 2
        staged[pair] = jnp.concatenate(done, axis=1).astype(staged.dtype)
        first = pl.multiple_of(heads[0] * group, 2 * group)
        copy = pltpu.make_async_copy(
            staged.at[pair], out.at[:, pl.ds(first, 2 * group)], sems.at[pair]
        )
        copy.start()
        copies.append(copy)

    waiting = None
    for begin in range(0, kv_count, 2):
        side = core if begin < half else 1 - core
        slots = [begin, begin + 1]
        heads = [side * half + slot % half for slot in slots]
        weighed = weigh(slots, heads)
        if waiting is not None:
            merge(*waiting)
        waiting = (slots, heads, *weighed)
    merge(*waiting)
    for copy in copies:
        copy.wait()


def shards(queries, key_heads, value_head_rows, doc_lengths):
    stride, heads, width = queries.shape
    kv_half = key_heads.shape[1]
    block = stride // 2
    kv_count = 2 * kv_half
    group = heads // kv_half
    lanes = block * group
    devices = lax.axis_size("ctx")
    core = lax.axis_index("head")
    stretches = 2 * devices

    def owner(place):
        return 2 * place if place < devices else 2 * (stretches - 1 - place) + 1

    def swap(array):
        return lax.ppermute(array, "head", [(0, 1), (1, 0)])

    def upwards(array, step):
        pairs = [(owner(at), owner(to)) for at, to in step.items()]
        return lax.ppermute(array, ("ctx", "head"), pairs)

    near_steps, far_steps, distances = schedule(stretches)
    smem = pl.BlockSpec(memory_space=pltpu.SMEM)
    vmem = pl.BlockSpec(memory_space=pltpu.VMEM)
    def pack(kept):
        arrays = (key_heads, value_head_rows, queries) if kept else (key_heads, value_head_rows)
        out_shape = [jax.ShapeDtypeStruct((2, kv_half, block, width), jnp.bfloat16)]
        if kept:
            out_shape.append(jax.ShapeDtypeStruct((block, heads, width), jnp.bfloat16))
        return pl.pallas_call(
            functools.partial(pack_kernel, kept=kept),
            out_shape=out_shape,
            in_specs=[pl.BlockSpec(memory_space=pltpu.HBM)] * len(arrays),
            out_specs=[vmem] * len(out_shape),
            scratch_shapes=[
                pltpu.VMEM((2, block, kv_half, width), jnp.bfloat16),
                pltpu.SemaphoreType.DMA((len(arrays),)),
            ],
            compiler_params=pltpu.CompilerParams(vmem_limit_bytes=6 * 2**20),
            cost_estimate=pl.CostEstimate(
                flops=0, bytes_accessed=len(arrays) * 2**20, transcendentals=0
            ),
            name="keep" if kept else "give",
        )(*[pltpu.with_memory_space_constraint(array, pltpu.HBM) for array in arrays])

    (given,) = pack(False)
    given = swap(given)
    keep, given_queries = pack(True)
    own = jnp.concatenate(
        [jnp.where(core == 0, keep, given), jnp.where(core == 0, given, keep)], axis=1
    )
    own, given_queries = lax.optimization_barrier((own, given_queries))
    partner_queries = swap(given_queries)
    first = upwards(own, near_steps[0])
    own, partner_queries = lax.optimization_barrier((own, partner_queries))
    second, third, fourth = [upwards(own, step) for step in near_steps[1:]]

    def bundle(name, held, choices):
        return pl.pallas_call(
            functools.partial(bundle_kernel, devices=devices, choices=choices),
            out_shape=jax.ShapeDtypeStruct((2, *own.shape), own.dtype),
            in_specs=[vmem] * len(held),
            out_specs=vmem,
            compiler_params=pltpu.CompilerParams(vmem_limit_bytes=6 * 2**20),
            name=name,
        )(*held)

    early = upwards(bundle("early", (own, first, second), EARLY_CHOICES), far_steps[0])
    late = upwards(
        bundle("late", (own, first, second, third, fourth), LATE_CHOICES), far_steps[1]
    )

    params = pltpu.CompilerParams(vmem_limit_bytes=14 * 2**20)
    row = jax.ShapeDtypeStruct((kv_count, 1, lanes), jnp.float32)
    state = [row, row, jax.ShapeDtypeStruct((kv_count, width, lanes), jnp.float32)]

    def cost(count):
        work = kv_count * count * block * lanes
        return pl.CostEstimate(
            flops=4 * work * width, bytes_accessed=4 * 2**20, transcendentals=work
        )

    near = (own, first, second, third, fourth)
    folded, far_bias, *known = pl.pallas_call(
        functools.partial(near_kernel, devices=devices, group=group),
        out_shape=[
            jax.ShapeDtypeStruct((kv_count, width, lanes), jnp.bfloat16),
            jax.ShapeDtypeStruct((2, 2 * block, lanes), jnp.float32),
            *state,
        ],
        in_specs=[smem] * 2 + [vmem] * (2 + len(near)),
        out_specs=[vmem] * 5,
        scratch_shapes=[pltpu.VMEM((len(near) * block, lanes), jnp.float32)],
        compiler_params=params,
        cost_estimate=cost(len(near)),
        name="near",
    )(doc_lengths, jnp.array(distances, jnp.int32), queries, partner_queries, *near)
    known = pl.pallas_call(
        functools.partial(far_kernel, number=0),
        out_shape=state,
        in_specs=[vmem] * 6,
        out_specs=[vmem] * 3,
        compiler_params=params,
        cost_estimate=cost(2),
        name="middle",
    )(folded, far_bias, *known, early)
    return pl.pallas_call(
        functools.partial(far_kernel, number=1),
        out_shape=jax.ShapeDtypeStruct((block, 2 * heads, width), jnp.bfloat16),
        in_specs=[vmem] * 6,
        out_specs=pl.BlockSpec(memory_space=pl.ANY),
        scratch_shapes=[
            pltpu.VMEM((kv_count // 2, block, 2 * group, width), jnp.bfloat16),
            pltpu.SemaphoreType.DMA((kv_count // 2,)),
        ],
        compiler_params=params,
        cost_estimate=cost(2),
        name="finish",
    )(folded, far_bias, *known, late)


def solution(mesh):
    in_specs = (P("ctx", "head", None), P("ctx", "head", None), P("ctx", "head", None), P())
    out_specs = P(("ctx", "head"), None, None)
    return jax.shard_map(shards, mesh=mesh, in_specs=in_specs, out_specs=out_specs, check_vma=False)
```

```python
import functools
import math

import jax
import jax.numpy as jnp
from jax import lax
from jax.experimental import pallas as pl
from jax.experimental.pallas import tpu as pltpu
from jax.sharding import PartitionSpec as P

REACH_LOG = 3
MASKED_SCORE = -1e30

ORDERS = ((3, 4, 1, 2), (1, 4, 3, 2))
EARLY_TARGETS = (0, 1, 3, 2)
LATE_TARGETS = (0, 2, 1, 3)
EARLY_CHOICES = ((1, (1, 1, 1, 1)), (2, (2, 2, 0, 2)))
LATE_CHOICES = ((3, (3, 1, 3, 1)), (4, (4, 0, 4, 2)))


def schedule(stretches):
    middle = stretches // 2
    near_steps = [{} for _ in range(4)]
    held = [{0: at} for at in range(stretches)]
    for at in range(stretches):
        for distance, step in enumerate(ORDERS[at % 2], 1):
            if at + distance < stretches:
                near_steps[step - 1][at] = at + distance
                held[at + distance][step] = at
    nothing = stretches
    distances = [
        [to - held[to].get(step, to - nothing) for step in range(1, 5)] + [nothing] * 4
        for to in range(stretches)
    ]
    far_steps = []
    for number, (targets, choices) in enumerate(
        ((EARLY_TARGETS, EARLY_CHOICES), (LATE_TARGETS, LATE_CHOICES))
    ):
        far_steps.append({})
        for at in range(stretches - 4):
            turning = middle - 4 <= at < middle
            row = at - (middle - 4)
            to = middle + targets[row] if turning else at + 4
            sent = [special[row] if turning else usual for usual, special in choices]
            if not any(what in held[at] for what in sent):
                continue
            far_steps[-1][at] = to
            for slot, what in enumerate(sent):
                if what in held[at]:
                    distances[to][4 + 2 * number + slot] = to - held[at][what]
    return near_steps, far_steps, distances


def query_bounds(first_place, lanes, group, doc_lengths):
    place = first_place + lax.broadcasted_iota(jnp.int32, (1, lanes), 1) // group
    begin = jnp.zeros((1, lanes), jnp.int32)
    end = jnp.int32(0)
    for j in range(doc_lengths.shape[0]):
        end = end + doc_lengths[j]
        begin = jnp.where(place >= end, end, begin)
    return place, begin


def block_bias(stretch, distance, block, group, doc_lengths):
    lanes = block * group
    first = stretch * block
    place, begin = query_bounds(first, lanes, group, doc_lengths)
    key_place = first - distance * block + lax.broadcasted_iota(jnp.int32, (block, lanes), 0)
    allowed = (key_place >= begin) & (key_place <= place)
    return jnp.where(allowed, 0.0, MASKED_SCORE)


def score(q, keys, bias):
    factor = math.log2(math.e) / math.sqrt(q.shape[0])
    return jnp.dot(keys, q, preferred_element_type=jnp.float32) * factor + bias


def mix(values, weights):
    return lax.dot_general(
        values,
        weights.astype(jnp.bfloat16),
        (((0,), (0,)), ((), ())),
        preferred_element_type=jnp.float32,
    )


def pack_kernel(*refs, kept):
    if kept:
        keys, values, queries, out, given_queries, staged, sems = refs
    else:
        keys, values, out, staged, sems = refs
    core = lax.axis_index("head")
    block = out.shape[2]
    given_rows = pl.ds((1 - core) * block, block)
    rows = pl.ds(core * block, block) if kept else given_rows
    copies = [
        pltpu.make_async_copy(keys.at[rows], staged.at[0], sems.at[0]),
        pltpu.make_async_copy(values.at[rows], staged.at[1], sems.at[1]),
    ]
    if kept:
        copies.append(pltpu.make_async_copy(queries.at[given_rows], given_queries, sems.at[2]))
    for copy in copies:
        copy.start()
    for kind in range(2):
        copies[kind].wait()
        out[kind] = jnp.swapaxes(staged[kind].astype(jnp.float32), 0, 1).astype(out.dtype)
    for copy in copies[2:]:
        copy.wait()


def chain_position(devices):
    device, core = lax.axis_index("ctx"), lax.axis_index("head")
    return jnp.where(core == 0, device, 2 * devices - 1 - device)


def bundle_kernel(*refs, devices, choices):
    held, out = refs[:-1], refs[-1]
    source = chain_position(devices) - (devices - 4)
    for slot, (usual, special) in enumerate(choices):
        for number, ref in enumerate(held):
            if number != usual and number not in special:
                continue
            chosen = jnp.bool_(number == usual)
            for row, other in enumerate(special):
                chosen = jnp.where(source == row, number == other, chosen)

            @pl.when(chosen)
            def _(slot=slot, ref=ref):
                out[slot] = ref[...]


def near_kernel(doc_lengths, distances, queries, partner_queries, *refs, devices, group):
    blocks, (folded, far_bias, peak, sums, mixes, bias) = refs[:-6], refs[-6:]
    stretch, core = chain_position(devices), lax.axis_index("head")
    kv_count, block, width = blocks[0].shape[1:]
    lanes = block * group
    for row in range(len(blocks)):
        distance = 0 if row == 0 else distances[stretch, row - 1]
        bias[row * block : (row + 1) * block, :] = block_bias(
            stretch, distance, block, group, doc_lengths
        )

    def gather(kind, head):
        return jnp.concatenate([ref[kind, head] for ref in blocks], axis=0)

    for half in range(2):
        side = core if half == 0 else 1 - core
        for begin in range(0, kv_count // 2, 2):
            first_head = side * (kv_count // 2) + begin
            slots = [half * (kv_count // 2) + begin + part for part in range(2)]
            heads = slice(begin * group, (begin + 2) * group)
            if half == 0:
                both = queries[pl.ds(core * block, block), heads, :]
            else:
                both = partner_queries[:, heads, :]
            both = both.astype(jnp.float32)
            qs = [
                both[:, part * group : (part + 1) * group, :]
                .reshape(lanes, width)
                .T.astype(jnp.bfloat16)
                for part in range(2)
            ]
            scores = [
                score(q, gather(0, first_head + part), bias[...]) for part, q in enumerate(qs)
            ]
            largest = [jnp.max(each, axis=0, keepdims=True) for each in scores]
            weights = [jnp.exp2(each - top) for each, top in zip(scores, largest)]
            for part, slot in enumerate(slots):
                folded[slot] = qs[part]
                peak[slot] = largest[part]
                sums[slot] = jnp.sum(weights[part], axis=0, keepdims=True)
                mixes[slot] = mix(gather(1, first_head + part), weights[part])
    for number in range(2):
        for row in range(2):
            far_bias[number, row * block : (row + 1) * block, :] = block_bias(
                stretch, distances[stretch, 4 + 2 * number + row], block, group, doc_lengths
            )


def far_kernel(folded, far_bias, peak, sums, mixes, blocks, *refs, number):
    ends = number == 1
    if ends:
        out, staged, sems = refs
    else:
        new_peak, new_sums, new_mixes = refs
    core = lax.axis_index("head")
    _, _, kv_count, block, width = blocks.shape
    group = folded.shape[2] // block
    half = kv_count // 2
    copies = []

    def weigh(slots, heads):
        scores = [
            score(
                folded[slot], blocks[:, 0, head].reshape(2 * block, width), far_bias[number]
            )
            for slot, head in zip(slots, heads)
        ]
        largest = [
            jnp.maximum(jnp.max(each, axis=0, keepdims=True), peak[slot])
            for each, slot in zip(scores, slots)
        ]
        weights = [jnp.exp2(each - top) for each, top in zip(scores, largest)]
        shrinks = [jnp.exp2(peak[slot] - top) for slot, top in zip(slots, largest)]
        totals = [
            jnp.sum(each, axis=0, keepdims=True) + sums[slot] * shrink
            for each, slot, shrink in zip(weights, slots, shrinks)
        ]
        return largest, weights, shrinks, totals

    def merge(slots, heads, largest, weights, shrinks, totals):
        mixed = [
            mix(blocks[:, 1, head].reshape(2 * block, width), each)
            for head, each in zip(heads, weights)
        ]
        if not ends:
            for part, slot in enumerate(slots):
                new_peak[slot] = largest[part]
                new_sums[slot] = totals[part]
                new_mixes[slot] = mixed[part] + mixes[slot] * shrinks[part]
            return
        done = []
        for part, slot in enumerate(slots):
            scale = 1.0 / totals[part]
            result = mixed[part] * scale + mixes[slot] * (shrinks[part] * scale)
            done.append(result.T.reshape(block, group, width))
        pair = slots[0] // 2
        staged[pair] = jnp.concatenate(done, axis=1).astype(staged.dtype)
        first = pl.multiple_of(heads[0] * group, 2 * group)
        copy = pltpu.make_async_copy(
            staged.at[pair], out.at[:, pl.ds(first, 2 * group)], sems.at[pair]
        )
        copy.start()
        copies.append(copy)

    waiting = None
    for begin in range(0, kv_count, 2):
        side = core if begin < half else 1 - core
        slots = [begin, begin + 1]
        heads = [side * half + slot % half for slot in slots]
        weighed = weigh(slots, heads)
        if waiting is not None:
            merge(*waiting)
        waiting = (slots, heads, *weighed)
    merge(*waiting)
    for copy in copies:
        copy.wait()


def shards(queries, key_heads, value_head_rows, doc_lengths):
    stride, heads, width = queries.shape
    kv_half = key_heads.shape[1]
    block = stride // 2
    kv_count = 2 * kv_half
    group = heads // kv_half
    lanes = block * group
    devices = lax.axis_size("ctx")
    core = lax.axis_index("head")
    stretches = 2 * devices

    def owner(place):
        return 2 * place if place < devices else 2 * (stretches - 1 - place) + 1

    def swap(array):
        return lax.ppermute(array, "head", [(0, 1), (1, 0)])

    def upwards(array, step):
        pairs = [(owner(at), owner(to)) for at, to in step.items()]
        return lax.ppermute(array, ("ctx", "head"), pairs)

    near_steps, far_steps, distances = schedule(stretches)
    smem = pl.BlockSpec(memory_space=pltpu.SMEM)
    vmem = pl.BlockSpec(memory_space=pltpu.VMEM)
    def pack(kept):
        arrays = (key_heads, value_head_rows, queries) if kept else (key_heads, value_head_rows)
        out_shape = [jax.ShapeDtypeStruct((2, kv_half, block, width), jnp.bfloat16)]
        if kept:
            out_shape.append(jax.ShapeDtypeStruct((block, heads, width), jnp.bfloat16))
        return pl.pallas_call(
            functools.partial(pack_kernel, kept=kept),
            out_shape=out_shape,
            in_specs=[pl.BlockSpec(memory_space=pltpu.HBM)] * len(arrays),
            out_specs=[vmem] * len(out_shape),
            scratch_shapes=[
                pltpu.VMEM((2, block, kv_half, width), jnp.bfloat16),
                pltpu.SemaphoreType.DMA((len(arrays),)),
            ],
            compiler_params=pltpu.CompilerParams(vmem_limit_bytes=6 * 2**20),
            cost_estimate=pl.CostEstimate(
                flops=0, bytes_accessed=len(arrays) * 2**20, transcendentals=0
            ),
            name="keep" if kept else "give",
        )(*[pltpu.with_memory_space_constraint(array, pltpu.HBM) for array in arrays])

    (given,) = pack(False)
    given = swap(given)
    keep, given_queries = pack(True)
    own = jnp.concatenate(
        [jnp.where(core == 0, keep, given), jnp.where(core == 0, given, keep)], axis=1
    )
    own, given_queries = lax.optimization_barrier((own, given_queries))
    partner_queries = swap(given_queries)
    first = upwards(own, near_steps[0])
    own, partner_queries = lax.optimization_barrier((own, partner_queries))
    second, third, fourth = [upwards(own, step) for step in near_steps[1:]]

    def bundle(name, held, choices):
        return pl.pallas_call(
            functools.partial(bundle_kernel, devices=devices, choices=choices),
            out_shape=jax.ShapeDtypeStruct((2, *own.shape), own.dtype),
            in_specs=[vmem] * len(held),
            out_specs=vmem,
            compiler_params=pltpu.CompilerParams(vmem_limit_bytes=6 * 2**20),
            name=name,
        )(*held)

    early = upwards(bundle("early", (own, first, second), EARLY_CHOICES), far_steps[0])
    late = upwards(
        bundle("late", (own, first, second, third, fourth), LATE_CHOICES), far_steps[1]
    )

    params = pltpu.CompilerParams(vmem_limit_bytes=14 * 2**20)
    row = jax.ShapeDtypeStruct((kv_count, 1, lanes), jnp.float32)
    state = [row, row, jax.ShapeDtypeStruct((kv_count, width, lanes), jnp.float32)]

    def cost(count):
        work = kv_count * count * block * lanes
        return pl.CostEstimate(
            flops=4 * work * width, bytes_accessed=4 * 2**20, transcendentals=work
        )

    near = (own, first, second, third, fourth)
    folded, far_bias, *known = pl.pallas_call(
        functools.partial(near_kernel, devices=devices, group=group),
        out_shape=[
            jax.ShapeDtypeStruct((kv_count, width, lanes), jnp.bfloat16),
            jax.ShapeDtypeStruct((2, 2 * block, lanes), jnp.float32),
            *state,
        ],
        in_specs=[smem] * 2 + [vmem] * (2 + len(near)),
        out_specs=[vmem] * 5,
        scratch_shapes=[pltpu.VMEM((len(near) * block, lanes), jnp.float32)],
        compiler_params=params,
        cost_estimate=cost(len(near)),
        name="near",
    )(doc_lengths, jnp.array(distances, jnp.int32), queries, partner_queries, *near)
    known = pl.pallas_call(
        functools.partial(far_kernel, number=0),
        out_shape=state,
        in_specs=[vmem] * 6,
        out_specs=[vmem] * 3,
        compiler_params=params,
        cost_estimate=cost(2),
        name="middle",
    )(folded, far_bias, *known, early)
    return pl.pallas_call(
        functools.partial(far_kernel, number=1),
        out_shape=jax.ShapeDtypeStruct((block, 2 * heads, width), jnp.bfloat16),
        in_specs=[vmem] * 6,
        out_specs=pl.BlockSpec(memory_space=pl.ANY),
        scratch_shapes=[
            pltpu.VMEM((kv_count // 2, block, 2 * group, width), jnp.bfloat16),
            pltpu.SemaphoreType.DMA((kv_count // 2,)),
        ],
        compiler_params=params,
        cost_estimate=cost(2),
        name="finish",
    )(folded, far_bias, *known, late)


def solution(mesh):
    in_specs = (P("ctx", "head", None), P("ctx", "head", None), P("ctx", "head", None), P())
    out_specs = P(("ctx", "head"), None, None)
    return jax.shard_map(shards, mesh=mesh, in_specs=in_specs, out_specs=out_specs, check_vma=False)
```

```python
import functools
import math

import jax
import jax.numpy as jnp
from jax import lax
from jax.experimental import pallas as pl
from jax.experimental.pallas import tpu as pltpu
from jax.sharding import PartitionSpec as P

REACH_LOG = 3
MASKED_SCORE = -1e30

STEPS = ((3, 1), (4, 4), (1, 3), (2, 2))
EARLY_TARGETS = (0, 1, 3, 2)
LATE_TARGETS = (0, 2, 1, 3)
EARLY_CHOICES = ((1, (1, 1, 1, 1)), (2, (2, 2, 0, 2)))
LATE_CHOICES = ((3, (3, 1, 3, 1)), (4, (4, 0, 4, 2)))
EARLY_DISTANCES = ((5, 7, (5, 7, 6, 6)), (8, 8, (8, 8, 7, 5)))
LATE_DISTANCES = ((7, 5, (7, 6, 8, 7)), (6, 6, (6, 5, 5, 8)))


def query_bounds(first_place, lanes, group, doc_lengths):
    place = first_place + lax.broadcasted_iota(jnp.int32, (1, lanes), 1) // group
    begin = jnp.zeros((1, lanes), jnp.int32)
    end = jnp.int32(0)
    for j in range(doc_lengths.shape[0]):
        end = end + doc_lengths[j]
        begin = jnp.where(place >= end, end, begin)
    return place, begin


def block_bias(stretch, distance, block, group, doc_lengths):
    lanes = block * group
    first = stretch * block
    place, begin = query_bounds(first, lanes, group, doc_lengths)
    key_place = first - distance * block + lax.broadcasted_iota(jnp.int32, (block, lanes), 0)
    allowed = (key_place >= begin) & (key_place <= place)
    return jnp.where(allowed, 0.0, MASKED_SCORE)


def score(q, keys, bias):
    factor = math.log2(math.e) / math.sqrt(q.shape[0])
    return jnp.dot(keys, q, preferred_element_type=jnp.float32) * factor + bias


def mix(values, weights):
    return lax.dot_general(
        values,
        weights.astype(jnp.bfloat16),
        (((0,), (0,)), ((), ())),
        preferred_element_type=jnp.float32,
    )


def pack_kernel(*refs, kept):
    if kept:
        keys, values, queries, out, given_queries, staged, sems = refs
    else:
        keys, values, out, staged, sems = refs
    core = lax.axis_index("head")
    block = out.shape[2]
    given_rows = pl.ds((1 - core) * block, block)
    rows = pl.ds(core * block, block) if kept else given_rows
    copies = [
        pltpu.make_async_copy(keys.at[rows], staged.at[0], sems.at[0]),
        pltpu.make_async_copy(values.at[rows], staged.at[1], sems.at[1]),
    ]
    if kept:
        copies.append(pltpu.make_async_copy(queries.at[given_rows], given_queries, sems.at[2]))
    for copy in copies:
        copy.start()
    for kind in range(2):
        copies[kind].wait()
        for head in range(out.shape[1]):
            out[kind, head] = staged[kind, :, head, :]
    for copy in copies[2:]:
        copy.wait()


def chain_position(devices):
    device, core = lax.axis_index("ctx"), lax.axis_index("head")
    return jnp.where(core == 0, device, 2 * devices - 1 - device)


def bundle_kernel(*refs, devices, choices):
    held, out = refs[:-1], refs[-1]
    source = chain_position(devices) - (devices - 4)
    for slot, (usual, special) in enumerate(choices):
        for number, ref in enumerate(held):
            if number != usual and number not in special:
                continue
            chosen = jnp.bool_(number == usual)
            for row, other in enumerate(special):
                chosen = jnp.where(source == row, number == other, chosen)

            @pl.when(chosen)
            def _(slot=slot, ref=ref):
                out[slot] = ref[...]


def near_kernel(doc_lengths, queries, partner_queries, *refs, devices, group):
    blocks, (folded, far_bias, peak, sums, mixes, bias) = refs[:-6], refs[-6:]
    stretch, core = chain_position(devices), lax.axis_index("head")
    kv_count, block, width = blocks[0].shape[1:]
    lanes = block * group
    odd = stretch % 2 == 1
    for row in range(len(blocks)):
        distance = 0
        if row > 0:
            by_even, by_odd = STEPS[row - 1]
            if by_even % 2 == 1:
                by_even, by_odd = by_odd, by_even
            distance = jnp.where(odd, by_odd, by_even)
        bias[row * block : (row + 1) * block, :] = block_bias(
            stretch, distance, block, group, doc_lengths
        )

    def gather(kind, head):
        return jnp.concatenate([ref[kind, head] for ref in blocks], axis=0)

    for half in range(2):
        side = core if half == 0 else 1 - core
        for begin in range(0, kv_count // 2, 2):
            first_head = side * (kv_count // 2) + begin
            slots = [half * (kv_count // 2) + begin + part for part in range(2)]
            heads = slice(begin * group, (begin + 2) * group)
            if half == 0:
                both = queries[pl.ds(core * block, block), heads, :]
            else:
                both = partner_queries[:, heads, :]
            both = both.astype(jnp.float32)
            qs = [
                both[:, part * group : (part + 1) * group, :]
                .reshape(lanes, width)
                .T.astype(jnp.bfloat16)
                for part in range(2)
            ]
            scores = [
                score(q, gather(0, first_head + part), bias[...]) for part, q in enumerate(qs)
            ]
            largest = [jnp.max(each, axis=0, keepdims=True) for each in scores]
            weights = [jnp.exp2(each - top) for each, top in zip(scores, largest)]
            for part, slot in enumerate(slots):
                folded[slot] = qs[part]
                peak[slot] = largest[part]
                sums[slot] = jnp.sum(weights[part], axis=0, keepdims=True)
                mixes[slot] = mix(gather(1, first_head + part), weights[part])
    turn = stretch - devices
    for number, table in enumerate((EARLY_DISTANCES, LATE_DISTANCES)):
        for row, (even_distance, odd_distance, special) in enumerate(table):
            distance = jnp.where(odd, odd_distance, even_distance)
            for at, other in enumerate(special):
                distance = jnp.where(turn == at, other, distance)
            far_bias[number, row * block : (row + 1) * block, :] = block_bias(
                stretch, distance, block, group, doc_lengths
            )


def far_kernel(folded, far_bias, peak, sums, mixes, blocks, *refs, number):
    ends = number == 1
    if ends:
        out, staged, sems = refs
    else:
        new_peak, new_sums, new_mixes = refs
    core = lax.axis_index("head")
    _, _, kv_count, block, width = blocks.shape
    group = folded.shape[2] // block
    half = kv_count // 2
    copies = []

    def weigh(slots, heads):
        scores = [
            score(
                folded[slot], blocks[:, 0, head].reshape(2 * block, width), far_bias[number]
            )
            for slot, head in zip(slots, heads)
        ]
        largest = [
            jnp.maximum(jnp.max(each, axis=0, keepdims=True), peak[slot])
            for each, slot in zip(scores, slots)
        ]
        weights = [jnp.exp2(each - top) for each, top in zip(scores, largest)]
        shrinks = [jnp.exp2(peak[slot] - top) for slot, top in zip(slots, largest)]
        totals = [
            jnp.sum(each, axis=0, keepdims=True) + sums[slot] * shrink
            for each, slot, shrink in zip(weights, slots, shrinks)
        ]
        return largest, weights, shrinks, totals

    def merge(slots, heads, largest, weights, shrinks, totals):
        mixed = [
            mix(blocks[:, 1, head].reshape(2 * block, width), each)
            for head, each in zip(heads, weights)
        ]
        if not ends:
            for part, slot in enumerate(slots):
                new_peak[slot] = largest[part]
                new_sums[slot] = totals[part]
                new_mixes[slot] = mixed[part] + mixes[slot] * shrinks[part]
            return
        done = []
        for part, slot in enumerate(slots):
            scale = 1.0 / totals[part]
            result = mixed[part] * scale + mixes[slot] * (shrinks[part] * scale)
            done.append(result.T.reshape(block, group, width))
        pair = slots[0] // 2
        staged[pair] = jnp.concatenate(done, axis=1).astype(staged.dtype)
        first = pl.multiple_of(heads[0] * group, 2 * group)
        copy = pltpu.make_async_copy(
            staged.at[pair], out.at[:, pl.ds(first, 2 * group)], sems.at[pair]
        )
        copy.start()
        copies.append(copy)

    waiting = None
    for begin in range(0, kv_count, 2):
        side = core if begin < half else 1 - core
        slots = [begin, begin + 1]
        heads = [side * half + slot % half for slot in slots]
        weighed = weigh(slots, heads)
        if waiting is not None:
            merge(*waiting)
        waiting = (slots, heads, *weighed)
    merge(*waiting)
    for copy in copies:
        copy.wait()


def shards(queries, key_heads, value_head_rows, doc_lengths):
    stride, heads, width = queries.shape
    kv_half = key_heads.shape[1]
    block = stride // 2
    kv_count = 2 * kv_half
    group = heads // kv_half
    lanes = block * group
    devices = lax.axis_size("ctx")
    core = lax.axis_index("head")
    stretches = 2 * devices

    def owner(place):
        return 2 * place if place < devices else 2 * (stretches - 1 - place) + 1

    def swap(array):
        return lax.ppermute(array, "head", [(0, 1), (1, 0)])

    def upwards(array, steps, turned=()):
        target = {at: at + steps[at % 2] for at in range(stretches)}
        for number, to in enumerate(turned):
            target[devices - 4 + number] = devices + to
        pairs = [(owner(at), owner(to)) for at, to in target.items() if to < stretches]
        return lax.ppermute(array, ("ctx", "head"), pairs)

    smem = pl.BlockSpec(memory_space=pltpu.SMEM)
    vmem = pl.BlockSpec(memory_space=pltpu.VMEM)
    def pack(kept):
        arrays = (key_heads, value_head_rows, queries) if kept else (key_heads, value_head_rows)
        out_shape = [jax.ShapeDtypeStruct((2, kv_half, block, width), jnp.bfloat16)]
        if kept:
            out_shape.append(jax.ShapeDtypeStruct((block, heads, width), jnp.bfloat16))
        return pl.pallas_call(
            functools.partial(pack_kernel, kept=kept),
            out_shape=out_shape,
            in_specs=[pl.BlockSpec(memory_space=pltpu.HBM)] * len(arrays),
            out_specs=[vmem] * len(out_shape),
            scratch_shapes=[
                pltpu.VMEM((2, block, kv_half, width), jnp.bfloat16),
                pltpu.SemaphoreType.DMA((len(arrays),)),
            ],
            compiler_params=pltpu.CompilerParams(vmem_limit_bytes=6 * 2**20),
            cost_estimate=pl.CostEstimate(
                flops=0, bytes_accessed=len(arrays) * 2**20, transcendentals=0
            ),
            name="keep" if kept else "give",
        )(*[pltpu.with_memory_space_constraint(array, pltpu.HBM) for array in arrays])

    (given,) = pack(False)
    given = swap(given)
    keep, given_queries = pack(True)
    own = jnp.concatenate(
        [jnp.where(core == 0, keep, given), jnp.where(core == 0, given, keep)], axis=1
    )
    own, given_queries = lax.optimization_barrier((own, given_queries))
    partner_queries = swap(given_queries)
    first = upwards(own, STEPS[0])
    own, partner_queries = lax.optimization_barrier((own, partner_queries))
    second, third, fourth = [upwards(own, steps) for steps in STEPS[1:]]

    def bundle(name, held, choices):
        return pl.pallas_call(
            functools.partial(bundle_kernel, devices=devices, choices=choices),
            out_shape=jax.ShapeDtypeStruct((2, *own.shape), own.dtype),
            in_specs=[vmem] * len(held),
            out_specs=vmem,
            compiler_params=pltpu.CompilerParams(vmem_limit_bytes=6 * 2**20),
            name=name,
        )(*held)

    early = upwards(bundle("early", (own, first, second), EARLY_CHOICES), (4, 4), EARLY_TARGETS)
    late = upwards(
        bundle("late", (own, first, second, third, fourth), LATE_CHOICES), (4, 4), LATE_TARGETS
    )

    params = pltpu.CompilerParams(vmem_limit_bytes=14 * 2**20)
    row = jax.ShapeDtypeStruct((kv_count, 1, lanes), jnp.float32)
    state = [row, row, jax.ShapeDtypeStruct((kv_count, width, lanes), jnp.float32)]

    def cost(count):
        work = kv_count * count * block * lanes
        return pl.CostEstimate(
            flops=4 * work * width, bytes_accessed=4 * 2**20, transcendentals=work
        )

    near = (own, first, second, third, fourth)
    folded, far_bias, *known = pl.pallas_call(
        functools.partial(near_kernel, devices=devices, group=group),
        out_shape=[
            jax.ShapeDtypeStruct((kv_count, width, lanes), jnp.bfloat16),
            jax.ShapeDtypeStruct((2, 2 * block, lanes), jnp.float32),
            *state,
        ],
        in_specs=[smem] + [vmem] * (2 + len(near)),
        out_specs=[vmem] * 5,
        scratch_shapes=[pltpu.VMEM((len(near) * block, lanes), jnp.float32)],
        compiler_params=params,
        cost_estimate=cost(len(near)),
        name="near",
    )(doc_lengths, queries, partner_queries, *near)
    known = pl.pallas_call(
        functools.partial(far_kernel, number=0),
        out_shape=state,
        in_specs=[vmem] * 6,
        out_specs=[vmem] * 3,
        compiler_params=params,
        cost_estimate=cost(2),
        name="middle",
    )(folded, far_bias, *known, early)
    return pl.pallas_call(
        functools.partial(far_kernel, number=1),
        out_shape=jax.ShapeDtypeStruct((block, 2 * heads, width), jnp.bfloat16),
        in_specs=[vmem] * 6,
        out_specs=pl.BlockSpec(memory_space=pl.ANY),
        scratch_shapes=[
            pltpu.VMEM((kv_count // 2, block, 2 * group, width), jnp.bfloat16),
            pltpu.SemaphoreType.DMA((kv_count // 2,)),
        ],
        compiler_params=params,
        cost_estimate=cost(2),
        name="finish",
    )(folded, far_bias, *known, late)


def solution(mesh):
    in_specs = (P("ctx", "head", None), P("ctx", "head", None), P("ctx", "head", None), P())
    out_specs = P(("ctx", "head"), None, None)
    return jax.shard_map(shards, mesh=mesh, in_specs=in_specs, out_specs=out_specs, check_vma=False)
```

```python
import functools
import math

import jax
import jax.numpy as jnp
from jax import lax
from jax.experimental import pallas as pl
from jax.experimental.pallas import tpu as pltpu
from jax.sharding import PartitionSpec as P

REACH_LOG = 3
MASKED_SCORE = -1e30

STEPS = ((3, 1), (4, 4), (1, 3), (2, 2))
EARLY_TARGETS = (0, 1, 3, 2)
LATE_TARGETS = (0, 2, 1, 3)
EARLY_CHOICES = ((1, (1, 1, 1, 1)), (2, (2, 2, 0, 2)))
LATE_CHOICES = ((3, (3, 1, 3, 1)), (4, (4, 0, 4, 2)))
EARLY_DISTANCES = ((5, 7, (5, 7, 6, 6)), (8, 8, (8, 8, 7, 5)))
LATE_DISTANCES = ((7, 5, (7, 6, 8, 7)), (6, 6, (6, 5, 5, 8)))


def query_bounds(first_place, lanes, group, doc_lengths):
    place = first_place + lax.broadcasted_iota(jnp.int32, (1, lanes), 1) // group
    begin = jnp.zeros((1, lanes), jnp.int32)
    end = jnp.int32(0)
    for j in range(doc_lengths.shape[0]):
        end = end + doc_lengths[j]
        begin = jnp.where(place >= end, end, begin)
    return place, begin


def block_bias(stretch, distance, block, group, doc_lengths):
    lanes = block * group
    first = stretch * block
    place, begin = query_bounds(first, lanes, group, doc_lengths)
    key_place = first - distance * block + lax.broadcasted_iota(jnp.int32, (block, lanes), 0)
    allowed = (key_place >= begin) & (key_place <= place)
    return jnp.where(allowed, 0.0, MASKED_SCORE)


def score(q, keys, bias):
    factor = math.log2(math.e) / math.sqrt(q.shape[0])
    return jnp.dot(keys, q, preferred_element_type=jnp.float32) * factor + bias


def mix(values, weights):
    return lax.dot_general(
        values,
        weights.astype(jnp.bfloat16),
        (((0,), (0,)), ((), ())),
        preferred_element_type=jnp.float32,
    )


def pack_kernel(*refs, kept):
    if kept:
        keys, values, queries, out, given_queries, staged, sems = refs
    else:
        keys, values, out, staged, sems = refs
    core = lax.axis_index("head")
    block = out.shape[2]
    given_rows = pl.ds((1 - core) * block, block)
    rows = pl.ds(core * block, block) if kept else given_rows
    copies = [
        pltpu.make_async_copy(keys.at[rows], staged.at[0], sems.at[0]),
        pltpu.make_async_copy(values.at[rows], staged.at[1], sems.at[1]),
    ]
    if kept:
        copies.append(pltpu.make_async_copy(queries.at[given_rows], given_queries, sems.at[2]))
    for number, copy in enumerate(copies):
        copy.start(priority=number % 2)
    for kind in range(2):
        copies[kind].wait()
        out[kind] = jnp.swapaxes(staged[kind].astype(jnp.float32), 0, 1).astype(out.dtype)
    for copy in copies[2:]:
        copy.wait()


def chain_position(devices):
    device, core = lax.axis_index("ctx"), lax.axis_index("head")
    return jnp.where(core == 0, device, 2 * devices - 1 - device)


def bundle_kernel(*refs, devices, choices):
    held, out = refs[:-1], refs[-1]
    source = chain_position(devices) - (devices - 4)
    for slot, (usual, special) in enumerate(choices):
        for number, ref in enumerate(held):
            if number != usual and number not in special:
                continue
            chosen = jnp.bool_(number == usual)
            for row, other in enumerate(special):
                chosen = jnp.where(source == row, number == other, chosen)

            @pl.when(chosen)
            def _(slot=slot, ref=ref):
                out[slot] = ref[...]


def near_kernel(doc_lengths, queries, partner_queries, *refs, devices, group):
    blocks, (folded, far_bias, peak, sums, mixes, bias) = refs[:-6], refs[-6:]
    stretch, core = chain_position(devices), lax.axis_index("head")
    kv_count, block, width = blocks[0].shape[1:]
    lanes = block * group
    odd = stretch % 2 == 1
    for row in range(len(blocks)):
        distance = 0
        if row > 0:
            by_even, by_odd = STEPS[row - 1]
            if by_even % 2 == 1:
                by_even, by_odd = by_odd, by_even
            distance = jnp.where(odd, by_odd, by_even)
        bias[row * block : (row + 1) * block, :] = block_bias(
            stretch, distance, block, group, doc_lengths
        )

    def gather(kind, head):
        return jnp.concatenate([ref[kind, head] for ref in blocks], axis=0)

    for half in range(2):
        side = core if half == 0 else 1 - core
        for begin in range(0, kv_count // 2, 2):
            first_head = side * (kv_count // 2) + begin
            slots = [half * (kv_count // 2) + begin + part for part in range(2)]
            heads = slice(begin * group, (begin + 2) * group)
            if half == 0:
                both = queries[pl.ds(core * block, block), heads, :]
            else:
                both = partner_queries[:, heads, :]
            both = both.astype(jnp.float32)
            qs = [
                both[:, part * group : (part + 1) * group, :]
                .reshape(lanes, width)
                .T.astype(jnp.bfloat16)
                for part in range(2)
            ]
            scores = [
                score(q, gather(0, first_head + part), bias[...]) for part, q in enumerate(qs)
            ]
            largest = [jnp.max(each, axis=0, keepdims=True) for each in scores]
            weights = [jnp.exp2(each - top) for each, top in zip(scores, largest)]
            for part, slot in enumerate(slots):
                folded[slot] = qs[part]
                peak[slot] = largest[part]
                sums[slot] = jnp.sum(weights[part], axis=0, keepdims=True)
                mixes[slot] = mix(gather(1, first_head + part), weights[part])
    turn = stretch - devices
    for number, table in enumerate((EARLY_DISTANCES, LATE_DISTANCES)):
        for row, (even_distance, odd_distance, special) in enumerate(table):
            distance = jnp.where(odd, odd_distance, even_distance)
            for at, other in enumerate(special):
                distance = jnp.where(turn == at, other, distance)
            far_bias[number, row * block : (row + 1) * block, :] = block_bias(
                stretch, distance, block, group, doc_lengths
            )


def far_kernel(folded, far_bias, peak, sums, mixes, blocks, *refs, number):
    ends = number == 1
    if ends:
        out, staged, sems = refs
    else:
        new_peak, new_sums, new_mixes = refs
    core = lax.axis_index("head")
    _, _, kv_count, block, width = blocks.shape
    group = folded.shape[2] // block
    half = kv_count // 2
    copies = []

    def weigh(slots, heads):
        scores = [
            score(
                folded[slot], blocks[:, 0, head].reshape(2 * block, width), far_bias[number]
            )
            for slot, head in zip(slots, heads)
        ]
        largest = [
            jnp.maximum(jnp.max(each, axis=0, keepdims=True), peak[slot])
            for each, slot in zip(scores, slots)
        ]
        weights = [jnp.exp2(each - top) for each, top in zip(scores, largest)]
        shrinks = [jnp.exp2(peak[slot] - top) for slot, top in zip(slots, largest)]
        totals = [
            jnp.sum(each, axis=0, keepdims=True) + sums[slot] * shrink
            for each, slot, shrink in zip(weights, slots, shrinks)
        ]
        return largest, weights, shrinks, totals

    def merge(slots, heads, largest, weights, shrinks, totals):
        mixed = [
            mix(blocks[:, 1, head].reshape(2 * block, width), each)
            for head, each in zip(heads, weights)
        ]
        if not ends:
            for part, slot in enumerate(slots):
                new_peak[slot] = largest[part]
                new_sums[slot] = totals[part]
                new_mixes[slot] = mixed[part] + mixes[slot] * shrinks[part]
            return
        done = []
        for part, slot in enumerate(slots):
            scale = 1.0 / totals[part]
            result = mixed[part] * scale + mixes[slot] * (shrinks[part] * scale)
            done.append(result.T.reshape(block, group, width))
        pair = slots[0] // 2
        staged[pair] = jnp.concatenate(done, axis=1).astype(staged.dtype)
        first = pl.multiple_of(heads[0] * group, 2 * group)
        copy = pltpu.make_async_copy(
            staged.at[pair], out.at[:, pl.ds(first, 2 * group)], sems.at[pair]
        )
        copy.start(priority=pair % 2)
        copies.append(copy)

    waiting = None
    for begin in range(0, kv_count, 2):
        side = core if begin < half else 1 - core
        slots = [begin, begin + 1]
        heads = [side * half + slot % half for slot in slots]
        weighed = weigh(slots, heads)
        if waiting is not None:
            merge(*waiting)
        waiting = (slots, heads, *weighed)
    merge(*waiting)
    for copy in copies:
        copy.wait()


def shards(queries, key_heads, value_head_rows, doc_lengths):
    stride, heads, width = queries.shape
    kv_half = key_heads.shape[1]
    block = stride // 2
    kv_count = 2 * kv_half
    group = heads // kv_half
    lanes = block * group
    devices = lax.axis_size("ctx")
    core = lax.axis_index("head")
    stretches = 2 * devices

    def owner(place):
        return 2 * place if place < devices else 2 * (stretches - 1 - place) + 1

    def swap(array):
        return lax.ppermute(array, "head", [(0, 1), (1, 0)])

    def upwards(array, steps, turned=()):
        target = {at: at + steps[at % 2] for at in range(stretches)}
        for number, to in enumerate(turned):
            target[devices - 4 + number] = devices + to
        pairs = [(owner(at), owner(to)) for at, to in target.items() if to < stretches]
        return lax.ppermute(array, ("ctx", "head"), pairs)

    smem = pl.BlockSpec(memory_space=pltpu.SMEM)
    vmem = pl.BlockSpec(memory_space=pltpu.VMEM)
    def pack(kept):
        arrays = (key_heads, value_head_rows, queries) if kept else (key_heads, value_head_rows)
        out_shape = [jax.ShapeDtypeStruct((2, kv_half, block, width), jnp.bfloat16)]
        if kept:
            out_shape.append(jax.ShapeDtypeStruct((block, heads, width), jnp.bfloat16))
        return pl.pallas_call(
            functools.partial(pack_kernel, kept=kept),
            out_shape=out_shape,
            in_specs=[pl.BlockSpec(memory_space=pltpu.HBM)] * len(arrays),
            out_specs=[vmem] * len(out_shape),
            scratch_shapes=[
                pltpu.VMEM((2, block, kv_half, width), jnp.bfloat16),
                pltpu.SemaphoreType.DMA((len(arrays),)),
            ],
            compiler_params=pltpu.CompilerParams(vmem_limit_bytes=6 * 2**20),
            cost_estimate=pl.CostEstimate(
                flops=0, bytes_accessed=len(arrays) * 2**20, transcendentals=0
            ),
            name="keep" if kept else "give",
        )(*[pltpu.with_memory_space_constraint(array, pltpu.HBM) for array in arrays])

    (given,) = pack(False)
    given = swap(given)
    keep, given_queries = pack(True)
    own = jnp.concatenate(
        [jnp.where(core == 0, keep, given), jnp.where(core == 0, given, keep)], axis=1
    )
    own, given_queries = lax.optimization_barrier((own, given_queries))
    partner_queries = swap(given_queries)
    first = upwards(own, STEPS[0])
    own, partner_queries = lax.optimization_barrier((own, partner_queries))
    second, third, fourth = [upwards(own, steps) for steps in STEPS[1:]]

    def bundle(name, held, choices):
        return pl.pallas_call(
            functools.partial(bundle_kernel, devices=devices, choices=choices),
            out_shape=jax.ShapeDtypeStruct((2, *own.shape), own.dtype),
            in_specs=[vmem] * len(held),
            out_specs=vmem,
            compiler_params=pltpu.CompilerParams(vmem_limit_bytes=6 * 2**20),
            name=name,
        )(*held)

    early = upwards(bundle("early", (own, first, second), EARLY_CHOICES), (4, 4), EARLY_TARGETS)
    late = upwards(
        bundle("late", (own, first, second, third, fourth), LATE_CHOICES), (4, 4), LATE_TARGETS
    )

    params = pltpu.CompilerParams(vmem_limit_bytes=14 * 2**20)
    row = jax.ShapeDtypeStruct((kv_count, 1, lanes), jnp.float32)
    state = [row, row, jax.ShapeDtypeStruct((kv_count, width, lanes), jnp.float32)]

    def cost(count):
        work = kv_count * count * block * lanes
        return pl.CostEstimate(
            flops=4 * work * width, bytes_accessed=4 * 2**20, transcendentals=work
        )

    near = (own, first, second, third, fourth)
    folded, far_bias, *known = pl.pallas_call(
        functools.partial(near_kernel, devices=devices, group=group),
        out_shape=[
            jax.ShapeDtypeStruct((kv_count, width, lanes), jnp.bfloat16),
            jax.ShapeDtypeStruct((2, 2 * block, lanes), jnp.float32),
            *state,
        ],
        in_specs=[smem] + [vmem] * (2 + len(near)),
        out_specs=[vmem] * 5,
        scratch_shapes=[pltpu.VMEM((len(near) * block, lanes), jnp.float32)],
        compiler_params=params,
        cost_estimate=cost(len(near)),
        name="near",
    )(doc_lengths, queries, partner_queries, *near)
    known = pl.pallas_call(
        functools.partial(far_kernel, number=0),
        out_shape=state,
        in_specs=[vmem] * 6,
        out_specs=[vmem] * 3,
        compiler_params=params,
        cost_estimate=cost(2),
        name="middle",
    )(folded, far_bias, *known, early)
    return pl.pallas_call(
        functools.partial(far_kernel, number=1),
        out_shape=jax.ShapeDtypeStruct((block, 2 * heads, width), jnp.bfloat16),
        in_specs=[vmem] * 6,
        out_specs=pl.BlockSpec(memory_space=pl.ANY),
        scratch_shapes=[
            pltpu.VMEM((kv_count // 2, block, 2 * group, width), jnp.bfloat16),
            pltpu.SemaphoreType.DMA((kv_count // 2,)),
        ],
        compiler_params=params,
        cost_estimate=cost(2),
        name="finish",
    )(folded, far_bias, *known, late)


def solution(mesh):
    in_specs = (P("ctx", "head", None), P("ctx", "head", None), P("ctx", "head", None), P())
    out_specs = P(("ctx", "head"), None, None)
    return jax.shard_map(shards, mesh=mesh, in_specs=in_specs, out_specs=out_specs, check_vma=False)
```

```python
import functools
import math

import jax
import jax.numpy as jnp
from jax import lax
from jax.experimental import pallas as pl
from jax.experimental.pallas import tpu as pltpu
from jax.sharding import PartitionSpec as P

REACH_LOG = 3
MASKED_SCORE = -1e30

STEPS = ((3, 1), (4, 4), (1, 3), (2, 2))
EARLY_TARGETS = (0, 1, 3, 2)
LATE_TARGETS = (0, 2, 1, 3)
EARLY_CHOICES = ((1, (1, 1, 1, 1)), (2, (2, 2, 0, 2)))
LATE_CHOICES = ((3, (3, 1, 3, 1)), (4, (4, 0, 4, 2)))
EARLY_DISTANCES = ((5, 7, (5, 7, 6, 6)), (8, 8, (8, 8, 7, 5)))
LATE_DISTANCES = ((7, 5, (7, 6, 8, 7)), (6, 6, (6, 5, 5, 8)))


def query_bounds(first_place, lanes, group, doc_lengths):
    place = first_place + lax.broadcasted_iota(jnp.int32, (1, lanes), 1) // group
    begin = jnp.zeros((1, lanes), jnp.int32)
    end = jnp.int32(0)
    for j in range(doc_lengths.shape[0]):
        end = end + doc_lengths[j]
        begin = jnp.where(place >= end, end, begin)
    return place, begin


def block_bias(stretch, distance, block, group, doc_lengths):
    lanes = block * group
    first = stretch * block
    place, begin = query_bounds(first, lanes, group, doc_lengths)
    key_place = first - distance * block + lax.broadcasted_iota(jnp.int32, (block, lanes), 0)
    allowed = (key_place >= begin) & (key_place <= place)
    return jnp.where(allowed, 0.0, MASKED_SCORE)


def score(q, keys, bias):
    factor = math.log2(math.e) / math.sqrt(q.shape[0])
    return jnp.dot(keys, q, preferred_element_type=jnp.float32) * factor + bias


def mix(values, weights):
    return lax.dot_general(
        values,
        weights.astype(jnp.bfloat16),
        (((0,), (0,)), ((), ())),
        preferred_element_type=jnp.float32,
    )


def pack_kernel(*refs, kept):
    if kept:
        keys, values, queries, out, given_queries, staged, sems = refs
    else:
        keys, values, out, staged, sems = refs
    core = lax.axis_index("head")
    block = out.shape[2]
    given_rows = pl.ds((1 - core) * block, block)
    rows = pl.ds(core * block, block) if kept else given_rows
    copies = [
        pltpu.make_async_copy(keys.at[rows], staged.at[0], sems.at[0]),
        pltpu.make_async_copy(values.at[rows], staged.at[1], sems.at[1]),
    ]
    if kept:
        copies.append(pltpu.make_async_copy(queries.at[given_rows], given_queries, sems.at[2]))
    for copy in copies:
        copy.start()
    for kind in range(2):
        copies[kind].wait()
        out[kind] = jnp.swapaxes(staged[kind].astype(jnp.float32), 0, 1).astype(out.dtype)
    for copy in copies[2:]:
        copy.wait()


def chain_position(devices):
    device, core = lax.axis_index("ctx"), lax.axis_index("head")
    return jnp.where(core == 0, device, 2 * devices - 1 - device)


def bundle_kernel(*refs, devices, choices):
    held, out = refs[:-1], refs[-1]
    source = chain_position(devices) - (devices - 4)
    for slot, (usual, special) in enumerate(choices):
        for number, ref in enumerate(held):
            if number != usual and number not in special:
                continue
            chosen = jnp.bool_(number == usual)
            for row, other in enumerate(special):
                chosen = jnp.where(source == row, number == other, chosen)

            @pl.when(chosen)
            def _(slot=slot, ref=ref):
                out[slot] = ref[...]


def near_kernel(doc_lengths, queries, partner_queries, *refs, devices, group):
    blocks, (folded, far_bias, peak, sums, mixes, bias) = refs[:-6], refs[-6:]
    stretch, core = chain_position(devices), lax.axis_index("head")
    kv_count, block, width = blocks[0].shape[1:]
    lanes = block * group
    odd = stretch % 2 == 1
    for row in range(len(blocks)):
        distance = 0
        if row > 0:
            by_even, by_odd = STEPS[row - 1]
            if by_even % 2 == 1:
                by_even, by_odd = by_odd, by_even
            distance = jnp.where(odd, by_odd, by_even)
        bias[row * block : (row + 1) * block, :] = block_bias(
            stretch, distance, block, group, doc_lengths
        )

    def gather(kind, head):
        return jnp.concatenate([ref[kind, head] for ref in blocks], axis=0)

    for half in range(2):
        side = core if half == 0 else 1 - core
        for begin in range(0, kv_count // 2, 2):
            first_head = side * (kv_count // 2) + begin
            slots = [half * (kv_count // 2) + begin + part for part in range(2)]
            heads = slice(begin * group, (begin + 2) * group)
            if half == 0:
                both = queries[pl.ds(core * block, block), heads, :]
            else:
                both = partner_queries[:, heads, :]
            both = both.astype(jnp.float32)
            qs = [
                both[:, part * group : (part + 1) * group, :]
                .reshape(lanes, width)
                .T.astype(jnp.bfloat16)
                for part in range(2)
            ]
            scores = [
                score(q, gather(0, first_head + part), bias[...]) for part, q in enumerate(qs)
            ]
            largest = [jnp.max(each, axis=0, keepdims=True) for each in scores]
            weights = [jnp.exp2(each - top) for each, top in zip(scores, largest)]
            for part, slot in enumerate(slots):
                folded[slot] = qs[part]
                peak[slot] = largest[part]
                sums[slot] = jnp.sum(weights[part], axis=0, keepdims=True)
                mixes[slot] = mix(gather(1, first_head + part), weights[part])
    turn = stretch - devices
    for number, table in enumerate((EARLY_DISTANCES, LATE_DISTANCES)):
        for row, (even_distance, odd_distance, special) in enumerate(table):
            distance = jnp.where(odd, odd_distance, even_distance)
            for at, other in enumerate(special):
                distance = jnp.where(turn == at, other, distance)
            far_bias[number, row * block : (row + 1) * block, :] = block_bias(
                stretch, distance, block, group, doc_lengths
            )


def far_kernel(folded, far_bias, peak, sums, mixes, blocks, *refs, number):
    ends = number == 1
    if ends:
        out, staged, sems = refs
    else:
        new_peak, new_sums, new_mixes = refs
    core = lax.axis_index("head")
    _, _, kv_count, block, width = blocks.shape
    group = folded.shape[2] // block
    half = kv_count // 2
    copies = []

    def weigh(slots, heads):
        scores = [
            score(
                folded[slot], blocks[:, 0, head].reshape(2 * block, width), far_bias[number]
            )
            for slot, head in zip(slots, heads)
        ]
        largest = [
            jnp.maximum(jnp.max(each, axis=0, keepdims=True), peak[slot])
            for each, slot in zip(scores, slots)
        ]
        weights = [jnp.exp2(each - top) for each, top in zip(scores, largest)]
        shrinks = [jnp.exp2(peak[slot] - top) for slot, top in zip(slots, largest)]
        totals = [
            jnp.sum(each, axis=0, keepdims=True) + sums[slot] * shrink
            for each, slot, shrink in zip(weights, slots, shrinks)
        ]
        return largest, weights, shrinks, totals

    def merge(slots, heads, largest, weights, shrinks, totals):
        mixed = [
            mix(blocks[:, 1, head].reshape(2 * block, width), each)
            for head, each in zip(heads, weights)
        ]
        if not ends:
            for part, slot in enumerate(slots):
                new_peak[slot] = largest[part]
                new_sums[slot] = totals[part]
                new_mixes[slot] = mixed[part] + mixes[slot] * shrinks[part]
            return
        done = []
        for part, slot in enumerate(slots):
            scale = 1.0 / totals[part]
            result = mixed[part] * scale + mixes[slot] * (shrinks[part] * scale)
            done.append(result.T.reshape(block, group, width))
        pair = slots[0] // 2
        staged[pair] = jnp.concatenate(done, axis=1).astype(staged.dtype)
        first = pl.multiple_of(heads[0] * group, 2 * group)
        copy = pltpu.make_async_copy(
            staged.at[pair], out.at[:, pl.ds(first, 2 * group)], sems.at[pair]
        )
        copy.start()
        copies.append(copy)

    waiting = None
    for begin in range(0, kv_count, 2):
        side = core if begin < half else 1 - core
        slots = [begin, begin + 1]
        heads = [side * half + slot % half for slot in slots]
        weighed = weigh(slots, heads)
        if waiting is not None:
            merge(*waiting)
        waiting = (slots, heads, *weighed)
    merge(*waiting)
    for copy in copies:
        copy.wait()


def shards(queries, key_heads, value_head_rows, doc_lengths):
    stride, heads, width = queries.shape
    kv_half = key_heads.shape[1]
    block = stride // 2
    kv_count = 2 * kv_half
    group = heads // kv_half
    lanes = block * group
    devices = lax.axis_size("ctx")
    core = lax.axis_index("head")
    stretches = 2 * devices

    def owner(place):
        return 2 * place if place < devices else 2 * (stretches - 1 - place) + 1

    def swap(array):
        return lax.ppermute(array, "head", [(0, 1), (1, 0)])

    def upwards(array, steps, turned=()):
        target = {at: at + steps[at % 2] for at in range(stretches)}
        for number, to in enumerate(turned):
            target[devices - 4 + number] = devices + to
        pairs = [(owner(at), owner(to)) for at, to in target.items() if to < stretches]
        return lax.ppermute(array, ("ctx", "head"), pairs)

    smem = pl.BlockSpec(memory_space=pltpu.SMEM)
    vmem = pl.BlockSpec(memory_space=pltpu.VMEM)
    def pack(kept):
        arrays = (key_heads, value_head_rows, queries) if kept else (key_heads, value_head_rows)
        out_shape = [jax.ShapeDtypeStruct((2, kv_half, block, width), jnp.bfloat16)]
        if kept:
            out_shape.append(jax.ShapeDtypeStruct((block, heads, width), jnp.bfloat16))
        return pl.pallas_call(
            functools.partial(pack_kernel, kept=kept),
            out_shape=out_shape,
            in_specs=[pl.BlockSpec(memory_space=pltpu.HBM)] * len(arrays),
            out_specs=[vmem] * len(out_shape),
            scratch_shapes=[
                pltpu.VMEM((2, block, kv_half, width), jnp.bfloat16),
                pltpu.SemaphoreType.DMA((len(arrays),)),
            ],
            compiler_params=pltpu.CompilerParams(vmem_limit_bytes=6 * 2**20),
            cost_estimate=pl.CostEstimate(
                flops=0, bytes_accessed=len(arrays) * 2**20, transcendentals=0
            ),
            name="keep" if kept else "give",
        )(*[pltpu.with_memory_space_constraint(array, pltpu.HBM) for array in arrays])

    (given,) = pack(False)
    given = swap(given)
    keep, given_queries = pack(True)
    given, given_queries = lax.optimization_barrier((given, given_queries))
    own = jnp.concatenate(
        [jnp.where(core == 0, keep, given), jnp.where(core == 0, given, keep)], axis=1
    )
    partner_queries = swap(given_queries)
    first = upwards(own, STEPS[0])
    own, partner_queries = lax.optimization_barrier((own, partner_queries))
    second, third, fourth = [upwards(own, steps) for steps in STEPS[1:]]

    def bundle(name, held, choices):
        return pl.pallas_call(
            functools.partial(bundle_kernel, devices=devices, choices=choices),
            out_shape=jax.ShapeDtypeStruct((2, *own.shape), own.dtype),
            in_specs=[vmem] * len(held),
            out_specs=vmem,
            compiler_params=pltpu.CompilerParams(vmem_limit_bytes=6 * 2**20),
            name=name,
        )(*held)

    early = upwards(bundle("early", (own, first, second), EARLY_CHOICES), (4, 4), EARLY_TARGETS)
    late = upwards(
        bundle("late", (own, first, second, third, fourth), LATE_CHOICES), (4, 4), LATE_TARGETS
    )

    params = pltpu.CompilerParams(vmem_limit_bytes=14 * 2**20)
    row = jax.ShapeDtypeStruct((kv_count, 1, lanes), jnp.float32)
    state = [row, row, jax.ShapeDtypeStruct((kv_count, width, lanes), jnp.float32)]

    def cost(count):
        work = kv_count * count * block * lanes
        return pl.CostEstimate(
            flops=4 * work * width, bytes_accessed=4 * 2**20, transcendentals=work
        )

    near = (own, first, second, third, fourth)
    folded, far_bias, *known = pl.pallas_call(
        functools.partial(near_kernel, devices=devices, group=group),
        out_shape=[
            jax.ShapeDtypeStruct((kv_count, width, lanes), jnp.bfloat16),
            jax.ShapeDtypeStruct((2, 2 * block, lanes), jnp.float32),
            *state,
        ],
        in_specs=[smem] + [vmem] * (2 + len(near)),
        out_specs=[vmem] * 5,
        scratch_shapes=[pltpu.VMEM((len(near) * block, lanes), jnp.float32)],
        compiler_params=params,
        cost_estimate=cost(len(near)),
        name="near",
    )(doc_lengths, queries, partner_queries, *near)
    known = pl.pallas_call(
        functools.partial(far_kernel, number=0),
        out_shape=state,
        in_specs=[vmem] * 6,
        out_specs=[vmem] * 3,
        compiler_params=params,
        cost_estimate=cost(2),
        name="middle",
    )(folded, far_bias, *known, early)
    return pl.pallas_call(
        functools.partial(far_kernel, number=1),
        out_shape=jax.ShapeDtypeStruct((block, 2 * heads, width), jnp.bfloat16),
        in_specs=[vmem] * 6,
        out_specs=pl.BlockSpec(memory_space=pl.ANY),
        scratch_shapes=[
            pltpu.VMEM((kv_count // 2, block, 2 * group, width), jnp.bfloat16),
            pltpu.SemaphoreType.DMA((kv_count // 2,)),
        ],
        compiler_params=params,
        cost_estimate=cost(2),
        name="finish",
    )(folded, far_bias, *known, late)


def solution(mesh):
    in_specs = (P("ctx", "head", None), P("ctx", "head", None), P("ctx", "head", None), P())
    out_specs = P(("ctx", "head"), None, None)
    return jax.shard_map(shards, mesh=mesh, in_specs=in_specs, out_specs=out_specs, check_vma=False)
```
